128 devices in a mesh: gx: 16 (over y, x), gy: 8 (over z, core).
Axes of the slice: x: 4, y: 4, z: 4, core: 2. Of those that a mesh axis runs over, the one named last changes fastest.
Arguments:
- concentration: float32 [24, 10, 256, 1024], P(None, None, 'gx', 'gy'), may hold values from -4 to 4
- base_volume: float32 [10, 256, 1024], P(None, 'gx', 'gy'), may hold values from 1 to 2
- flow_x: float32 [10, 256, 1024], P(None, 'gx', 'gy'), may hold values from -3 to 3
- flow_y: float32 [10, 256, 1024], P(None, 'gx', 'gy'), may hold values from -3 to 3
- face_wet_x: int32 [10, 256, 1024], P(None, 'gx', 'gy'), may hold values 0 or 1
- face_wet_y: int32 [10, 256, 1024], P(None, 'gx', 'gy'), may hold values 0 or 1
- diffusivity: float32 [9, 256, 1024], P(None, 'gx', 'gy'), may hold values from 0.05 to 2
- decay_rates: float32 [23], replicated, may hold values from 0.05 to 1.5
- inflow: float32 [24], replicated, may hold values from -2 to 2
- fine_volume: float32 [10, 4194304], P(None, ('gx', 'gy')), may hold values from 0.02 to 0.12
- fine_discharge: float32 [10, 4194304], P(None, ('gx', 'gy')), may hold values from 0 to 0.04
- cell_wet: int32 [4194304], P(('gx', 'gy')), may hold values from 0 to 1
- seg_local: int32 [4194304], P(('gx', 'gy')), may hold values from 0 to 2047
Outputs:
- updated: float32 [24, 10, 256, 1024], P(None, None, 'gx', 'gy')
The draws below stay inside these ranges and needn't reach their ends.
All inputs are finite; a program needn't handle non-finite values. No bound on the sum of `face_wet_x` or of `face_wet_y` on one device may be relied on, other than what follows from the above.
Results may differ from the reference program's by a relative error of at most 0.0003.
Values sent between devices are 32-bit elements; how exact they have to be, the bound alone decides.
No kernel may reach another device: no remote copies, remote signals or barrier semaphores. Data moves between devices by JAX's collectives and lax.ppermute only.
A program may use at most 192 MiB of HBM per device.

```python
import math
import jax
import jax.numpy as jnp
from jax import lax

SUBS = 24
LAYERS = 10
SX = 16
SY = 128
SUBSTEPS = 3
SEGS_DEV = 2048
FINE_DEV = 32768
OWNERS = 128
CAP = 256
NSX = 256
NSY = 1024
NFINE = 4194304


def draw_cell_wet(key, part):
    key = jax.random.fold_in(key, 11)
    level_key, cell_key = jax.random.split(key)
    levels = jax.random.randint(level_key, (OWNERS, OWNERS, 1), 1, 9)
    rolls = jax.random.randint(cell_key, (OWNERS, OWNERS, CAP), 0, 8)
    return (rolls < levels).astype(jnp.int32).reshape(-1)


def with_ends(values, own_key, smallest, largest):
    longest = values.shape.index(max(values.shape))
    spots = []
    for shift in (0, 1):
        where = [jax.random.randint(jax.random.fold_in(own_key, axis), (), 0, length) for axis, length in enumerate(values.shape)]
        where[longest] = (where[longest] + shift) % values.shape[longest]
        spots.append(tuple(where))
    return values.at[spots[0]].set(smallest).at[spots[1]].set(largest)


def shard_levels(rng, dims, cuts, least, top_value):
    level = 1.0
    for dim, shards_of in cuts:
        steps = jax.random.uniform(jax.random.fold_in(jax.random.fold_in(rng, 6), dim), (shards_of,), jnp.float32, least / len(cuts), top_value / len(cuts))
        level = level * jnp.repeat(jnp.exp(steps), dims[dim] // shards_of).reshape((-1,) + (1,) * (len(dims) - 1 - dim))
    return level


def noise(stream_key, extent, scale, reach, pieces=(), kind=jnp.bfloat16):
    gain = shard_levels(stream_key, extent, pieces, -0.22, 0.18) if pieces else 1.0
    entries = jax.random.normal(stream_key, extent, jnp.float32) * scale * gain
    return jnp.minimum(jnp.maximum(entries, -reach), reach).astype(kind)


def setup_inputs(seed: int = 0) -> dict:
    keys = jax.random.split(jax.random.key(seed), 14)
    return {
        "concentration": noise(keys[0], (SUBS, LAYERS, NSX, NSY), 1.0, 4.0, ((2, 16), (3, 8)), jnp.float32),
        "base_volume": jnp.clip(1.0 + 1.0 * jax.random.uniform(keys[1], (LAYERS, NSX, NSY), jnp.float32) ** shard_levels(keys[1], (LAYERS, NSX, NSY), ((1, 16), (2, 8)), -0.2, 0.2), 1.0, 2.0),
        "flow_x": noise(keys[2], (LAYERS, NSX, NSY), 0.25, 3.0, ((1, 16), (2, 8)), jnp.float32),
        "flow_y": noise(keys[3], (LAYERS, NSX, NSY), 0.25, 3.0, ((1, 16), (2, 8)), jnp.float32),
        "face_wet_x": with_ends((jax.random.randint(keys[4], (LAYERS, NSX, NSY), 0, 8) < 7).astype(jnp.int32), jax.random.fold_in(keys[4], 1), 0, 1),
        "face_wet_y": with_ends((jax.random.randint(keys[5], (LAYERS, NSX, NSY), 0, 8) < 7).astype(jnp.int32), jax.random.fold_in(keys[5], 1), 0, 1),
        "diffusivity": jnp.clip(jnp.exp(math.log(2.0) - 3.6888794 * jax.random.uniform(keys[6], (LAYERS - 1, NSX, NSY), jnp.float32) ** shard_levels(keys[6], (LAYERS - 1, NSX, NSY), ((1, 16), (2, 8)), -0.2, 0.2)), 0.05, 2.0),
        "decay_rates": jnp.clip(jnp.exp(jax.random.uniform(keys[7], (SUBS - 1,), jnp.float32, math.log(0.05), math.log(1.5))), 0.05, 1.5),
        "inflow": jnp.clip(jax.random.uniform(keys[8], (SUBS,), jnp.float32, -2.0, 2.0), -2.0, 2.0),
        "fine_volume": jnp.clip(0.02 + 0.09999999776482582 * jax.random.uniform(keys[9], (LAYERS, NFINE), jnp.float32) ** shard_levels(keys[9], (LAYERS, NFINE), ((1, 128),), -0.2, 0.2), 0.02, 0.12),
        "fine_discharge": jnp.clip(0.04 * jax.random.uniform(keys[10], (LAYERS, NFINE), jnp.float32) ** shard_levels(keys[10], (LAYERS, NFINE), ((1, 128),), -0.2, 0.2), 0.0, 0.04),
        "cell_wet": draw_cell_wet(jax.random.fold_in(keys[13], 71), 0),
        "seg_local": with_ends(jax.random.randint(keys[12], (NFINE,), 0, SEGS_DEV), jax.random.fold_in(keys[12], 1), 0, SEGS_DEV - 1).astype(jnp.int32),
    }


def minmod(left, right):
    return 0.5 * (jnp.sign(left) + jnp.sign(right)) * jnp.minimum(jnp.abs(left), jnp.abs(right))


def divergence(extended, flows, axis):
    count = extended.shape[axis] - 4
    steps = jnp.diff(extended, axis=axis)
    slope = minmod(lax.slice_in_dim(steps, 0, count + 2, axis=axis), lax.slice_in_dim(steps, 1, count + 3, axis=axis))
    middle = lax.slice_in_dim(extended, 1, count + 3, axis=axis)
    left = lax.slice_in_dim(middle, 0, count + 1, axis=axis) + 0.5 * lax.slice_in_dim(slope, 0, count + 1, axis=axis)
    right = lax.slice_in_dim(middle, 1, count + 2, axis=axis) - 0.5 * lax.slice_in_dim(slope, 1, count + 2, axis=axis)
    flux = jnp.maximum(flows, 0.0) * left + jnp.minimum(flows, 0.0) * right
    return lax.slice_in_dim(flux, 1, count + 1, axis=axis) - lax.slice_in_dim(flux, 0, count, axis=axis)


def factorize(volume, diffusivity):
    layers = volume.shape[0]
    step_size = 1.0 / SUBSTEPS
    zero = jnp.zeros_like(volume[0])
    uppers = [step_size * diffusivity[l] / volume[l] if l < layers - 1 else zero for l in range(layers)]
    downs = [step_size * diffusivity[l - 1] / volume[l] if l > 0 else zero for l in range(layers)]
    factors = [zero]
    pivots = [1.0 + uppers[0] + downs[0]]
    for l in range(1, layers):
        factor = -downs[l] / pivots[l - 1]
        factors.append(factor)
        pivots.append(1.0 + uppers[l] + downs[l] + factor * uppers[l - 1])
    return factors, pivots, uppers


def vertical_solve(star, factors, pivots, uppers):
    layers = star.shape[1]
    forward = [star[:, 0]]
    for l in range(1, layers):
        forward.append(star[:, l] - factors[l] * forward[l - 1])
    result = [None] * layers
    result[layers - 1] = forward[layers - 1] / pivots[layers - 1]
    for l in range(layers - 2, -1, -1):
        result[l] = (forward[l] + uppers[l] * result[l + 1]) / pivots[l]
    return jnp.stack(result, axis=1)


def substep(state, padded, volume, discharge, flows_x, flows_y, rates, inflow, factors, pivots, uppers):
    step_size = 1.0 / SUBSTEPS
    div = divergence(padded[:, :, :, 2:-2], flows_x, 2) + divergence(padded[:, :, 2:-2, :], flows_y, 3)
    converted = rates[:, None, None, None] * state
    react = jnp.concatenate([jnp.zeros_like(converted[:1]), converted[:-1]], axis=0) - converted
    star = state + step_size * ((discharge * (inflow[:, None, None, None] - state) - div) / volume + react)
    return vertical_solve(star, factors, pivots, uppers)


def reference(concentration, base_volume, flow_x, flow_y, face_wet_x, face_wet_y, diffusivity, decay_rates, inflow, fine_volume, fine_discharge, cell_wet, seg_local):
    blocks_y = NSY // SY
    slots = jnp.arange(NFINE, dtype=jnp.int32)
    seg_owner = ((slots % FINE_DEV) // CAP).astype(jnp.int32)
    row = (seg_owner // blocks_y) * SX + seg_local // SY
    col = (seg_owner % blocks_y) * SY + seg_local % SY
    flat = jnp.where(cell_wet == 1, row * NSY + col, NSX * NSY).astype(jnp.int32)
    payload = jnp.concatenate([fine_volume, fine_discharge], axis=0)

    def sum_row(values):
        return jax.ops.segment_sum(values, flat, num_segments=NSX * NSY + 1)[:-1]

    totals = lax.map(sum_row, payload).reshape(2 * LAYERS, NSX, NSY)
    volume = base_volume + totals[:LAYERS]
    discharge = totals[LAYERS:]
    keep_x = (jnp.arange(NSX) < NSX - 1).astype(jnp.float32)[None, :, None]
    keep_y = (jnp.arange(NSY) < NSY - 1).astype(jnp.float32)[None, None, :]
    flows_x = flow_x * face_wet_x.astype(jnp.float32) * keep_x
    flows_y = flow_y * face_wet_y.astype(jnp.float32) * keep_y
    flows_x = jnp.concatenate([jnp.zeros_like(flows_x[:, :1, :]), flows_x], axis=1)
    flows_y = jnp.concatenate([jnp.zeros_like(flows_y[:, :, :1]), flows_y], axis=2)
    rates = jnp.concatenate([jnp.zeros((1,), jnp.float32), decay_rates])
    factors, pivots, uppers = factorize(volume, diffusivity)
    state = concentration
    for step in range(SUBSTEPS):
        padded = jnp.pad(state, ((0, 0), (0, 0), (2, 2), (2, 2)))
        state = substep(state, padded, volume, discharge, flows_x, flows_y, rates, inflow, factors, pivots, uppers)
    return state
```

```python
import functools

import jax
import jax.numpy as jnp
from jax import lax
from jax.experimental import pallas as pl
from jax.experimental.pallas import tpu as pltpu
from jax.sharding import PartitionSpec as P

SUBSTEPS = 3
STEP = 1.0 / SUBSTEPS
VMEM_BYTES = 48 * 1024 * 1024
F32 = jnp.float32
BF16 = jnp.bfloat16

VMEM = pl.BlockSpec(memory_space=pltpu.VMEM)
SMEM = pl.BlockSpec(memory_space=pltpu.SMEM)


def half_minmod(left, right):
    return jnp.minimum(
        jnp.maximum(left, jnp.minimum(right, 0.0)), jnp.maximum(right, 0.0)
    )


def roll(values, shift):
    return pltpu.roll(values, shift % values.shape[-1], values.ndim - 1)


def lanes(shape):
    return lax.broadcasted_iota(jnp.int32, shape, len(shape) - 1)


def pack_kernel(volume, discharge, wet, segment, out):
    layers = volume.shape[0]
    rows = 2 * layers + 1
    groups = wet.shape[0]
    missing = 16 * 128
    label = jnp.where(wet[...] == 1, segment[...], missing).astype(F32)
    for k in range(groups):
        out[k * rows : k * rows + layers, :] = volume[:, k * 128 : (k + 1) * 128]
        out[k * rows + layers : k * rows + 2 * layers, :] = discharge[:, k * 128 : (k + 1) * 128]
        out[k * rows + 2 * layers : (k + 1) * rows, :] = label[k : k + 1, :]


def pack_slots(volume, discharge, wet, segment):
    layers, fine = volume.shape
    groups = fine // 128
    rows = 2 * layers + 1
    step = 32 if groups % 32 == 0 else 8
    return pl.pallas_call(
        pack_kernel,
        grid=(groups // step,),
        in_specs=[
            pl.BlockSpec((layers, step * 128), lambda i: (0, i)),
            pl.BlockSpec((layers, step * 128), lambda i: (0, i)),
            pl.BlockSpec((step, 128), lambda i: (i, 0)),
            pl.BlockSpec((step, 128), lambda i: (i, 0)),
        ],
        out_specs=pl.BlockSpec((step * rows, 128), lambda i: (i, 0)),
        out_shape=jax.ShapeDtypeStruct((groups * rows, 128), F32),
        compiler_params=pltpu.CompilerParams(vmem_limit_bytes=VMEM_BYTES),
        cost_estimate=pl.CostEstimate(flops=0, bytes_accessed=8 * 10**6, transcendentals=0),
        name="pack_slots",
    )(volume, discharge, wet.reshape(groups, 128), segment.reshape(groups, 128))


def pack_columns(load, count, tile):
    packed = None
    for par in range(2):
        for row in range(16):
            k = par * 16 + row
            moved = roll(load(tile * 2 + par, row), 4 * k + 2)
            if packed is None:
                packed = moved
            else:
                packed = jnp.where(lanes(moved.shape) // 4 == k, moved, packed)
    return packed


def start_kernel(
    last, conc, flow_x, flow_y, wet_x, wet_y, state, low_x, high_x, edges_y, qx, qy
):
    layers, rows = flow_x.shape[0], flow_x.shape[1]
    subs = conc.shape[0] // (layers * rows)
    row = lax.broadcasted_iota(jnp.int32, flow_x.shape, 1)
    col = lax.broadcasted_iota(jnp.int32, flow_x.shape, 2)
    keep_x = jnp.where((row == rows - 1) & (last[0] == 1), 0.0, 1.0)
    keep_y = jnp.where((col == 127) & (last[1] == 1), 0.0, 1.0)
    qx[...] = flow_x[...] * wet_x[...].astype(F32) * keep_x
    qy[...] = flow_y[...] * wet_y[...].astype(F32) * keep_y
    high_x[...] = jnp.zeros_like(high_x)
    edges_y[...] = jnp.zeros_like(edges_y)

    def layer(l, carry):
        for i in range(rows):
            c = conc[pl.ds(l * rows + i, subs, stride=layers * rows), :]
            state[l, i] = c
            if i < 2:
                low_x[l, i] = c
            if i >= rows - 2:
                high_x[l, i - rows + 2] = c
        high_x[layers, 0, pl.ds(l, 1), :] = qx[l, rows - 1 :, :]
        return carry

    lax.fori_loop(0, layers, layer, 0)

    def tile(t, carry):
        edges_y[t] = pack_columns(lambda l, i: state[l, i], subs, t)
        flows = pack_columns(lambda l, i: roll(qy[l, i : i + 1, :], -1), 1, t)
        edges_y[layers // 2, pl.ds(t, 1), :] = flows
        return carry

    lax.fori_loop(0, layers // 2, tile, 0)


def start(last, conc, flow_x, flow_y, wet_x, wet_y):
    subs, layers, rows, cols = conc.shape
    flows = jax.ShapeDtypeStruct(flow_x.shape, F32)
    return pl.pallas_call(
        start_kernel,
        in_specs=[SMEM] + [VMEM] * 5,
        out_specs=[VMEM] * 6,
        out_shape=[
            jax.ShapeDtypeStruct((layers, rows, subs, cols), F32),
            jax.ShapeDtypeStruct((layers, 2, subs, cols), F32),
            jax.ShapeDtypeStruct((layers + 1, 2, subs, cols), F32),
            jax.ShapeDtypeStruct((layers // 2 + 1, subs, cols), F32),
            flows,
            flows,
        ],
        compiler_params=pltpu.CompilerParams(vmem_limit_bytes=VMEM_BYTES),
        cost_estimate=pl.CostEstimate(flops=10**6, bytes_accessed=8 * 10**6, transcendentals=0),
        name="start_state",
    )(last, conc.reshape(subs * layers * rows, cols), flow_x, flow_y, wet_x, wet_y)


def edge_fluxes(own, left, right, flows_own, flows_left, inserts, fluxes):
    shape = own.shape
    place = lanes(shape) % 4

    def flux(four, flows):
        steps = 0.5 * (roll(four, -1) - four)
        slope = half_minmod(steps, roll(steps, -1))
        before = roll(four, -1) + slope
        after = roll(four, -2) - roll(slope, -1)
        return jnp.maximum(flows, 0.0) * before + jnp.minimum(flows, 0.0) * after

    first = jnp.where(place < 2, left, own)
    last = jnp.where(place < 2, own, right)
    inserts[...] = jnp.where(place == 0, roll(last, -2), first)
    fluxes[...] = jnp.where(place == 0, flux(last, flows_own), roll(flux(first, flows_left), 1))


def edge_pass(edges, edges_left, edges_right, flow_edges, flow_left, inserts, fluxes):
    tiles = inserts.shape[0]
    edge_fluxes(
        edges[:tiles],
        edges_left[:tiles],
        edges_right[:tiles],
        flow_edges[tiles, :tiles, :][:, None, :],
        flow_left[tiles, :tiles, :][:, None, :],
        inserts,
        fluxes,
    )


def divergence_layer(state, west, east, inserts, fluxes, qx, qx_west, qy, tile, par, emit):
    l = tile * 2 + par
    rows = qx.shape[1]
    lane = lanes(state.shape[2:])

    def get(i):
        if i < 0:
            return west[l, i + 2]
        if i >= rows:
            return east[l, i - rows]
        return state[l, i]

    before, here = (get(-2), get(-1))
    step = 0.5 * (here - before)
    flux = None
    left = None
    for i in range(-1, rows + 1):
        after = get(i + 1)
        step_after = 0.5 * (after - here)
        slope = half_minmod(step, step_after)
        right = here - slope
        if i >= 0:
            q = qx_west if i == 0 else qx[l, i - 1 : i, :]
            new_flux = jnp.maximum(q, 0.0) * left + jnp.minimum(q, 0.0) * right
            if i >= 1:
                c = before
                edge = 127 - 4 * (par * 16 + i - 1)
                insert = roll(inserts[tile], edge)
                cl = jnp.where(lane == 0, insert, roll(c, 1))
                cr = jnp.where(lane == 127, insert, roll(c, -1))
                slope_y = half_minmod(0.5 * (c - cl), 0.5 * (cr - c))
                qr = qy[l, i - 1 : i, :]
                fy = jnp.maximum(qr, 0.0) * (c + slope_y) + jnp.minimum(qr, 0.0) * roll(
                    c - slope_y, -1
                )
                flux_edge = roll(fluxes[tile], edge)
                fm = jnp.where(lane == 0, flux_edge, roll(fy, 1))
                fy = jnp.where(lane == 127, flux_edge, fy)
                emit(l, i - 1, c, (new_flux - flux) + (fy - fm))
            flux = new_flux
        left = here + slope
        before, here, step = (here, after, step_after)


def first_divergence_kernel(
    state, west, east, edges, edges_left, edges_right, qx, qy, div, inserts, fluxes
):
    layers = qx.shape[0]
    edge_pass(edges, edges_left, edges_right, edges, edges_left, inserts, fluxes)

    def emit(l, i, c, value):
        div[l, i] = value

    def tile(t, carry):
        for par in range(2):
            qx_west = west[layers, 0, pl.ds(t * 2 + par, 1), :]
            divergence_layer(
                state, west, east, inserts, fluxes, qx, qx_west, qy, t, par, emit
            )
        return carry

    lax.fori_loop(0, layers // 2, tile, 0)


def first_divergence(state, west, east, edges, edges_left, edges_right, qx, qy):
    layers, rows, subs, cols = state.shape
    tiles = pltpu.VMEM((layers // 2, subs, cols), F32)
    return pl.pallas_call(
        first_divergence_kernel,
        in_specs=[VMEM] * 8,
        out_specs=VMEM,
        out_shape=jax.ShapeDtypeStruct(state.shape, F32),
        scratch_shapes=[tiles, tiles],
        compiler_params=pltpu.CompilerParams(vmem_limit_bytes=VMEM_BYTES),
        cost_estimate=pl.CostEstimate(flops=2 * 10**7, bytes_accessed=10**7, transcendentals=0),
        name="first_divergence",
    )(state, west, east, edges, edges_left, edges_right, qx, qy)


def explicit_value(c, div, rates, rates_before, inflow, renewal, scale):
    carried = pltpu.roll(c, 1, 0)
    return (
        c
        + ((renewal * (inflow - c) - scale * div) + (rates_before * carried - rates * c))
    )


def solve_row(star, row, coef, out, emit):
    layers = coef.shape[1]

    def get(which, l):
        return coef[which, l, pl.ds(row, 1), :]

    forward = [star[0, row]]
    for l in range(1, layers):
        forward.append(star[l, row] - get(0, l) * forward[l - 1])
    value = forward[layers - 1] * get(1, layers - 1)
    emit(layers - 1, row, value)
    for l in range(layers - 2, -1, -1):
        value = (forward[l] + get(2, l) * value) * get(1, l)
        emit(l, row, value)


def emit_edges(state, low_x, high_x, edges_y):
    layers, rows = state.shape[0], state.shape[1]
    low_x[...] = state[:, :2]
    high_x[...] = state[:, rows - 2 :]

    def tile(t, carry):
        edges_y[t] = pack_columns(lambda l, i: state[l, i], 0, t)
        return carry

    lax.fori_loop(0, layers // 2, tile, 0)


def aggregate(slots, spread, hot, total):
    rows = 21
    groups = slots.shape[0] // rows
    step = 8
    sub8 = lax.broadcasted_iota(jnp.int32, (8, 128), 0)
    column = lax.broadcasted_iota(jnp.int32, (128, 128), 0)
    total[...] = jnp.zeros_like(total)

    def chunk(it, carry):
        base = pl.multiple_of(it * (step * rows), 8)
        for j in range(step):
            at = base + j * rows
            label = slots[pl.ds(at + 20, 1), :].astype(jnp.int32)
            mask = jnp.where(jnp.broadcast_to((label >> 7) & 7, (8, 128)) == sub8, 1.0, 0.0)
            mask = jnp.concatenate([mask, mask], axis=0).astype(BF16)
            for ch in range(20):
                value = jnp.broadcast_to(slots[pl.ds(at + ch, 1), :], (8, 128))
                high = value.astype(BF16).astype(F32)
                both = jnp.concatenate([high, value - high], axis=0).astype(BF16)
                spread[ch * 16 : (ch + 1) * 16, j * 128 : (j + 1) * 128] = both * mask
            same = (label & 127) == column
            half = label >> 10
            for h in range(2):
                hit = jnp.where(same, jnp.where(half == h, 1.0, 0.0), 0.0).astype(BF16)
                hot[h * 128 : (h + 1) * 128, j * 128 : (j + 1) * 128] = hit
        total[...] += lax.dot_general(
            spread[...], hot[...], (((1,), (1,)), ((), ())), preferred_element_type=F32
        )
        return carry

    lax.fori_loop(0, groups // step, chunk, 0)


def first_step_kernel(
    slots,
    base_volume,
    diffusivity,
    state,
    div,
    rates,
    rates_before,
    inflow,
    new,
    low_x,
    high_x,
    edges_y,
    coef,
    spread,
    hot,
    total,
    star,
):
    layers, rows = base_volume.shape[0], base_volume.shape[1]
    aggregate(slots, spread, hot, total)
    uppers, downs = ([], [])
    for l in range(layers):
        parts = []
        for ch in (l, layers + l):
            parts.append(
                jnp.concatenate(
                    [
                        total[ch * 16 : ch * 16 + 8, h * 128 : (h + 1) * 128]
                        + total[ch * 16 + 8 : ch * 16 + 16, h * 128 : (h + 1) * 128]
                        for h in range(2)
                    ],
                    axis=0,
                )
            )
        scale = STEP / (base_volume[l] + parts[0])
        coef[3, l] = scale
        coef[4, l] = scale * parts[1]
        uppers.append(scale * diffusivity[l] if l < layers - 1 else jnp.zeros_like(scale))
        downs.append(scale * diffusivity[l - 1] if l > 0 else jnp.zeros_like(scale))
    pivot = 1.0 + uppers[0]
    coef[0, 0] = jnp.zeros_like(pivot)
    for l in range(layers):
        inverse = 1.0 / pivot
        coef[1, l] = inverse
        coef[2, l] = uppers[l]
        if l + 1 < layers:
            factor = -downs[l + 1] * inverse
            coef[0, l + 1] = factor
            pivot = 1.0 + uppers[l + 1] + downs[l + 1] + factor * uppers[l]

    def explicit(l, carry):
        for i in range(rows):
            star[l, i] = explicit_value(
                state[l, i],
                div[l, i],
                rates[...],
                rates_before[...],
                inflow[...],
                coef[4, l, i : i + 1, :],
                coef[3, l, i : i + 1, :],
            )
        return carry

    lax.fori_loop(0, layers, explicit, 0)

    def emit(l, i, value):
        new[l, i] = value

    def row(i, carry):
        solve_row(star, i, coef, new, emit)
        return carry

    lax.fori_loop(0, rows, row, 0)
    emit_edges(new, low_x, high_x, edges_y)


def state_shapes(shape):
    layers, rows, subs, cols = shape
    return [
        jax.ShapeDtypeStruct(shape, F32),
        jax.ShapeDtypeStruct((layers, 2, subs, cols), F32),
        jax.ShapeDtypeStruct((layers, 2, subs, cols), F32),
        jax.ShapeDtypeStruct((layers // 2, subs, cols), F32),
    ]


def first_step(slots, base_volume, diffusivity, state, div, rates, rates_before, inflow):
    layers, rows, subs, cols = state.shape
    return pl.pallas_call(
        first_step_kernel,
        in_specs=[VMEM] * 8,
        out_specs=[VMEM] * 5,
        out_shape=state_shapes(state.shape)
        + [jax.ShapeDtypeStruct((5, layers, rows, cols), F32)],
        scratch_shapes=[
            pltpu.VMEM((2 * layers * 16, 1024), BF16),
            pltpu.VMEM((256, 1024), BF16),
            pltpu.VMEM((2 * layers * 16, 256), F32),
            pltpu.VMEM(state.shape, F32),
        ],
        compiler_params=pltpu.CompilerParams(vmem_limit_bytes=VMEM_BYTES),
        cost_estimate=pl.CostEstimate(flops=10**9, bytes_accessed=10**7, transcendentals=0),
        name="aggregate_and_first_step",
    )(slots, base_volume, diffusivity, state, div, rates, rates_before, inflow)


def later_step_kernel(
    final,
    state,
    west,
    east,
    edges,
    edges_left,
    edges_right,
    flow_west,
    flow_edges,
    flow_left,
    qx,
    qy,
    coef,
    rates,
    rates_before,
    inflow,
    *refs,
):
    layers, rows = qx.shape[0], qx.shape[1]
    if final:
        out, inserts, fluxes, star = refs
        subs = out.shape[0] // (layers * rows)
    else:
        new, low_x, high_x, edges_y, inserts, fluxes, star = refs
    edge_pass(edges, edges_left, edges_right, flow_edges, flow_left, inserts, fluxes)

    def explicit(l, i, c, div):
        star[l, i] = explicit_value(
            c,
            div,
            rates[...],
            rates_before[...],
            inflow[...],
            coef[4, l, i : i + 1, :],
            coef[3, l, i : i + 1, :],
        )

    def tile(t, carry):
        for par in range(2):
            qx_west = flow_west[layers, 0, pl.ds(t * 2 + par, 1), :]
            divergence_layer(
                state, west, east, inserts, fluxes, qx, qx_west, qy, t, par, explicit
            )
        return carry

    lax.fori_loop(0, layers // 2, tile, 0)

    def emit(l, i, value):
        if final:
            out[pl.ds(l * rows + i, subs, stride=layers * rows), :] = value
        else:
            new[l, i] = value

    def row(i, carry):
        solve_row(star, i, coef, None, emit)
        return carry

    lax.fori_loop(0, rows, row, 0)
    if not final:
        emit_edges(new, low_x, high_x, edges_y)


def later_step(final, state, *args):
    layers, rows, subs, cols = state.shape
    tiles = pltpu.VMEM((layers // 2, subs, cols), F32)
    if final:
        shapes = jax.ShapeDtypeStruct((subs * layers * rows, cols), F32)
        specs = VMEM
    else:
        shapes = state_shapes(state.shape)
        specs = [VMEM] * 4
    return pl.pallas_call(
        functools.partial(later_step_kernel, final),
        in_specs=[VMEM] * 15,
        out_specs=specs,
        out_shape=shapes,
        scratch_shapes=[tiles, tiles, pltpu.VMEM(state.shape, F32)],
        compiler_params=pltpu.CompilerParams(vmem_limit_bytes=VMEM_BYTES),
        cost_estimate=pl.CostEstimate(flops=3 * 10**7, bytes_accessed=10**7, transcendentals=0),
        name="last_step" if final else "middle_step",
    )(state, *args)


def to_next(values, axis):
    size = lax.axis_size(axis)
    return lax.ppermute(values, axis, [(i, i + 1) for i in range(size - 1)])


def to_previous(values, axis):
    size = lax.axis_size(axis)
    return lax.ppermute(values, axis, [(i + 1, i) for i in range(size - 1)])


def exchange(low_x, high_x, edges_y):
    west = to_next(high_x, "gx")
    east = to_previous(low_x, "gx")
    left = to_next(edges_y, "gy")
    right = to_previous(edges_y, "gy")
    return (west, east, left, right)


def local(
    concentration,
    base_volume,
    flow_x,
    flow_y,
    face_wet_x,
    face_wet_y,
    diffusivity,
    decay_rates,
    inflow,
    fine_volume,
    fine_discharge,
    cell_wet,
    seg_local,
):
    subs, layers, rows, cols = concentration.shape
    size_x, size_y = (lax.axis_size("gx"), lax.axis_size("gy"))
    owners = size_x * size_y
    sent = pack_slots(fine_volume, fine_discharge, cell_wet, seg_local)
    arrived = lax.all_to_all(
        sent.reshape(owners, 1, -1), ("gx", "gy"), split_axis=0, concat_axis=0, tiled=True
    ).reshape(sent.shape)

    last = jnp.stack(
        [
            (lax.axis_index("gx") == size_x - 1).astype(jnp.int32),
            (lax.axis_index("gy") == size_y - 1).astype(jnp.int32),
        ]
    )
    rates = jnp.concatenate([jnp.zeros((1,), F32), decay_rates]) * STEP
    rates_before = jnp.concatenate([jnp.zeros((1,), F32), rates[:-1]])
    rates, rates_before, inflow = (
        jnp.broadcast_to(v[:, None], (subs, cols)) for v in (rates, rates_before, inflow)
    )
    state, low_x, high_x, edges, qx, qy = start(
        last, concentration, flow_x, flow_y, face_wet_x, face_wet_y
    )
    west, east, left, right = exchange(low_x, high_x, edges)
    flow_west, flow_edges, flow_left = (west, edges, left)
    div = first_divergence(state, west, east, edges, left, right, qx, qy)
    state, low_x, high_x, edges, coef = first_step(
        arrived, base_volume, diffusivity, state, div, rates, rates_before, inflow
    )
    for step in range(1, SUBSTEPS):
        final = step == SUBSTEPS - 1
        halos = exchange(low_x, high_x, edges)
        result = later_step(
            final,
            state,
            halos[0],
            halos[1],
            edges,
            halos[2],
            halos[3],
            flow_west,
            flow_edges,
            flow_left,
            qx,
            qy,
            coef,
            rates,
            rates_before,
            inflow,
        )
        if not final:
            state, low_x, high_x, edges = result
    return result.reshape(concentration.shape)


def solution(mesh):
    fine = P(None, ("gx", "gy"))
    block = P(None, "gx", "gy")
    return jax.shard_map(
        local,
        mesh=mesh,
        in_specs=(
            P(None, None, "gx", "gy"),
            block,
            block,
            block,
            block,
            block,
            block,
            P(),
            P(),
            fine,
            fine,
            P(("gx", "gy")),
            P(("gx", "gy")),
        ),
        out_specs=P(None, None, "gx", "gy"),
        check_vma=False,
    )
```

```python
import functools

import jax
import jax.numpy as jnp
from jax import lax
from jax.experimental import pallas as pl
from jax.experimental.pallas import tpu as pltpu
from jax.sharding import PartitionSpec as P

SUBSTEPS = 3
STEP = 1.0 / SUBSTEPS
VMEM_BYTES = 48 * 1024 * 1024
PACK_VMEM_BYTES = 62 * 1024 * 1024
F32 = jnp.float32
BF16 = jnp.bfloat16

VMEM = pl.BlockSpec(memory_space=pltpu.VMEM)
SMEM = pl.BlockSpec(memory_space=pltpu.SMEM)


def half_minmod(left, right):
    return jnp.minimum(
        jnp.maximum(left, jnp.minimum(right, 0.0)), jnp.maximum(right, 0.0)
    )


def roll(values, shift):
    return pltpu.roll(values, shift % values.shape[-1], values.ndim - 1)


def lanes(shape):
    return lax.broadcasted_iota(jnp.int32, shape, len(shape) - 1)


def pack_kernel(volume, discharge, wet, segment, out):
    layers = volume.shape[0]
    rows = 2 * layers + 1
    groups = wet.shape[0]
    missing = 16 * 128
    label = jnp.where(wet[...] == 1, segment[...], missing).astype(F32)
    for k in range(groups):
        out[k * rows : k * rows + layers, :] = volume[:, k * 128 : (k + 1) * 128]
        out[k * rows + layers : k * rows + 2 * layers, :] = discharge[:, k * 128 : (k + 1) * 128]
        out[k * rows + 2 * layers : (k + 1) * rows, :] = label[k : k + 1, :]


def pack_slots(volume, discharge, wet, segment):
    layers, fine = volume.shape
    groups = fine // 128
    rows = 2 * layers + 1
    step = 32 if groups % 32 == 0 else 8
    return pl.pallas_call(
        pack_kernel,
        grid=(groups // step,),
        in_specs=[
            pl.BlockSpec((layers, step * 128), lambda i: (0, i)),
            pl.BlockSpec((layers, step * 128), lambda i: (0, i)),
            pl.BlockSpec((step, 128), lambda i: (i, 0)),
            pl.BlockSpec((step, 128), lambda i: (i, 0)),
        ],
        out_specs=pl.BlockSpec((step * rows, 128), lambda i: (i, 0)),
        out_shape=jax.ShapeDtypeStruct((groups * rows, 128), F32),
        compiler_params=pltpu.CompilerParams(vmem_limit_bytes=PACK_VMEM_BYTES),
        cost_estimate=pl.CostEstimate(flops=0, bytes_accessed=8 * 10**6, transcendentals=0),
        name="pack_slots",
    )(volume, discharge, wet.reshape(groups, 128), segment.reshape(groups, 128))


def places(shape):
    return lanes(shape) % 8


def pack_layer(rows_of_layer):
    packed = None
    for i, values in enumerate(rows_of_layer):
        moved = roll(values, 8 * i + 4)
        packed = moved if i == 0 else jnp.where(lanes(moved.shape) // 8 == i, moved, packed)
    return packed


def narrow(edges, low, high):
    even, odd = (edges[low], edges[high])
    place = places(even.shape)
    return jnp.where((place >= 2) & (place < 6), even, roll(odd, 4))


def widen(sent, layer):
    tile = sent[layer // 2]
    return tile if layer % 2 == 0 else roll(tile, -4)


def edge_divergence(own, left, right, flows_own, flows_left):
    place = places(own.shape)

    def divergence(four, flows):
        step = 0.5 * (roll(four, -1) - four)
        slope = half_minmod(roll(step, 1), step)
        flux = jnp.maximum(flows, 0.0) * (four + slope) + jnp.minimum(flows, 0.0) * roll(
            four - slope, -1
        )
        return flux - roll(flux, 1)

    first = divergence(
        jnp.where(place >= 4, own, left),
        jnp.where(places(flows_own.shape) >= 4, flows_own, flows_left),
    )
    last = divergence(jnp.where(place < 4, own, right), flows_own)
    return jnp.where(place < 4, last, first)


def edge_pass(edges, left, right, flow_edges, flow_left, fixes):
    layers = fixes.shape[0]
    flows_sent = layers // 2
    for l in range(layers):
        flow = flow_edges[layers, l : l + 1, :]
        other = flow_left[flows_sent, l // 2 : l // 2 + 1, :]
        fixes[l] = edge_divergence(
            edges[l],
            widen(left, l),
            widen(right, l),
            flow,
            other if l % 2 == 0 else roll(other, -4),
        )


def at_edges(shape):
    lane = lanes(shape)
    return (lane < 2) | (lane >= 126)


def emit_sent(edges, sent, with_flows):
    layers = edges.shape[0] - (1 if with_flows else 0)
    for t in range(layers // 2):
        sent[t] = narrow(edges, 2 * t, 2 * t + 1)
        if with_flows:
            even = edges[layers, 2 * t : 2 * t + 1, :]
            odd = edges[layers, 2 * t + 1 : 2 * t + 2, :]
            place = places(even.shape)
            sent[layers // 2, t : t + 1, :] = jnp.where(
                (place >= 2) & (place < 6), even, roll(odd, 4)
            )


def start_kernel(
    last, conc, flow_x, flow_y, wet_x, wet_y, state, low_x, high_x, edges, sent, qx, qy
):
    layers, rows = flow_x.shape[0], flow_x.shape[1]
    subs = conc.shape[0] // (layers * rows)
    row = lax.broadcasted_iota(jnp.int32, flow_x.shape, 1)
    col = lax.broadcasted_iota(jnp.int32, flow_x.shape, 2)
    keep_x = jnp.where((row == rows - 1) & (last[0] == 1), 0.0, 1.0)
    keep_y = jnp.where((col == 127) & (last[1] == 1), 0.0, 1.0)
    qx[...] = flow_x[...] * wet_x[...].astype(F32) * keep_x
    qy[...] = flow_y[...] * wet_y[...].astype(F32) * keep_y
    high_x[layers] = jnp.zeros_like(high_x[layers])
    edges[layers] = jnp.zeros_like(edges[layers])
    sent[layers // 2] = jnp.zeros_like(sent[layers // 2])

    def layer(l, carry):
        values = []
        for i in range(rows):
            c = conc[pl.ds(l * rows + i, subs, stride=layers * rows), :]
            values.append(c)
            state[l, i] = c
            if i < 2:
                low_x[l, i] = c
            if i >= rows - 2:
                high_x[l, i - rows + 2] = c
        edges[l] = pack_layer(values)
        edges[layers, pl.ds(l, 1), :] = pack_layer([qy[l, i : i + 1, :] for i in range(rows)])
        high_x[layers, 0, pl.ds(l, 1), :] = qx[l, rows - 1 :, :]
        return carry

    lax.fori_loop(0, layers, layer, 0)
    emit_sent(edges, sent, True)


def start(last, conc, flow_x, flow_y, wet_x, wet_y):
    subs, layers, rows, cols = conc.shape
    flows = jax.ShapeDtypeStruct(flow_x.shape, F32)
    return pl.pallas_call(
        start_kernel,
        in_specs=[SMEM] + [VMEM] * 5,
        out_specs=[VMEM] * 7,
        out_shape=[
            jax.ShapeDtypeStruct((layers, rows, subs, cols), F32),
            jax.ShapeDtypeStruct((layers, 2, subs, cols), F32),
            jax.ShapeDtypeStruct((layers + 1, 2, subs, cols), F32),
            jax.ShapeDtypeStruct((layers + 1, subs, cols), F32),
            jax.ShapeDtypeStruct((layers // 2 + 1, subs, cols), F32),
            flows,
            flows,
        ],
        compiler_params=pltpu.CompilerParams(vmem_limit_bytes=VMEM_BYTES),
        cost_estimate=pl.CostEstimate(flops=10**6, bytes_accessed=8 * 10**6, transcendentals=0),
        name="start_state",
    )(last, conc.reshape(subs * layers * rows, cols), flow_x, flow_y, wet_x, wet_y)


def y_divergence(c, flows):
    before = [roll(v, 1) for v in c]
    after = [roll(v, -1) for v in c]
    slope = [0.5 * half_minmod(v - b, a - v) for v, b, a in zip(c, before, after)]
    right = [roll(v - s, -1) for v, s in zip(c, slope)]
    flux = [
        jnp.maximum(q, 0.0) * (v + s) + jnp.minimum(q, 0.0) * r
        for q, v, s, r in zip(flows, c, slope, right)
    ]
    return [f - roll(f, 1) for f in flux]


def x_faces(get, flow, first, last):
    here = get(first)
    step = 0.5 * (here - get(first - 1))
    fluxes = []
    left = None
    for i in range(first, last + 2):
        after = get(i + 1)
        step_after = 0.5 * (after - here)
        slope = half_minmod(step, step_after)
        if i > first:
            q = flow(i - 1)
            fluxes.append(
                jnp.maximum(q, 0.0) * left + jnp.minimum(q, 0.0) * (here - slope)
            )
        left = here + slope
        here, step = (after, step_after)
    return fluxes


def x_rows(state, west, east, l, rows):
    def get(i):
        if i < 0:
            return west[l, i + 2]
        if i >= rows:
            return east[l, i - rows]
        return state[l, i]

    return get


def x_flows(qx, qx_west, l):
    return lambda i: qx_west if i < 0 else qx[l, i : i + 1, :]


def first_divergence_kernel(state, qx, qy, div):
    layers, rows = qx.shape[0], qx.shape[1]
    edge = at_edges(state.shape[2:])

    def layer(l, carry):
        c = [state[l, i] for i in range(rows)]
        parts = y_divergence(c, [qy[l, i : i + 1, :] for i in range(rows)])
        faces = x_faces(x_rows(state, None, None, l, rows), x_flows(qx, None, l), 1, rows - 3)
        for i in range(rows):
            value = jnp.where(edge, 0.0, parts[i])
            if 2 <= i < rows - 2:
                value = value + (faces[i - 1] - faces[i - 2])
            div[l, i] = value
        return carry

    lax.fori_loop(0, layers, layer, 0)


def first_divergence(state, qx, qy):
    return pl.pallas_call(
        first_divergence_kernel,
        in_specs=[VMEM] * 3,
        out_specs=VMEM,
        out_shape=jax.ShapeDtypeStruct(state.shape, F32),
        compiler_params=pltpu.CompilerParams(vmem_limit_bytes=VMEM_BYTES),
        cost_estimate=pl.CostEstimate(flops=2 * 10**7, bytes_accessed=10**7, transcendentals=0),
        name="first_divergence",
    )(state, qx, qy)


def explicit_value(c, div, rates, rates_before, inflow, renewal, scale):
    carried = pltpu.roll(c, 1, 0)
    return (
        c
        + ((renewal * (inflow - c) - scale * div) + (rates_before * carried - rates * c))
    )


def solve(star, coef, emit):
    layers, rows = star.shape[0], star.shape[1]
    batch = 4

    def some(b, carry):
        ids = [b * batch + j for j in range(batch)]

        def get(which, l, i):
            return coef[which, l, pl.ds(i, 1), :]

        value = [star[0, i] for i in ids]
        for l in range(1, layers):
            value = [star[l, i] - get(0, l, i) * v for i, v in zip(ids, value)]
            for i, v in zip(ids, value):
                star[l, i] = v
        value = [v * get(1, layers - 1, i) for i, v in zip(ids, value)]
        for i, v in zip(ids, value):
            emit(layers - 1, i, v)
        for l in range(layers - 2, -1, -1):
            value = [
                (star[l, i] + get(2, l, i) * v) * get(1, l, i) for i, v in zip(ids, value)
            ]
            for i, v in zip(ids, value):
                emit(l, i, v)
        return carry

    lax.fori_loop(0, rows // batch, some, 0)


def emit_edges(state, low_x, high_x, edges, sent):
    layers, rows = state.shape[0], state.shape[1]
    low_x[...] = state[:, :2]
    high_x[...] = state[:, rows - 2 :]

    def layer(l, carry):
        edges[l] = pack_layer([state[l, i] for i in range(rows)])
        return carry

    lax.fori_loop(0, layers, layer, 0)
    emit_sent(edges, sent, False)


def spread_slots(slots, chunk, terms, spread, hot):
    rows = 21
    halves = spread.shape[1] // 128
    sub8 = lax.broadcasted_iota(jnp.int32, (8, 128), 0)
    column = lax.broadcasted_iota(jnp.int32, (128, 128), 0).astype(F32).astype(BF16)
    base = pl.multiple_of(chunk * (halves * rows), 8)
    values = slots[pl.ds(base, halves * rows), :]
    high = values.astype(BF16).astype(F32)
    terms[0] = high
    terms[1] = values - high
    for j in range(halves):
        to = slice(j * 128, (j + 1) * 128)

        def term(which, ch):
            at = j * rows + ch
            return terms[which, at : at + 1, :]

        label = (term(0, 20) + term(1, 20)).astype(jnp.int32)
        mask = jnp.where(jnp.broadcast_to((label >> 7) & 7, (8, 128)) == sub8, 1.0, 0.0)
        mask = jnp.concatenate([mask, mask], axis=0).astype(BF16)
        for ch in range(20):
            both = [jnp.broadcast_to(term(which, ch), (8, 128)) for which in range(2)]
            both = jnp.concatenate(both, axis=0).astype(BF16)
            spread[ch * 16 : (ch + 1) * 16, to] = both * mask
        place = jnp.broadcast_to((label & 127).astype(F32), (16, 128)).astype(BF16)
        half = label >> 10
        hits = [
            jnp.broadcast_to(jnp.where(half == h, 1.0, 0.0), (16, 128)).astype(BF16)
            for h in range(2)
        ]
        zero = jnp.zeros((16, 128), BF16)
        for g in range(8):
            same = column[g * 16 : (g + 1) * 16] == place
            for h in range(2):
                at = h * 128 + g * 16
                hot[at : at + 16, to] = jnp.where(same, hits[h], zero)


def aggregate(slots, terms, spread, hot, total):
    total[...] = jnp.zeros_like(total)

    def chunk(i, carry):
        spread_slots(slots, i, terms, spread, hot)
        total[...] += lax.dot_general(
            spread[...], hot[...], (((1,), (1,)), ((), ())), preferred_element_type=F32
        )
        return carry

    lax.fori_loop(0, slots.shape[0] // terms.shape[1], chunk, 0)


def factorize(total, base_volume, diffusivity, coef):
    layers = base_volume.shape[0]
    uppers, downs = ([], [])
    for l in range(layers):
        parts = []
        for ch in (l, layers + l):
            parts.append(
                jnp.concatenate(
                    [
                        total[ch * 16 : ch * 16 + 8, h * 128 : (h + 1) * 128]
                        + total[ch * 16 + 8 : ch * 16 + 16, h * 128 : (h + 1) * 128]
                        for h in range(2)
                    ],
                    axis=0,
                )
            )
        scale = STEP / (base_volume[l] + parts[0])
        coef[3, l] = scale
        coef[4, l] = scale * parts[1]
        uppers.append(scale * diffusivity[l] if l < layers - 1 else jnp.zeros_like(scale))
        downs.append(scale * diffusivity[l - 1] if l > 0 else jnp.zeros_like(scale))
    pivot = 1.0 + uppers[0]
    coef[0, 0] = jnp.zeros_like(pivot)
    for l in range(layers):
        inverse = 1.0 / pivot
        coef[1, l] = inverse
        coef[2, l] = uppers[l]
        if l + 1 < layers:
            factor = -downs[l + 1] * inverse
            coef[0, l + 1] = factor
            pivot = 1.0 + uppers[l + 1] + downs[l + 1] + factor * uppers[l]


def first_step_kernel(
    slots,
    base_volume,
    diffusivity,
    state,
    div,
    west,
    east,
    edges_before,
    left,
    right,
    qx,
    rates,
    rates_before,
    inflow,
    new,
    low_x,
    high_x,
    edges,
    sent,
    coef,
    terms,
    spread,
    hot,
    total,
    fixes,
    star,
):
    layers, rows = base_volume.shape[0], base_volume.shape[1]
    aggregate(slots, terms, spread, hot, total)
    factorize(total, base_volume, diffusivity, coef)
    edge_pass(edges_before, left, right, edges_before, left, fixes)
    edge = at_edges(state.shape[2:])

    def explicit(l, carry):
        get = x_rows(state, west, east, l, rows)
        flow = x_flows(qx, west[layers, 0, pl.ds(l, 1), :], l)
        low = x_faces(get, flow, -1, 1)
        high = x_faces(get, flow, rows - 3, rows - 1)
        fix = [roll(fixes[l], 124 - 8 * i) for i in range(rows)]
        for i in range(rows):
            value = div[l, i] + jnp.where(edge, fix[i], 0.0)
            if i < 2:
                value = value + (low[i + 1] - low[i])
            if i >= rows - 2:
                j = i - rows + 3
                value = value + (high[j] - high[j - 1])
            star[l, i] = explicit_value(
                state[l, i],
                value,
                rates[...],
                rates_before[...],
                inflow[...],
                coef[4, l, i : i + 1, :],
                coef[3, l, i : i + 1, :],
            )
        return carry

    lax.fori_loop(0, layers, explicit, 0)

    def emit(l, i, value):
        new[l, i] = value

    solve(star, coef, emit)
    emit_edges(new, low_x, high_x, edges, sent)


def state_shapes(shape):
    layers, rows, subs, cols = shape
    return [
        jax.ShapeDtypeStruct(shape, F32),
        jax.ShapeDtypeStruct((layers, 2, subs, cols), F32),
        jax.ShapeDtypeStruct((layers, 2, subs, cols), F32),
        jax.ShapeDtypeStruct((layers, subs, cols), F32),
        jax.ShapeDtypeStruct((layers // 2, subs, cols), F32),
    ]


def first_step(slots, base_volume, diffusivity, state, *args):
    layers, rows, subs, cols = state.shape
    depth = min(2048, slots.shape[0] // 21 * 128)
    return pl.pallas_call(
        first_step_kernel,
        in_specs=[VMEM] * 14,
        out_specs=[VMEM] * 6,
        out_shape=state_shapes(state.shape)
        + [jax.ShapeDtypeStruct((5, layers, rows, cols), F32)],
        scratch_shapes=[
            pltpu.VMEM((2, depth // 128 * 21, 128), F32),
            pltpu.VMEM((2 * layers * 16, depth), BF16),
            pltpu.VMEM((256, depth), BF16),
            pltpu.VMEM((2 * layers * 16, 256), F32),
            pltpu.VMEM((layers, subs, cols), F32),
            pltpu.VMEM(state.shape, F32),
        ],
        compiler_params=pltpu.CompilerParams(vmem_limit_bytes=VMEM_BYTES),
        cost_estimate=pl.CostEstimate(flops=10**9, bytes_accessed=10**7, transcendentals=0),
        name="aggregate_and_first_step",
    )(slots, base_volume, diffusivity, state, *args)


def later_step_kernel(
    final,
    state,
    west,
    east,
    edges_before,
    left,
    right,
    flow_west,
    flow_edges,
    flow_left,
    qx,
    qy,
    coef,
    rates,
    rates_before,
    inflow,
    *refs,
):
    layers, rows = qx.shape[0], qx.shape[1]
    if final:
        out, fixes, star = refs
        subs = out.shape[0] // (layers * rows)
    else:
        new, low_x, high_x, edges, sent, fixes, star = refs
    edge_pass(edges_before, left, right, flow_edges, flow_left, fixes)
    edge = at_edges(state.shape[2:])

    def layer(l, carry):
        c = [state[l, i] for i in range(rows)]
        fix = [roll(fixes[l], 124 - 8 * i) for i in range(rows)]
        parts = y_divergence(c, [qy[l, i : i + 1, :] for i in range(rows)])
        parts = [jnp.where(edge, f, p) for f, p in zip(fix, parts)]
        flow = x_flows(qx, flow_west[layers, 0, pl.ds(l, 1), :], l)
        faces = x_faces(x_rows(state, west, east, l, rows), flow, -1, rows - 1)
        for i in range(rows):
            star[l, i] = explicit_value(
                state[l, i],
                parts[i] + (faces[i + 1] - faces[i]),
                rates[...],
                rates_before[...],
                inflow[...],
                coef[4, l, i : i + 1, :],
                coef[3, l, i : i + 1, :],
            )
        return carry

    lax.fori_loop(0, layers, layer, 0)

    def emit(l, i, value):
        if final:
            out[pl.ds(l * rows + i, subs, stride=layers * rows), :] = value
        else:
            new[l, i] = value

    solve(star, coef, emit)
    if not final:
        emit_edges(new, low_x, high_x, edges, sent)


def later_step(final, state, *args):
    layers, rows, subs, cols = state.shape
    if final:
        shapes = jax.ShapeDtypeStruct((subs * layers * rows, cols), F32)
        specs = VMEM
    else:
        shapes = state_shapes(state.shape)
        specs = [VMEM] * 5
    return pl.pallas_call(
        functools.partial(later_step_kernel, final),
        in_specs=[VMEM] * 15,
        out_specs=specs,
        out_shape=shapes,
        scratch_shapes=[pltpu.VMEM((layers, subs, cols), F32), pltpu.VMEM(state.shape, F32)],
        compiler_params=pltpu.CompilerParams(vmem_limit_bytes=VMEM_BYTES),
        cost_estimate=pl.CostEstimate(flops=3 * 10**7, bytes_accessed=10**7, transcendentals=0),
        name="last_step" if final else "middle_step",
    )(state, *args)


def to_next(values, axis):
    size = lax.axis_size(axis)
    return lax.ppermute(values, axis, [(i, i + 1) for i in range(size - 1)])


def to_previous(values, axis):
    size = lax.axis_size(axis)
    return lax.ppermute(values, axis, [(i + 1, i) for i in range(size - 1)])


def exchange(low_x, high_x, sent):
    west = to_next(high_x, "gx")
    east = to_previous(low_x, "gx")
    left = to_next(sent, "gy")
    right = to_previous(sent, "gy")
    return (west, east, left, right)


def local(
    concentration,
    base_volume,
    flow_x,
    flow_y,
    face_wet_x,
    face_wet_y,
    diffusivity,
    decay_rates,
    inflow,
    fine_volume,
    fine_discharge,
    cell_wet,
    seg_local,
):
    subs, layers, rows, cols = concentration.shape
    size_x, size_y = (lax.axis_size("gx"), lax.axis_size("gy"))
    owners = size_x * size_y
    slots = pack_slots(fine_volume, fine_discharge, cell_wet, seg_local)
    arrived = lax.all_to_all(
        slots.reshape(owners, 1, -1), ("gx", "gy"), split_axis=0, concat_axis=0, tiled=True
    ).reshape(slots.shape)

    last = jnp.stack(
        [
            (lax.axis_index("gx") == size_x - 1).astype(jnp.int32),
            (lax.axis_index("gy") == size_y - 1).astype(jnp.int32),
        ]
    )
    rates = jnp.concatenate([jnp.zeros((1,), F32), decay_rates]) * STEP
    rates_before = jnp.concatenate([jnp.zeros((1,), F32), rates[:-1]])
    rates, rates_before, inflow = (
        jnp.broadcast_to(v[:, None], (subs, cols)) for v in (rates, rates_before, inflow)
    )
    state, low_x, high_x, edges, sent, qx, qy = start(
        last, concentration, flow_x, flow_y, face_wet_x, face_wet_y
    )
    west, east, left, right = exchange(low_x, high_x, sent)
    flow_west, flow_edges, flow_left = (west, edges, left)
    div = first_divergence(state, qx, qy)
    constants = (rates, rates_before, inflow)
    state, low_x, high_x, edges, sent, coef = first_step(
        arrived, base_volume, diffusivity, state, div, west, east, edges, left, right, qx, *constants
    )
    for step in range(1, SUBSTEPS):
        final = step == SUBSTEPS - 1
        west, east, left, right = exchange(low_x, high_x, sent)
        flows = (flow_west, flow_edges, flow_left, qx, qy, coef)
        result = later_step(final, state, west, east, edges, left, right, *flows, *constants)
        if not final:
            state, low_x, high_x, edges, sent = result
    return result.reshape(concentration.shape)


def solution(mesh):
    fine = P(None, ("gx", "gy"))
    block = P(None, "gx", "gy")
    return jax.shard_map(
        local,
        mesh=mesh,
        in_specs=(
            P(None, None, "gx", "gy"),
            block,
            block,
            block,
            block,
            block,
            block,
            P(),
            P(),
            fine,
            fine,
            P(("gx", "gy")),
            P(("gx", "gy")),
        ),
        out_specs=P(None, None, "gx", "gy"),
        check_vma=False,
    )
```

```python
import functools

import jax
import jax.numpy as jnp
from jax import lax
from jax.experimental import pallas as pl
from jax.experimental.pallas import tpu as pltpu
from jax.sharding import PartitionSpec as P

SUBSTEPS = 3
STEP = 1.0 / SUBSTEPS
VMEM_BYTES = 24 * 1024 * 1024
PACK_VMEM_BYTES = 62 * 1024 * 1024
F32 = jnp.float32
BF16 = jnp.bfloat16

VMEM = pl.BlockSpec(memory_space=pltpu.VMEM)
SMEM = pl.BlockSpec(memory_space=pltpu.SMEM)


def half_minmod(left, right):
    return jnp.minimum(
        jnp.maximum(left, jnp.minimum(right, 0.0)), jnp.maximum(right, 0.0)
    )


def roll(values, shift):
    return pltpu.roll(values, shift % values.shape[-1], values.ndim - 1)


def lanes(shape):
    return lax.broadcasted_iota(jnp.int32, shape, len(shape) - 1)


def pack_kernel(volume, discharge, wet, segment, out):
    layers = volume.shape[0]
    rows = 2 * layers + 1
    groups = wet.shape[0]
    missing = 16 * 128
    label = jnp.where(wet[...] == 1, segment[...], missing).astype(F32)
    for k in range(groups):
        out[k * rows : k * rows + layers, :] = volume[:, k * 128 : (k + 1) * 128]
        out[k * rows + layers : k * rows + 2 * layers, :] = discharge[:, k * 128 : (k + 1) * 128]
        out[k * rows + 2 * layers : (k + 1) * rows, :] = label[k : k + 1, :]


def pack_slots(volume, discharge, wet, segment):
    layers, fine = volume.shape
    groups = fine // 128
    rows = 2 * layers + 1
    step = 128 if groups % 128 == 0 else groups
    return pl.pallas_call(
        pack_kernel,
        grid=(groups // step,),
        in_specs=[
            pl.BlockSpec((layers, step * 128), lambda i: (0, i)),
            pl.BlockSpec((layers, step * 128), lambda i: (0, i)),
            pl.BlockSpec((step, 128), lambda i: (i, 0)),
            pl.BlockSpec((step, 128), lambda i: (i, 0)),
        ],
        out_specs=pl.BlockSpec((step * rows, 128), lambda i: (i, 0)),
        out_shape=jax.ShapeDtypeStruct((groups * rows, 128), F32),
        compiler_params=pltpu.CompilerParams(vmem_limit_bytes=PACK_VMEM_BYTES),
        cost_estimate=pl.CostEstimate(flops=0, bytes_accessed=8 * 10**6, transcendentals=0),
        name="pack_slots",
    )(volume, discharge, wet.reshape(groups, 128), segment.reshape(groups, 128))


def places(shape):
    return lanes(shape) % 8


def pack_layer(rows_of_layer):
    packed = None
    for i, values in enumerate(rows_of_layer):
        moved = roll(values, 8 * i + 4)
        packed = moved if i == 0 else jnp.where(lanes(moved.shape) // 8 == i, moved, packed)
    return packed


def narrow(edges, low, high):
    even, odd = (edges[low], edges[high])
    place = places(even.shape)
    return jnp.where((place >= 2) & (place < 6), even, roll(odd, 4))


def widen(tile, layer):
    return tile if layer % 2 == 0 else roll(tile, -4)


def edge_divergence(own, left, right, flows_own, flows_left):
    place = places(own.shape)

    def divergence(four, flows):
        step = 0.5 * (roll(four, -1) - four)
        slope = half_minmod(roll(step, 1), step)
        flux = jnp.maximum(flows, 0.0) * (four + slope) + jnp.minimum(flows, 0.0) * roll(
            four - slope, -1
        )
        return flux - roll(flux, 1)

    first = divergence(
        jnp.where(place >= 4, own, left),
        jnp.where(places(flows_own.shape) >= 4, flows_own, flows_left),
    )
    last = divergence(jnp.where(place < 4, own, right), flows_own)
    return jnp.where(place < 4, last, first)


def edge_pass(place, edges, edges_swapped, flow_edges, flow_swapped, fixes):
    layers = fixes.shape[0]
    odd = place[3] == 1
    for l in range(layers):
        flow = flow_edges[layers, l : l + 1, :]
        tile = [ref[l // 2] for ref in edges_swapped]
        other = jnp.where(
            odd, *[ref[layers // 2, l // 2 : l // 2 + 1, :] for ref in flow_swapped]
        )
        fixes[l] = edge_divergence(
            edges[l],
            widen(jnp.where(odd, tile[0], tile[1]), l),
            widen(jnp.where(odd, tile[1], tile[0]), l),
            flow,
            widen(other, l),
        )


def at_edges(shape):
    lane = lanes(shape)
    return (lane < 2) | (lane >= 126)


def emit_swaps(place, state, swap_a, swap_b):
    layers, rows = state.shape[0], state.shape[1]
    low = place[2] * (rows - 2)
    swap_b[:layers] = state[:, pl.ds(low, 2)]
    swap_a[:layers] = state[:, pl.ds(rows - 2 - low, 2)]


def emit_sent(edges, sent, with_flows):
    layers = edges.shape[0] - (1 if with_flows else 0)
    for t in range(layers // 2):
        sent[t] = narrow(edges, 2 * t, 2 * t + 1)
        if with_flows:
            even = edges[layers, 2 * t : 2 * t + 1, :]
            odd = edges[layers, 2 * t + 1 : 2 * t + 2, :]
            place = places(even.shape)
            sent[layers // 2, t : t + 1, :] = jnp.where(
                (place >= 2) & (place < 6), even, roll(odd, 4)
            )


def start_kernel(
    place, conc, flow_x, flow_y, wet_x, wet_y, state, swap_a, swap_b, edges, sent, qx, qy
):
    layers, rows = flow_x.shape[0], flow_x.shape[1]
    subs = conc.shape[0] // (layers * rows)
    row = lax.broadcasted_iota(jnp.int32, flow_x.shape, 1)
    col = lax.broadcasted_iota(jnp.int32, flow_x.shape, 2)
    keep_x = jnp.where((row == rows - 1) & (place[0] == 1), 0.0, 1.0)
    keep_y = jnp.where((col == 127) & (place[1] == 1), 0.0, 1.0)
    qx[...] = flow_x[...] * wet_x[...].astype(F32) * keep_x
    qy[...] = flow_y[...] * wet_y[...].astype(F32) * keep_y
    for swap in (swap_a, swap_b):
        swap[layers] = jnp.zeros_like(swap[layers])
    edges[layers] = jnp.zeros_like(edges[layers])
    sent[layers // 2] = jnp.zeros_like(sent[layers // 2])

    def layer(l, carry):
        values = []
        for i in range(rows):
            c = conc[pl.ds(l * rows + i, subs, stride=layers * rows), :]
            values.append(c)
            state[l, i] = c
        edges[l] = pack_layer(values)
        edges[layers, pl.ds(l, 1), :] = pack_layer([qy[l, i : i + 1, :] for i in range(rows)])
        for swap in (swap_a, swap_b):
            swap[layers, 0, pl.ds(l, 1), :] = qx[l, rows - 1 :, :]
        return carry

    lax.fori_loop(0, layers, layer, 0)
    emit_swaps(place, state, swap_a, swap_b)
    emit_sent(edges, sent, True)


def start(place, conc, flow_x, flow_y, wet_x, wet_y):
    subs, layers, rows, cols = conc.shape
    flows = jax.ShapeDtypeStruct(flow_x.shape, F32)
    return pl.pallas_call(
        start_kernel,
        in_specs=[SMEM] + [VMEM] * 5,
        out_specs=[VMEM] * 7,
        out_shape=[
            jax.ShapeDtypeStruct((layers, rows, subs, cols), F32),
            jax.ShapeDtypeStruct((layers + 1, 2, subs, cols), F32),
            jax.ShapeDtypeStruct((layers + 1, 2, subs, cols), F32),
            jax.ShapeDtypeStruct((layers + 1, subs, cols), F32),
            jax.ShapeDtypeStruct((layers // 2 + 1, subs, cols), F32),
            flows,
            flows,
        ],
        compiler_params=pltpu.CompilerParams(vmem_limit_bytes=VMEM_BYTES),
        cost_estimate=pl.CostEstimate(flops=10**6, bytes_accessed=8 * 10**6, transcendentals=0),
        name="start_state",
    )(place, conc.reshape(subs * layers * rows, cols), flow_x, flow_y, wet_x, wet_y)


def y_divergence(c, flows):
    before = [roll(v, 1) for v in c]
    after = [roll(v, -1) for v in c]
    slope = [0.5 * half_minmod(v - b, a - v) for v, b, a in zip(c, before, after)]
    right = [roll(v - s, -1) for v, s in zip(c, slope)]
    flux = [
        jnp.maximum(q, 0.0) * (v + s) + jnp.minimum(q, 0.0) * r
        for q, v, s, r in zip(flows, c, slope, right)
    ]
    return [f - roll(f, 1) for f in flux]


def x_faces(get, flow, first, last):
    here = get(first)
    step = 0.5 * (here - get(first - 1))
    fluxes = []
    left = None
    for i in range(first, last + 2):
        after = get(i + 1)
        step_after = 0.5 * (after - here)
        slope = half_minmod(step, step_after)
        if i > first:
            q = flow(i - 1)
            fluxes.append(
                jnp.maximum(q, 0.0) * left + jnp.minimum(q, 0.0) * (here - slope)
            )
        left = here + slope
        here, step = (after, step_after)
    return fluxes


def x_rows(state, place, swapped, l, rows):
    def get(i):
        if 0 <= i < rows:
            return state[l, i]
        j = i + 2 if i < 0 else i - rows
        pair = [ref[l, j] for ref in (swapped if i < 0 else swapped[::-1])]
        return jnp.where(place[2] == 1, *pair)

    return get


def x_flows(qx, qx_west, l):
    return lambda i: qx_west if i < 0 else qx[l, i : i + 1, :]


def west_flow(place, flow_swapped, layers, l):
    return jnp.where(place[2] == 1, *[ref[layers, 0, pl.ds(l, 1), :] for ref in flow_swapped])


def first_divergence_kernel(state, qx, qy, div):
    layers, rows = qx.shape[0], qx.shape[1]
    edge = at_edges(state.shape[2:])

    def layer(l, carry):
        c = [state[l, i] for i in range(rows)]
        parts = y_divergence(c, [qy[l, i : i + 1, :] for i in range(rows)])
        faces = x_faces(x_rows(state, None, None, l, rows), x_flows(qx, None, l), 1, rows - 3)
        for i in range(rows):
            value = jnp.where(edge, 0.0, parts[i])
            if 2 <= i < rows - 2:
                value = value + (faces[i - 1] - faces[i - 2])
            div[l, i] = value
        return carry

    lax.fori_loop(0, layers, layer, 0)


def first_divergence(state, qx, qy):
    return pl.pallas_call(
        first_divergence_kernel,
        in_specs=[VMEM] * 3,
        out_specs=VMEM,
        out_shape=jax.ShapeDtypeStruct(state.shape, F32),
        compiler_params=pltpu.CompilerParams(vmem_limit_bytes=VMEM_BYTES),
        cost_estimate=pl.CostEstimate(flops=2 * 10**7, bytes_accessed=10**7, transcendentals=0),
        name="first_divergence",
    )(state, qx, qy)


def explicit_value(c, div, rates, rates_before, inflow, renewal, scale):
    carried = pltpu.roll(c, 1, 0)
    return (
        c
        + ((renewal * (inflow - c) - scale * div) + (rates_before * carried - rates * c))
    )


def solve(star, coef, emit):
    layers, rows = star.shape[0], star.shape[1]
    batch = 4

    def some(b, carry):
        ids = [b * batch + j for j in range(batch)]

        def get(which, l, i):
            return coef[which, l, pl.ds(i, 1), :]

        value = [star[0, i] for i in ids]
        for l in range(1, layers):
            value = [star[l, i] - get(0, l, i) * v for i, v in zip(ids, value)]
            for i, v in zip(ids, value):
                star[l, i] = v
        value = [v * get(1, layers - 1, i) for i, v in zip(ids, value)]
        for i, v in zip(ids, value):
            emit(layers - 1, i, v)
        for l in range(layers - 2, -1, -1):
            value = [
                (star[l, i] + get(2, l, i) * v) * get(1, l, i) for i, v in zip(ids, value)
            ]
            for i, v in zip(ids, value):
                emit(l, i, v)
        return carry

    lax.fori_loop(0, rows // batch, some, 0)


def emit_edges(place, state, swap_a, swap_b, edges, sent):
    layers, rows = state.shape[0], state.shape[1]
    emit_swaps(place, state, swap_a, swap_b)

    def layer(l, carry):
        edges[l] = pack_layer([state[l, i] for i in range(rows)])
        return carry

    lax.fori_loop(0, layers, layer, 0)
    emit_sent(edges, sent, False)


def spread_slots(slots, chunk, terms, spread, hot):
    rows = 21
    halves = spread.shape[1] // 128
    sub8 = lax.broadcasted_iota(jnp.int32, (8, 128), 0)
    column = lax.broadcasted_iota(jnp.int32, (128, 128), 0).astype(F32).astype(BF16)
    base = pl.multiple_of(chunk * (halves * rows), 8)
    values = slots[pl.ds(base, halves * rows), :]
    high = values.astype(BF16).astype(F32)
    terms[0] = high
    terms[1] = values - high
    for j in range(halves):
        to = slice(j * 128, (j + 1) * 128)

        def term(which, ch):
            at = j * rows + ch
            return terms[which, at : at + 1, :]

        label = (term(0, 20) + term(1, 20)).astype(jnp.int32)
        mask = jnp.where(jnp.broadcast_to((label >> 7) & 7, (8, 128)) == sub8, 1.0, 0.0)
        mask = jnp.concatenate([mask, mask], axis=0).astype(BF16)
        for ch in range(20):
            both = [jnp.broadcast_to(term(which, ch), (8, 128)) for which in range(2)]
            both = jnp.concatenate(both, axis=0).astype(BF16)
            spread[ch * 16 : (ch + 1) * 16, to] = both * mask
        place = jnp.broadcast_to((label & 127).astype(F32), (16, 128)).astype(BF16)
        half = label >> 10
        hits = [
            jnp.broadcast_to(jnp.where(half == h, 1.0, 0.0), (16, 128)).astype(BF16)
            for h in range(2)
        ]
        zero = jnp.zeros((16, 128), BF16)
        for g in range(8):
            same = column[g * 16 : (g + 1) * 16] == place
            for h in range(2):
                at = h * 128 + g * 16
                hot[at : at + 16, to] = jnp.where(same, hits[h], zero)


def aggregate(slots, terms, spread, hot, total):
    total[...] = jnp.zeros_like(total)

    def chunk(i, carry):
        spread_slots(slots, i, terms, spread, hot)
        total[...] += lax.dot_general(
            spread[...], hot[...], (((1,), (1,)), ((), ())), preferred_element_type=F32
        )
        return carry

    lax.fori_loop(0, slots.shape[0] // terms.shape[1], chunk, 0)


def factorize(total, base_volume, diffusivity, coef):
    layers = base_volume.shape[0]
    uppers, downs = ([], [])
    for l in range(layers):
        parts = []
        for ch in (l, layers + l):
            parts.append(
                jnp.concatenate(
                    [
                        total[ch * 16 : ch * 16 + 8, h * 128 : (h + 1) * 128]
                        + total[ch * 16 + 8 : ch * 16 + 16, h * 128 : (h + 1) * 128]
                        for h in range(2)
                    ],
                    axis=0,
                )
            )
        scale = STEP / (base_volume[l] + parts[0])
        coef[3, l] = scale
        coef[4, l] = scale * parts[1]
        uppers.append(scale * diffusivity[l] if l < layers - 1 else jnp.zeros_like(scale))
        downs.append(scale * diffusivity[l - 1] if l > 0 else jnp.zeros_like(scale))
    pivot = 1.0 + uppers[0]
    coef[0, 0] = jnp.zeros_like(pivot)
    for l in range(layers):
        inverse = 1.0 / pivot
        coef[1, l] = inverse
        coef[2, l] = uppers[l]
        if l + 1 < layers:
            factor = -downs[l + 1] * inverse
            coef[0, l + 1] = factor
            pivot = 1.0 + uppers[l + 1] + downs[l + 1] + factor * uppers[l]


def first_step_kernel(
    place,
    slots,
    base_volume,
    diffusivity,
    state,
    div,
    received_a,
    received_b,
    edges_before,
    edges_a,
    edges_b,
    qx,
    rates,
    rates_before,
    inflow,
    new,
    swap_a,
    swap_b,
    edges,
    sent,
    coef,
    terms,
    spread,
    hot,
    total,
    fixes,
    star,
):
    layers, rows = base_volume.shape[0], base_volume.shape[1]
    aggregate(slots, terms, spread, hot, total)
    factorize(total, base_volume, diffusivity, coef)
    received = (received_a, received_b)
    edges_swapped = (edges_a, edges_b)
    edge_pass(place, edges_before, edges_swapped, edges_before, edges_swapped, fixes)
    edge = at_edges(state.shape[2:])

    def explicit(l, carry):
        get = x_rows(state, place, received, l, rows)
        flow = x_flows(qx, west_flow(place, received, layers, l), l)
        low = x_faces(get, flow, -1, 1)
        high = x_faces(get, flow, rows - 3, rows - 1)
        fix = [roll(fixes[l], 124 - 8 * i) for i in range(rows)]
        for i in range(rows):
            value = div[l, i] + jnp.where(edge, fix[i], 0.0)
            if i < 2:
                value = value + (low[i + 1] - low[i])
            if i >= rows - 2:
                j = i - rows + 3
                value = value + (high[j] - high[j - 1])
            star[l, i] = explicit_value(
                state[l, i],
                value,
                rates[...],
                rates_before[...],
                inflow[...],
                coef[4, l, i : i + 1, :],
                coef[3, l, i : i + 1, :],
            )
        return carry

    lax.fori_loop(0, layers, explicit, 0)

    def emit(l, i, value):
        new[l, i] = value

    solve(star, coef, emit)
    emit_edges(place, new, swap_a, swap_b, edges, sent)


def state_shapes(shape):
    layers, rows, subs, cols = shape
    return [
        jax.ShapeDtypeStruct(shape, F32),
        jax.ShapeDtypeStruct((layers, 2, subs, cols), F32),
        jax.ShapeDtypeStruct((layers, 2, subs, cols), F32),
        jax.ShapeDtypeStruct((layers, subs, cols), F32),
        jax.ShapeDtypeStruct((layers // 2, subs, cols), F32),
    ]


def first_step(place, slots, base_volume, diffusivity, state, *args):
    layers, rows, subs, cols = state.shape
    depth = min(2048, slots.shape[0] // 21 * 128)
    return pl.pallas_call(
        first_step_kernel,
        in_specs=[SMEM] + [VMEM] * 14,
        out_specs=[VMEM] * 6,
        out_shape=state_shapes(state.shape)
        + [jax.ShapeDtypeStruct((5, layers, rows, cols), F32)],
        scratch_shapes=[
            pltpu.VMEM((2, depth // 128 * 21, 128), F32),
            pltpu.VMEM((2 * layers * 16, depth), BF16),
            pltpu.VMEM((256, depth), BF16),
            pltpu.VMEM((2 * layers * 16, 256), F32),
            pltpu.VMEM((layers, subs, cols), F32),
            pltpu.VMEM(state.shape, F32),
        ],
        compiler_params=pltpu.CompilerParams(vmem_limit_bytes=VMEM_BYTES),
        cost_estimate=pl.CostEstimate(flops=10**9, bytes_accessed=10**7, transcendentals=0),
        name="aggregate_and_first_step",
    )(place, slots, base_volume, diffusivity, state, *args)


def later_step_kernel(
    final,
    place,
    state,
    received_a,
    received_b,
    edges_before,
    edges_a,
    edges_b,
    flow_a,
    flow_b,
    flow_edges,
    flow_edges_a,
    flow_edges_b,
    qx,
    qy,
    coef,
    rates,
    rates_before,
    inflow,
    *refs,
):
    layers, rows = qx.shape[0], qx.shape[1]
    if final:
        out, fixes, star = refs
        subs = out.shape[0] // (layers * rows)
    else:
        new, swap_a, swap_b, edges, sent, fixes, star = refs
    edge_pass(
        place, edges_before, (edges_a, edges_b), flow_edges, (flow_edges_a, flow_edges_b), fixes
    )
    edge = at_edges(state.shape[2:])

    def layer(l, carry):
        c = [state[l, i] for i in range(rows)]
        fix = [roll(fixes[l], 124 - 8 * i) for i in range(rows)]
        parts = y_divergence(c, [qy[l, i : i + 1, :] for i in range(rows)])
        parts = [jnp.where(edge, f, p) for f, p in zip(fix, parts)]
        flow = x_flows(qx, west_flow(place, (flow_a, flow_b), layers, l), l)
        get = x_rows(state, place, (received_a, received_b), l, rows)
        faces = x_faces(get, flow, -1, rows - 1)
        for i in range(rows):
            star[l, i] = explicit_value(
                state[l, i],
                parts[i] + (faces[i + 1] - faces[i]),
                rates[...],
                rates_before[...],
                inflow[...],
                coef[4, l, i : i + 1, :],
                coef[3, l, i : i + 1, :],
            )
        return carry

    lax.fori_loop(0, layers, layer, 0)

    def emit(l, i, value):
        if final:
            out[pl.ds(l * rows + i, subs, stride=layers * rows), :] = value
        else:
            new[l, i] = value

    solve(star, coef, emit)
    if not final:
        emit_edges(place, new, swap_a, swap_b, edges, sent)


def later_step(final, place, state, *args):
    layers, rows, subs, cols = state.shape
    if final:
        shapes = jax.ShapeDtypeStruct((subs * layers * rows, cols), F32)
        specs = VMEM
    else:
        shapes = state_shapes(state.shape)
        specs = [VMEM] * 5
    return pl.pallas_call(
        functools.partial(later_step_kernel, final),
        in_specs=[SMEM] + [VMEM] * 17,
        out_specs=specs,
        out_shape=shapes,
        scratch_shapes=[pltpu.VMEM((layers, subs, cols), F32), pltpu.VMEM(state.shape, F32)],
        compiler_params=pltpu.CompilerParams(vmem_limit_bytes=VMEM_BYTES),
        cost_estimate=pl.CostEstimate(flops=3 * 10**7, bytes_accessed=10**7, transcendentals=0),
        name="last_step" if final else "middle_step",
    )(place, state, *args)


def swap(values, axis, first):
    pairs = [(i, i + 1) for i in range(first, lax.axis_size(axis) - 1, 2)]
    return lax.ppermute(values, axis, pairs + [(j, i) for i, j in pairs])


def exchange(swap_a, swap_b, sent):
    rows = (swap(swap_a, "gx", 0), swap(swap_b, "gx", 1))
    columns = (swap(sent, "gy", 0), swap(sent, "gy", 1))
    return (rows, columns)


def local(
    concentration,
    base_volume,
    flow_x,
    flow_y,
    face_wet_x,
    face_wet_y,
    diffusivity,
    decay_rates,
    inflow,
    fine_volume,
    fine_discharge,
    cell_wet,
    seg_local,
):
    subs, layers, rows, cols = concentration.shape
    size_x, size_y = (lax.axis_size("gx"), lax.axis_size("gy"))
    owners = size_x * size_y
    slots = pack_slots(fine_volume, fine_discharge, cell_wet, seg_local)
    arrived = lax.all_to_all(
        slots.reshape(owners, 1, -1), ("gx", "gy"), split_axis=0, concat_axis=0, tiled=True
    ).reshape(slots.shape)

    at_x, at_y = (lax.axis_index("gx"), lax.axis_index("gy"))
    place = jnp.stack(
        [
            (at_x == size_x - 1).astype(jnp.int32),
            (at_y == size_y - 1).astype(jnp.int32),
            at_x.astype(jnp.int32) % 2,
            at_y.astype(jnp.int32) % 2,
        ]
    )
    rates = jnp.concatenate([jnp.zeros((1,), F32), decay_rates]) * STEP
    rates_before = jnp.concatenate([jnp.zeros((1,), F32), rates[:-1]])
    rates, rates_before, inflow = (
        jnp.broadcast_to(v[:, None], (subs, cols)) for v in (rates, rates_before, inflow)
    )
    state, swap_a, swap_b, edges, sent, qx, qy = start(
        place, concentration, flow_x, flow_y, face_wet_x, face_wet_y
    )
    rows_in, columns_in = exchange(swap_a, swap_b, sent)
    flows = (*rows_in, edges, *columns_in, qx, qy)
    div = first_divergence(state, qx, qy)
    constants = (rates, rates_before, inflow)
    state, swap_a, swap_b, edges, sent, coef = first_step(
        place,
        arrived,
        base_volume,
        diffusivity,
        state,
        div,
        *rows_in,
        edges,
        *columns_in,
        qx,
        *constants,
    )
    for step in range(1, SUBSTEPS):
        final = step == SUBSTEPS - 1
        rows_in, columns_in = exchange(swap_a, swap_b, sent)
        result = later_step(
            final, place, state, *rows_in, edges, *columns_in, *flows, coef, *constants
        )
        if not final:
            state, swap_a, swap_b, edges, sent = result
    return result.reshape(concentration.shape)


def solution(mesh):
    fine = P(None, ("gx", "gy"))
    block = P(None, "gx", "gy")
    return jax.shard_map(
        local,
        mesh=mesh,
        in_specs=(
            P(None, None, "gx", "gy"),
            block,
            block,
            block,
            block,
            block,
            block,
            P(),
            P(),
            fine,
            fine,
            P(("gx", "gy")),
            P(("gx", "gy")),
        ),
        out_specs=P(None, None, "gx", "gy"),
        check_vma=False,
    )
```

```python
import functools

import jax
import jax.numpy as jnp
from jax import lax
from jax.experimental import pallas as pl
from jax.experimental.pallas import tpu as pltpu
from jax.sharding import PartitionSpec as P

SUBSTEPS = 3
STEP = 1.0 / SUBSTEPS
VMEM_BYTES = 24 * 1024 * 1024
PACK_VMEM_BYTES = 62 * 1024 * 1024
F32 = jnp.float32
BF16 = jnp.bfloat16

VMEM = pl.BlockSpec(memory_space=pltpu.VMEM)
SMEM = pl.BlockSpec(memory_space=pltpu.SMEM)


def half_minmod(left, right):
    return jnp.minimum(
        jnp.maximum(left, jnp.minimum(right, 0.0)), jnp.maximum(right, 0.0)
    )


def roll(values, shift):
    return pltpu.roll(values, shift % values.shape[-1], values.ndim - 1)


def lanes(shape):
    return lax.broadcasted_iota(jnp.int32, shape, len(shape) - 1)


def pack_kernel(volume, discharge, wet, segment, out):
    layers = volume.shape[0]
    rows = 2 * layers + 1
    groups = wet.shape[0]
    missing = 16 * 128
    label = jnp.where(wet[...] == 1, segment[...], missing).astype(F32)
    for k in range(groups):
        out[k * rows : k * rows + layers, :] = volume[:, k * 128 : (k + 1) * 128]
        out[k * rows + layers : k * rows + 2 * layers, :] = discharge[:, k * 128 : (k + 1) * 128]
        out[k * rows + 2 * layers : (k + 1) * rows, :] = label[k : k + 1, :]


def pack_slots(volume, discharge, wet, segment):
    layers, fine = volume.shape
    groups = fine // 128
    rows = 2 * layers + 1
    step = 128 if groups % 128 == 0 else groups
    return pl.pallas_call(
        pack_kernel,
        grid=(groups // step,),
        in_specs=[
            pl.BlockSpec((layers, step * 128), lambda i: (0, i)),
            pl.BlockSpec((layers, step * 128), lambda i: (0, i)),
            pl.BlockSpec((step, 128), lambda i: (i, 0)),
            pl.BlockSpec((step, 128), lambda i: (i, 0)),
        ],
        out_specs=pl.BlockSpec((step * rows, 128), lambda i: (i, 0)),
        out_shape=jax.ShapeDtypeStruct((groups * rows, 128), F32),
        compiler_params=pltpu.CompilerParams(vmem_limit_bytes=PACK_VMEM_BYTES),
        cost_estimate=pl.CostEstimate(flops=0, bytes_accessed=8 * 10**6, transcendentals=0),
        name="pack_slots",
    )(volume, discharge, wet.reshape(groups, 128), segment.reshape(groups, 128))


def places(shape):
    return lanes(shape) % 8


def pack_layer(rows_of_layer):
    packed = None
    for i, values in enumerate(rows_of_layer):
        moved = roll(values, 8 * i + 4)
        packed = moved if i == 0 else jnp.where(lanes(moved.shape) // 8 == i, moved, packed)
    return packed


def narrow(edges, low, high):
    even, odd = (edges[low], edges[high])
    place = places(even.shape)
    return jnp.where((place >= 2) & (place < 6), even, roll(odd, 4))


def widen(tile, layer):
    return tile if layer % 2 == 0 else roll(tile, -4)


def edge_divergence(own, left, right, flows_own, flows_left):
    place = places(own.shape)

    def divergence(four, flows):
        step = 0.5 * (roll(four, -1) - four)
        slope = half_minmod(roll(step, 1), step)
        flux = jnp.maximum(flows, 0.0) * (four + slope) + jnp.minimum(flows, 0.0) * roll(
            four - slope, -1
        )
        return flux - roll(flux, 1)

    first = divergence(
        jnp.where(place >= 4, own, left),
        jnp.where(places(flows_own.shape) >= 4, flows_own, flows_left),
    )
    last = divergence(jnp.where(place < 4, own, right), flows_own)
    return jnp.where(place < 4, last, first)


def edge_pass(place, edges, edges_swapped, flow_edges, flow_swapped, fixes):
    layers = fixes.shape[0]
    odd = place[3] == 1
    for l in range(layers):
        flow = flow_edges[layers, l : l + 1, :]
        tile = [ref[l // 2] for ref in edges_swapped]
        other = jnp.where(
            odd, *[ref[layers // 2, l // 2 : l // 2 + 1, :] for ref in flow_swapped]
        )
        fixes[l] = edge_divergence(
            edges[l],
            widen(jnp.where(odd, tile[0], tile[1]), l),
            widen(jnp.where(odd, tile[1], tile[0]), l),
            flow,
            widen(other, l),
        )


def at_edges(shape):
    lane = lanes(shape)
    return (lane < 2) | (lane >= 126)


def emit_swaps(place, state, swap_a, swap_b):
    layers, rows = state.shape[0], state.shape[1]
    low = place[2] * (rows - 2)
    swap_b[:layers] = state[:, pl.ds(low, 2)]
    swap_a[:layers] = state[:, pl.ds(rows - 2 - low, 2)]


def emit_sent(edges, sent, with_flows):
    layers = edges.shape[0] - (1 if with_flows else 0)
    for t in range(layers // 2):
        sent[t] = narrow(edges, 2 * t, 2 * t + 1)
        if with_flows:
            even = edges[layers, 2 * t : 2 * t + 1, :]
            odd = edges[layers, 2 * t + 1 : 2 * t + 2, :]
            place = places(even.shape)
            sent[layers // 2, t : t + 1, :] = jnp.where(
                (place >= 2) & (place < 6), even, roll(odd, 4)
            )


def start_kernel(
    place, conc, flow_x, flow_y, wet_x, wet_y, state, swap_a, swap_b, edges, sent, qx, qy
):
    layers, rows = flow_x.shape[0], flow_x.shape[1]
    subs = conc.shape[0] // (layers * rows)
    row = lax.broadcasted_iota(jnp.int32, flow_x.shape, 1)
    col = lax.broadcasted_iota(jnp.int32, flow_x.shape, 2)
    keep_x = jnp.where((row == rows - 1) & (place[0] == 1), 0.0, 1.0)
    keep_y = jnp.where((col == 127) & (place[1] == 1), 0.0, 1.0)
    qx[...] = flow_x[...] * wet_x[...].astype(F32) * keep_x
    qy[...] = flow_y[...] * wet_y[...].astype(F32) * keep_y
    for swap in (swap_a, swap_b):
        swap[layers] = jnp.zeros_like(swap[layers])
    edges[layers] = jnp.zeros_like(edges[layers])
    sent[layers // 2] = jnp.zeros_like(sent[layers // 2])

    def layer(l, carry):
        values = []
        for i in range(rows):
            c = conc[pl.ds(l * rows + i, subs, stride=layers * rows), :]
            values.append(c)
            state[l, i] = c
        edges[l] = pack_layer(values)
        edges[layers, pl.ds(l, 1), :] = pack_layer([qy[l, i : i + 1, :] for i in range(rows)])
        for swap in (swap_a, swap_b):
            swap[layers, 0, pl.ds(l, 1), :] = qx[l, rows - 1 :, :]
        return carry

    lax.fori_loop(0, layers, layer, 0)
    emit_swaps(place, state, swap_a, swap_b)
    emit_sent(edges, sent, True)


def start(place, conc, flow_x, flow_y, wet_x, wet_y):
    subs, layers, rows, cols = conc.shape
    flows = jax.ShapeDtypeStruct(flow_x.shape, F32)
    return pl.pallas_call(
        start_kernel,
        in_specs=[SMEM] + [VMEM] * 5,
        out_specs=[VMEM] * 7,
        out_shape=[
            jax.ShapeDtypeStruct((layers, rows, subs, cols), F32),
            jax.ShapeDtypeStruct((layers + 1, 2, subs, cols), F32),
            jax.ShapeDtypeStruct((layers + 1, 2, subs, cols), F32),
            jax.ShapeDtypeStruct((layers + 1, subs, cols), F32),
            jax.ShapeDtypeStruct((layers // 2 + 1, subs, cols), F32),
            flows,
            flows,
        ],
        compiler_params=pltpu.CompilerParams(vmem_limit_bytes=VMEM_BYTES),
        cost_estimate=pl.CostEstimate(flops=10**6, bytes_accessed=8 * 10**6, transcendentals=0),
        name="start_state",
    )(place, conc.reshape(subs * layers * rows, cols), flow_x, flow_y, wet_x, wet_y)


def y_divergence(c, flows):
    before = [roll(v, 1) for v in c]
    after = [roll(v, -1) for v in c]
    slope = [0.5 * half_minmod(v - b, a - v) for v, b, a in zip(c, before, after)]
    right = [roll(v - s, -1) for v, s in zip(c, slope)]
    flux = [
        jnp.maximum(q, 0.0) * (v + s) + jnp.minimum(q, 0.0) * r
        for q, v, s, r in zip(flows, c, slope, right)
    ]
    return [f - roll(f, 1) for f in flux]


def x_faces(get, flow, first, last):
    here = get(first)
    step = 0.5 * (here - get(first - 1))
    fluxes = []
    left = None
    for i in range(first, last + 2):
        after = get(i + 1)
        step_after = 0.5 * (after - here)
        slope = half_minmod(step, step_after)
        if i > first:
            q = flow(i - 1)
            fluxes.append(
                jnp.maximum(q, 0.0) * left + jnp.minimum(q, 0.0) * (here - slope)
            )
        left = here + slope
        here, step = (after, step_after)
    return fluxes


def x_rows(state, place, swapped, l, rows):
    def get(i):
        if 0 <= i < rows:
            return state[l, i]
        j = i + 2 if i < 0 else i - rows
        pair = [ref[l, j] for ref in (swapped if i < 0 else swapped[::-1])]
        return jnp.where(place[2] == 1, *pair)

    return get


def x_flows(qx, qx_west, l):
    return lambda i: qx_west if i < 0 else qx[l, i : i + 1, :]


def west_flow(place, flow_swapped, layers, l):
    return jnp.where(place[2] == 1, *[ref[layers, 0, pl.ds(l, 1), :] for ref in flow_swapped])


def first_divergence_kernel(state, qx, qy, div):
    layers, rows = qx.shape[0], qx.shape[1]
    edge = at_edges(state.shape[2:])

    def layer(l, carry):
        c = [state[l, i] for i in range(rows)]
        parts = y_divergence(c, [qy[l, i : i + 1, :] for i in range(rows)])
        faces = x_faces(x_rows(state, None, None, l, rows), x_flows(qx, None, l), 1, rows - 3)
        for i in range(rows):
            value = jnp.where(edge, 0.0, parts[i])
            if 2 <= i < rows - 2:
                value = value + (faces[i - 1] - faces[i - 2])
            div[l, i] = value
        return carry

    lax.fori_loop(0, layers, layer, 0)


def first_divergence(state, qx, qy):
    return pl.pallas_call(
        first_divergence_kernel,
        in_specs=[VMEM] * 3,
        out_specs=VMEM,
        out_shape=jax.ShapeDtypeStruct(state.shape, F32),
        compiler_params=pltpu.CompilerParams(vmem_limit_bytes=VMEM_BYTES),
        cost_estimate=pl.CostEstimate(flops=2 * 10**7, bytes_accessed=10**7, transcendentals=0),
        name="first_divergence",
    )(state, qx, qy)


def explicit_value(c, div, rates, rates_before, inflow, renewal, scale):
    carried = pltpu.roll(c, 1, 0)
    return (
        c
        + ((renewal * (inflow - c) - scale * div) + (rates_before * carried - rates * c))
    )


def solve(star, coef, emit):
    layers, rows = star.shape[0], star.shape[1]
    batch = 4

    def some(b, carry):
        ids = [b * batch + j for j in range(batch)]

        def get(which, l, i):
            return coef[which, l, pl.ds(i, 1), :]

        value = [star[0, i] for i in ids]
        for l in range(1, layers):
            value = [star[l, i] - get(0, l, i) * v for i, v in zip(ids, value)]
            for i, v in zip(ids, value):
                star[l, i] = v
        value = [v * get(1, layers - 1, i) for i, v in zip(ids, value)]
        for i, v in zip(ids, value):
            emit(layers - 1, i, v)
        for l in range(layers - 2, -1, -1):
            value = [
                (star[l, i] + get(2, l, i) * v) * get(1, l, i) for i, v in zip(ids, value)
            ]
            for i, v in zip(ids, value):
                emit(l, i, v)
        return carry

    lax.fori_loop(0, rows // batch, some, 0)


def emit_edges(place, state, swap_a, swap_b, edges, sent):
    layers, rows = state.shape[0], state.shape[1]
    emit_swaps(place, state, swap_a, swap_b)

    def layer(l, carry):
        edges[l] = pack_layer([state[l, i] for i in range(rows)])
        return carry

    lax.fori_loop(0, layers, layer, 0)
    emit_sent(edges, sent, False)


def spread_slots(slots, chunk, terms, spread, hot):
    rows = 21
    halves = spread.shape[1] // 128
    sub8 = lax.broadcasted_iota(jnp.int32, (8, 128), 0)
    column = lax.broadcasted_iota(jnp.int32, (128, 128), 0).astype(F32).astype(BF16)
    base = pl.multiple_of(chunk * (halves * rows), 8)
    values = slots[pl.ds(base, halves * rows), :]
    high = values.astype(BF16).astype(F32)
    terms[0] = high
    terms[1] = values - high
    for j in range(halves):
        to = slice(j * 128, (j + 1) * 128)

        def term(which, ch):
            at = j * rows + ch
            return terms[which, at : at + 1, :]

        label = (term(0, 20) + term(1, 20)).astype(jnp.int32)
        mask = jnp.where(jnp.broadcast_to((label >> 7) & 7, (8, 128)) == sub8, 1.0, 0.0)
        mask = jnp.concatenate([mask, mask], axis=0).astype(BF16)
        for ch in range(20):
            both = [jnp.broadcast_to(term(which, ch), (8, 128)) for which in range(2)]
            both = jnp.concatenate(both, axis=0).astype(BF16)
            spread[ch * 16 : (ch + 1) * 16, to] = both * mask
        place = jnp.broadcast_to((label & 127).astype(F32), (16, 128)).astype(BF16)
        half = label >> 10
        hits = [
            jnp.broadcast_to(jnp.where(half == h, 1.0, 0.0), (16, 128)).astype(BF16)
            for h in range(2)
        ]
        zero = jnp.zeros((16, 128), BF16)
        for g in range(8):
            same = column[g * 16 : (g + 1) * 16] == place
            for h in range(2):
                at = h * 128 + g * 16
                hot[at : at + 16, to] = jnp.where(same, hits[h], zero)


def aggregate(slots, terms, spread, hot, total):
    total[...] = jnp.zeros_like(total)

    def chunk(i, carry):
        spread_slots(slots, i, terms, spread, hot)
        total[...] += lax.dot_general(
            spread[...], hot[...], (((1,), (1,)), ((), ())), preferred_element_type=F32
        )
        return carry

    lax.fori_loop(0, slots.shape[0] // terms.shape[1], chunk, 0)


def totals_kernel(slots, total, terms, spread, hot):
    aggregate(slots, terms, spread, hot, total)


def totals(slots):
    depth = min(2048, slots.shape[0] // 21 * 128)
    return pl.pallas_call(
        totals_kernel,
        in_specs=[VMEM],
        out_specs=VMEM,
        out_shape=jax.ShapeDtypeStruct((320, 256), F32),
        scratch_shapes=[
            pltpu.VMEM((2, depth // 128 * 21, 128), F32),
            pltpu.VMEM((320, depth), BF16),
            pltpu.VMEM((256, depth), BF16),
        ],
        compiler_params=pltpu.CompilerParams(vmem_limit_bytes=VMEM_BYTES),
        cost_estimate=pl.CostEstimate(
            flops=12 * 10**9, bytes_accessed=4 * 10**6, transcendentals=0
        ),
        name="aggregate",
    )(slots)


def factorize(total, base_volume, diffusivity, coef):
    layers = base_volume.shape[0]
    uppers, downs = ([], [])
    for l in range(layers):
        parts = []
        for ch in (l, layers + l):
            parts.append(
                jnp.concatenate(
                    [
                        total[ch * 16 : ch * 16 + 8, h * 128 : (h + 1) * 128]
                        + total[ch * 16 + 8 : ch * 16 + 16, h * 128 : (h + 1) * 128]
                        for h in range(2)
                    ],
                    axis=0,
                )
            )
        scale = STEP / (base_volume[l] + parts[0])
        coef[3, l] = scale
        coef[4, l] = scale * parts[1]
        uppers.append(scale * diffusivity[l] if l < layers - 1 else jnp.zeros_like(scale))
        downs.append(scale * diffusivity[l - 1] if l > 0 else jnp.zeros_like(scale))
    pivot = 1.0 + uppers[0]
    coef[0, 0] = jnp.zeros_like(pivot)
    for l in range(layers):
        inverse = 1.0 / pivot
        coef[1, l] = inverse
        coef[2, l] = uppers[l]
        if l + 1 < layers:
            factor = -downs[l + 1] * inverse
            coef[0, l + 1] = factor
            pivot = 1.0 + uppers[l + 1] + downs[l + 1] + factor * uppers[l]


def first_step_kernel(
    place,
    total,
    base_volume,
    diffusivity,
    state,
    div,
    received_a,
    received_b,
    edges_before,
    edges_a,
    edges_b,
    qx,
    rates,
    rates_before,
    inflow,
    new,
    swap_a,
    swap_b,
    edges,
    sent,
    coef,
    fixes,
    star,
):
    layers, rows = base_volume.shape[0], base_volume.shape[1]
    factorize(total, base_volume, diffusivity, coef)
    received = (received_a, received_b)
    edges_swapped = (edges_a, edges_b)
    edge_pass(place, edges_before, edges_swapped, edges_before, edges_swapped, fixes)
    edge = at_edges(state.shape[2:])

    def explicit(l, carry):
        get = x_rows(state, place, received, l, rows)
        flow = x_flows(qx, west_flow(place, received, layers, l), l)
        low = x_faces(get, flow, -1, 1)
        high = x_faces(get, flow, rows - 3, rows - 1)
        fix = [roll(fixes[l], 124 - 8 * i) for i in range(rows)]
        for i in range(rows):
            value = div[l, i] + jnp.where(edge, fix[i], 0.0)
            if i < 2:
                value = value + (low[i + 1] - low[i])
            if i >= rows - 2:
                j = i - rows + 3
                value = value + (high[j] - high[j - 1])
            star[l, i] = explicit_value(
                state[l, i],
                value,
                rates[...],
                rates_before[...],
                inflow[...],
                coef[4, l, i : i + 1, :],
                coef[3, l, i : i + 1, :],
            )
        return carry

    lax.fori_loop(0, layers, explicit, 0)

    def emit(l, i, value):
        new[l, i] = value

    solve(star, coef, emit)
    emit_edges(place, new, swap_a, swap_b, edges, sent)


def state_shapes(shape):
    layers, rows, subs, cols = shape
    return [
        jax.ShapeDtypeStruct(shape, F32),
        jax.ShapeDtypeStruct((layers, 2, subs, cols), F32),
        jax.ShapeDtypeStruct((layers, 2, subs, cols), F32),
        jax.ShapeDtypeStruct((layers, subs, cols), F32),
        jax.ShapeDtypeStruct((layers // 2, subs, cols), F32),
    ]


def first_step(place, total, base_volume, diffusivity, state, *args):
    layers, rows, subs, cols = state.shape
    return pl.pallas_call(
        first_step_kernel,
        in_specs=[SMEM] + [VMEM] * 14,
        out_specs=[VMEM] * 6,
        out_shape=state_shapes(state.shape)
        + [jax.ShapeDtypeStruct((5, layers, rows, cols), F32)],
        scratch_shapes=[
            pltpu.VMEM((layers, subs, cols), F32),
            pltpu.VMEM(state.shape, F32),
        ],
        compiler_params=pltpu.CompilerParams(vmem_limit_bytes=VMEM_BYTES),
        cost_estimate=pl.CostEstimate(flops=2 * 10**7, bytes_accessed=10**7, transcendentals=0),
        name="first_step",
    )(place, total, base_volume, diffusivity, state, *args)


def later_step_kernel(
    final,
    place,
    state,
    received_a,
    received_b,
    edges_before,
    edges_a,
    edges_b,
    flow_a,
    flow_b,
    flow_edges,
    flow_edges_a,
    flow_edges_b,
    qx,
    qy,
    coef,
    rates,
    rates_before,
    inflow,
    *refs,
):
    layers, rows = qx.shape[0], qx.shape[1]
    if final:
        out, fixes, star = refs
        subs = out.shape[0] // (layers * rows)
    else:
        new, swap_a, swap_b, edges, sent, fixes, star = refs
    edge_pass(
        place, edges_before, (edges_a, edges_b), flow_edges, (flow_edges_a, flow_edges_b), fixes
    )
    edge = at_edges(state.shape[2:])

    def layer(l, carry):
        c = [state[l, i] for i in range(rows)]
        fix = [roll(fixes[l], 124 - 8 * i) for i in range(rows)]
        parts = y_divergence(c, [qy[l, i : i + 1, :] for i in range(rows)])
        parts = [jnp.where(edge, f, p) for f, p in zip(fix, parts)]
        flow = x_flows(qx, west_flow(place, (flow_a, flow_b), layers, l), l)
        get = x_rows(state, place, (received_a, received_b), l, rows)
        faces = x_faces(get, flow, -1, rows - 1)
        for i in range(rows):
            star[l, i] = explicit_value(
                state[l, i],
                parts[i] + (faces[i + 1] - faces[i]),
                rates[...],
                rates_before[...],
                inflow[...],
                coef[4, l, i : i + 1, :],
                coef[3, l, i : i + 1, :],
            )
        return carry

    lax.fori_loop(0, layers, layer, 0)

    def emit(l, i, value):
        if final:
            out[pl.ds(l * rows + i, subs, stride=layers * rows), :] = value
        else:
            new[l, i] = value

    solve(star, coef, emit)
    if not final:
        emit_edges(place, new, swap_a, swap_b, edges, sent)


def later_step(final, place, state, *args):
    layers, rows, subs, cols = state.shape
    if final:
        shapes = jax.ShapeDtypeStruct((subs * layers * rows, cols), F32)
        specs = VMEM
    else:
        shapes = state_shapes(state.shape)
        specs = [VMEM] * 5
    return pl.pallas_call(
        functools.partial(later_step_kernel, final),
        in_specs=[SMEM] + [VMEM] * 17,
        out_specs=specs,
        out_shape=shapes,
        scratch_shapes=[pltpu.VMEM((layers, subs, cols), F32), pltpu.VMEM(state.shape, F32)],
        compiler_params=pltpu.CompilerParams(vmem_limit_bytes=VMEM_BYTES),
        cost_estimate=pl.CostEstimate(flops=3 * 10**7, bytes_accessed=10**7, transcendentals=0),
        name="last_step" if final else "middle_step",
    )(place, state, *args)


def swap(values, axis, first):
    pairs = [(i, i + 1) for i in range(first, lax.axis_size(axis) - 1, 2)]
    return lax.ppermute(values, axis, pairs + [(j, i) for i, j in pairs])


def exchange(swap_a, swap_b, sent):
    rows = (swap(swap_a, "gx", 0), swap(swap_b, "gx", 1))
    columns = (swap(sent, "gy", 0), swap(sent, "gy", 1))
    return (rows, columns)


def local(
    concentration,
    base_volume,
    flow_x,
    flow_y,
    face_wet_x,
    face_wet_y,
    diffusivity,
    decay_rates,
    inflow,
    fine_volume,
    fine_discharge,
    cell_wet,
    seg_local,
):
    subs, layers, rows, cols = concentration.shape
    size_x, size_y = (lax.axis_size("gx"), lax.axis_size("gy"))
    owners = size_x * size_y
    slots = pack_slots(fine_volume, fine_discharge, cell_wet, seg_local)
    arrived = lax.all_to_all(
        slots.reshape(owners, 1, -1), ("gx", "gy"), split_axis=0, concat_axis=0, tiled=True
    ).reshape(slots.shape)

    at_x, at_y = (lax.axis_index("gx"), lax.axis_index("gy"))
    place = jnp.stack(
        [
            (at_x == size_x - 1).astype(jnp.int32),
            (at_y == size_y - 1).astype(jnp.int32),
            at_x.astype(jnp.int32) % 2,
            at_y.astype(jnp.int32) % 2,
        ]
    )
    rates = jnp.concatenate([jnp.zeros((1,), F32), decay_rates]) * STEP
    rates_before = jnp.concatenate([jnp.zeros((1,), F32), rates[:-1]])
    rates, rates_before, inflow = (
        jnp.broadcast_to(v[:, None], (subs, cols)) for v in (rates, rates_before, inflow)
    )
    state, swap_a, swap_b, edges, sent, qx, qy = start(
        place, concentration, flow_x, flow_y, face_wet_x, face_wet_y
    )
    rows_in, columns_in = exchange(swap_a, swap_b, sent)
    flows = (*rows_in, edges, *columns_in, qx, qy)
    div = first_divergence(state, qx, qy)
    constants = (rates, rates_before, inflow)
    state, swap_a, swap_b, edges, sent, coef = first_step(
        place,
        totals(arrived),
        base_volume,
        diffusivity,
        state,
        div,
        *rows_in,
        edges,
        *columns_in,
        qx,
        *constants,
    )
    for step in range(1, SUBSTEPS):
        final = step == SUBSTEPS - 1
        rows_in, columns_in = exchange(swap_a, swap_b, sent)
        result = later_step(
            final, place, state, *rows_in, edges, *columns_in, *flows, coef, *constants
        )
        if not final:
            state, swap_a, swap_b, edges, sent = result
    return result.reshape(concentration.shape)


def solution(mesh):
    fine = P(None, ("gx", "gy"))
    block = P(None, "gx", "gy")
    return jax.shard_map(
        local,
        mesh=mesh,
        in_specs=(
            P(None, None, "gx", "gy"),
            block,
            block,
            block,
            block,
            block,
            block,
            P(),
            P(),
            fine,
            fine,
            P(("gx", "gy")),
            P(("gx", "gy")),
        ),
        out_specs=P(None, None, "gx", "gy"),
        check_vma=False,
    )
```

```python
import functools

import jax
import jax.numpy as jnp
from jax import lax
from jax.experimental import pallas as pl
from jax.experimental.pallas import tpu as pltpu
from jax.sharding import PartitionSpec as P

SUBSTEPS = 3
STEP = 1.0 / SUBSTEPS
VMEM_BYTES = 24 * 1024 * 1024
PACK_VMEM_BYTES = 62 * 1024 * 1024
F32 = jnp.float32
BF16 = jnp.bfloat16

VMEM = pl.BlockSpec(memory_space=pltpu.VMEM)
SMEM = pl.BlockSpec(memory_space=pltpu.SMEM)


def half_minmod(left, right):
    return jnp.minimum(
        jnp.maximum(left, jnp.minimum(right, 0.0)), jnp.maximum(right, 0.0)
    )


def roll(values, shift):
    return pltpu.roll(values, shift % values.shape[-1], values.ndim - 1)


def lanes(shape):
    return lax.broadcasted_iota(jnp.int32, shape, len(shape) - 1)


def pack_kernel(volume, discharge, wet, segment, out):
    layers = volume.shape[0]
    rows = 2 * layers + 1
    groups = wet.shape[0]
    missing = 16 * 128
    label = jnp.where(wet[...] == 1, segment[...], missing).astype(F32)
    for k in range(groups):
        out[k * rows : k * rows + layers, :] = volume[:, k * 128 : (k + 1) * 128]
        out[k * rows + layers : k * rows + 2 * layers, :] = discharge[:, k * 128 : (k + 1) * 128]
        out[k * rows + 2 * layers : (k + 1) * rows, :] = label[k : k + 1, :]


def pack_slots(volume, discharge, wet, segment):
    layers, fine = volume.shape
    groups = fine // 128
    rows = 2 * layers + 1
    step = 128 if groups % 128 == 0 else groups
    return pl.pallas_call(
        pack_kernel,
        grid=(groups // step,),
        in_specs=[
            pl.BlockSpec((layers, step * 128), lambda i: (0, i)),
            pl.BlockSpec((layers, step * 128), lambda i: (0, i)),
            pl.BlockSpec((step, 128), lambda i: (i, 0)),
            pl.BlockSpec((step, 128), lambda i: (i, 0)),
        ],
        out_specs=pl.BlockSpec((step * rows, 128), lambda i: (i, 0)),
        out_shape=jax.ShapeDtypeStruct((groups * rows, 128), F32),
        compiler_params=pltpu.CompilerParams(vmem_limit_bytes=PACK_VMEM_BYTES),
        cost_estimate=pl.CostEstimate(flops=0, bytes_accessed=8 * 10**6, transcendentals=0),
        name="pack_slots",
    )(volume, discharge, wet.reshape(groups, 128), segment.reshape(groups, 128))


def places(shape):
    return lanes(shape) % 8


def pack_layer(rows_of_layer):
    packed = None
    for i, values in enumerate(rows_of_layer):
        moved = roll(values, 8 * i + 4)
        packed = moved if i == 0 else jnp.where(lanes(moved.shape) // 8 == i, moved, packed)
    return packed


def narrow(edges, low, high):
    even, odd = (edges[low], edges[high])
    place = places(even.shape)
    return jnp.where((place >= 2) & (place < 6), even, roll(odd, 4))


def widen(tile, layer):
    return tile if layer % 2 == 0 else roll(tile, -4)


def edge_divergence(own, left, right, flows_own, flows_left):
    place = places(own.shape)

    def divergence(four, flows):
        step = 0.5 * (roll(four, -1) - four)
        slope = half_minmod(roll(step, 1), step)
        flux = jnp.maximum(flows, 0.0) * (four + slope) + jnp.minimum(flows, 0.0) * roll(
            four - slope, -1
        )
        return flux - roll(flux, 1)

    first = divergence(
        jnp.where(place >= 4, own, left),
        jnp.where(places(flows_own.shape) >= 4, flows_own, flows_left),
    )
    last = divergence(jnp.where(place < 4, own, right), flows_own)
    return jnp.where(place < 4, last, first)


def edge_pass(place, edges, edges_swapped, flow_edges, flow_swapped, fixes):
    layers = fixes.shape[0]
    odd = place[3] == 1
    for l in range(layers):
        flow = flow_edges[layers, l : l + 1, :]
        tile = [ref[l // 2] for ref in edges_swapped]
        other = jnp.where(
            odd, *[ref[layers // 2, l // 2 : l // 2 + 1, :] for ref in flow_swapped]
        )
        fixes[l] = edge_divergence(
            edges[l],
            widen(jnp.where(odd, tile[0], tile[1]), l),
            widen(jnp.where(odd, tile[1], tile[0]), l),
            flow,
            widen(other, l),
        )


def at_edges(shape):
    lane = lanes(shape)
    return (lane < 2) | (lane >= 126)


def emit_swaps(place, state, swap_a, swap_b):
    layers, rows = state.shape[0], state.shape[1]
    low = place[2] * (rows - 2)
    swap_b[:layers] = state[:, pl.ds(low, 2)]
    swap_a[:layers] = state[:, pl.ds(rows - 2 - low, 2)]


def emit_sent(edges, sent, with_flows):
    layers = edges.shape[0] - (1 if with_flows else 0)
    for t in range(layers // 2):
        sent[t] = narrow(edges, 2 * t, 2 * t + 1)
        if with_flows:
            even = edges[layers, 2 * t : 2 * t + 1, :]
            odd = edges[layers, 2 * t + 1 : 2 * t + 2, :]
            place = places(even.shape)
            sent[layers // 2, t : t + 1, :] = jnp.where(
                (place >= 2) & (place < 6), even, roll(odd, 4)
            )


def start_kernel(
    place, conc, flow_x, flow_y, wet_x, wet_y, state, swap_a, swap_b, edges, sent, qx, qy
):
    layers, rows = flow_x.shape[0], flow_x.shape[1]
    subs = conc.shape[0] // (layers * rows)
    row = lax.broadcasted_iota(jnp.int32, flow_x.shape, 1)
    col = lax.broadcasted_iota(jnp.int32, flow_x.shape, 2)
    keep_x = jnp.where((row == rows - 1) & (place[0] == 1), 0.0, 1.0)
    keep_y = jnp.where((col == 127) & (place[1] == 1), 0.0, 1.0)
    qx[...] = flow_x[...] * wet_x[...].astype(F32) * keep_x
    qy[...] = flow_y[...] * wet_y[...].astype(F32) * keep_y
    for swap in (swap_a, swap_b):
        swap[layers] = jnp.zeros_like(swap[layers])
    edges[layers] = jnp.zeros_like(edges[layers])
    sent[layers // 2] = jnp.zeros_like(sent[layers // 2])

    def layer(l, carry):
        values = []
        for i in range(rows):
            c = conc[pl.ds(l * rows + i, subs, stride=layers * rows), :]
            values.append(c)
            state[l, i] = c
        edges[l] = pack_layer(values)
        edges[layers, pl.ds(l, 1), :] = pack_layer([qy[l, i : i + 1, :] for i in range(rows)])
        for swap in (swap_a, swap_b):
            swap[layers, 0, pl.ds(l, 1), :] = qx[l, rows - 1 :, :]
        return carry

    lax.fori_loop(0, layers, layer, 0)
    emit_swaps(place, state, swap_a, swap_b)
    emit_sent(edges, sent, True)


def start(place, conc, flow_x, flow_y, wet_x, wet_y):
    subs, layers, rows, cols = conc.shape
    flows = jax.ShapeDtypeStruct(flow_x.shape, F32)
    return pl.pallas_call(
        start_kernel,
        in_specs=[SMEM] + [VMEM] * 5,
        out_specs=[VMEM] * 7,
        out_shape=[
            jax.ShapeDtypeStruct((layers, rows, subs, cols), F32),
            jax.ShapeDtypeStruct((layers + 1, 2, subs, cols), F32),
            jax.ShapeDtypeStruct((layers + 1, 2, subs, cols), F32),
            jax.ShapeDtypeStruct((layers + 1, subs, cols), F32),
            jax.ShapeDtypeStruct((layers // 2 + 1, subs, cols), F32),
            flows,
            flows,
        ],
        compiler_params=pltpu.CompilerParams(vmem_limit_bytes=VMEM_BYTES),
        cost_estimate=pl.CostEstimate(flops=10**6, bytes_accessed=8 * 10**6, transcendentals=0),
        name="start_state",
    )(place, conc.reshape(subs * layers * rows, cols), flow_x, flow_y, wet_x, wet_y)


def y_divergence(c, flows):
    before = [roll(v, 1) for v in c]
    after = [roll(v, -1) for v in c]
    slope = [0.5 * half_minmod(v - b, a - v) for v, b, a in zip(c, before, after)]
    right = [roll(v - s, -1) for v, s in zip(c, slope)]
    flux = [
        jnp.maximum(q, 0.0) * (v + s) + jnp.minimum(q, 0.0) * r
        for q, v, s, r in zip(flows, c, slope, right)
    ]
    return [f - roll(f, 1) for f in flux]


def x_faces(get, flow, first, last):
    here = get(first)
    step = 0.5 * (here - get(first - 1))
    fluxes = []
    left = None
    for i in range(first, last + 2):
        after = get(i + 1)
        step_after = 0.5 * (after - here)
        slope = half_minmod(step, step_after)
        if i > first:
            q = flow(i - 1)
            fluxes.append(
                jnp.maximum(q, 0.0) * left + jnp.minimum(q, 0.0) * (here - slope)
            )
        left = here + slope
        here, step = (after, step_after)
    return fluxes


def x_rows(state, place, swapped, l, rows):
    def get(i):
        if 0 <= i < rows:
            return state[l, i]
        j = i + 2 if i < 0 else i - rows
        pair = [ref[l, j] for ref in (swapped if i < 0 else swapped[::-1])]
        return jnp.where(place[2] == 1, *pair)

    return get


def x_flows(qx, qx_west, l):
    return lambda i: qx_west if i < 0 else qx[l, i : i + 1, :]


def west_flow(place, flow_swapped, layers, l):
    return jnp.where(place[2] == 1, *[ref[layers, 0, pl.ds(l, 1), :] for ref in flow_swapped])


def first_divergence_kernel(state, qx, qy, div):
    layers, rows = qx.shape[0], qx.shape[1]
    edge = at_edges(state.shape[2:])

    def layer(l, carry):
        c = [state[l, i] for i in range(rows)]
        parts = y_divergence(c, [qy[l, i : i + 1, :] for i in range(rows)])
        faces = x_faces(x_rows(state, None, None, l, rows), x_flows(qx, None, l), 1, rows - 3)
        for i in range(rows):
            value = jnp.where(edge, 0.0, parts[i])
            if 2 <= i < rows - 2:
                value = value + (faces[i - 1] - faces[i - 2])
            div[l, i] = value
        return carry

    lax.fori_loop(0, layers, layer, 0)


def first_divergence(state, qx, qy):
    return pl.pallas_call(
        first_divergence_kernel,
        in_specs=[VMEM] * 3,
        out_specs=VMEM,
        out_shape=jax.ShapeDtypeStruct(state.shape, F32),
        compiler_params=pltpu.CompilerParams(vmem_limit_bytes=VMEM_BYTES),
        cost_estimate=pl.CostEstimate(flops=2 * 10**7, bytes_accessed=10**7, transcendentals=0),
        name="first_divergence",
    )(state, qx, qy)


def explicit_value(c, div, rates, rates_before, inflow, renewal, scale):
    carried = pltpu.roll(c, 1, 0)
    return (
        c
        + ((renewal * (inflow - c) - scale * div) + (rates_before * carried - rates * c))
    )


def solve(star, coef, emit):
    layers, rows = star.shape[0], star.shape[1]
    batch = 4

    def some(b, carry):
        ids = [b * batch + j for j in range(batch)]

        def get(which, l, i):
            return coef[which, l, pl.ds(i, 1), :]

        value = [star[0, i] for i in ids]
        for l in range(1, layers):
            value = [star[l, i] - get(0, l, i) * v for i, v in zip(ids, value)]
            for i, v in zip(ids, value):
                star[l, i] = v
        value = [v * get(1, layers - 1, i) for i, v in zip(ids, value)]
        for i, v in zip(ids, value):
            emit(layers - 1, i, v)
        for l in range(layers - 2, -1, -1):
            value = [
                (star[l, i] + get(2, l, i) * v) * get(1, l, i) for i, v in zip(ids, value)
            ]
            for i, v in zip(ids, value):
                emit(l, i, v)
        return carry

    lax.fori_loop(0, rows // batch, some, 0)


def emit_edges(place, state, swap_a, swap_b, edges, sent):
    layers, rows = state.shape[0], state.shape[1]
    emit_swaps(place, state, swap_a, swap_b)

    def some(t, carry):
        for l in range(5):
            l = t * 5 + l
            edges[l] = pack_layer([state[l, i] for i in range(rows)])
        return carry

    lax.fori_loop(0, layers // 5, some, 0)
    emit_sent(edges, sent, False)


def spread_slots(slots, chunk, terms, spread, hot):
    rows = 21
    halves = spread.shape[1] // 128
    sub8 = lax.broadcasted_iota(jnp.int32, (8, 128), 0)
    column = lax.broadcasted_iota(jnp.int32, (128, 128), 0).astype(F32).astype(BF16)
    base = pl.multiple_of(chunk * (halves * rows), 8)
    values = slots[pl.ds(base, halves * rows), :]
    high = values.astype(BF16).astype(F32)
    terms[0] = high
    terms[1] = values - high
    for j in range(halves):
        to = slice(j * 128, (j + 1) * 128)

        def term(which, ch):
            at = j * rows + ch
            return terms[which, at : at + 1, :]

        label = (term(0, 20) + term(1, 20)).astype(jnp.int32)
        mask = jnp.where(jnp.broadcast_to((label >> 7) & 7, (8, 128)) == sub8, 1.0, 0.0)
        mask = jnp.concatenate([mask, mask], axis=0).astype(BF16)
        for ch in range(20):
            both = [jnp.broadcast_to(term(which, ch), (8, 128)) for which in range(2)]
            both = jnp.concatenate(both, axis=0).astype(BF16)
            spread[ch * 16 : (ch + 1) * 16, to] = both * mask
        place = jnp.broadcast_to((label & 127).astype(F32), (16, 128)).astype(BF16)
        half = label >> 10
        hits = [
            jnp.broadcast_to(jnp.where(half == h, 1.0, 0.0), (16, 128)).astype(BF16)
            for h in range(2)
        ]
        zero = jnp.zeros((16, 128), BF16)
        for g in range(8):
            same = column[g * 16 : (g + 1) * 16] == place
            for h in range(2):
                at = h * 128 + g * 16
                hot[at : at + 16, to] = jnp.where(same, hits[h], zero)


def aggregate(slots, terms, spread, hot, total):
    total[...] = jnp.zeros_like(total)

    def chunk(i, carry):
        spread_slots(slots, i, terms, spread, hot)
        total[...] += lax.dot_general(
            spread[...], hot[...], (((1,), (1,)), ((), ())), preferred_element_type=F32
        )
        return carry

    lax.fori_loop(0, slots.shape[0] // terms.shape[1], chunk, 0)


def totals_kernel(slots, total, terms, spread, hot):
    aggregate(slots, terms, spread, hot, total)


def totals(slots):
    depth = min(2048, slots.shape[0] // 21 * 128)
    return pl.pallas_call(
        totals_kernel,
        in_specs=[VMEM],
        out_specs=VMEM,
        out_shape=jax.ShapeDtypeStruct((320, 256), F32),
        scratch_shapes=[
            pltpu.VMEM((2, depth // 128 * 21, 128), F32),
            pltpu.VMEM((320, depth), BF16),
            pltpu.VMEM((256, depth), BF16),
        ],
        compiler_params=pltpu.CompilerParams(vmem_limit_bytes=VMEM_BYTES),
        cost_estimate=pl.CostEstimate(
            flops=12 * 10**9, bytes_accessed=4 * 10**6, transcendentals=0
        ),
        name="aggregate",
    )(slots)


def factorize(total, base_volume, diffusivity, coef):
    layers = base_volume.shape[0]
    uppers, downs = ([], [])
    for l in range(layers):
        parts = []
        for ch in (l, layers + l):
            parts.append(
                jnp.concatenate(
                    [
                        total[ch * 16 : ch * 16 + 8, h * 128 : (h + 1) * 128]
                        + total[ch * 16 + 8 : ch * 16 + 16, h * 128 : (h + 1) * 128]
                        for h in range(2)
                    ],
                    axis=0,
                )
            )
        scale = STEP / (base_volume[l] + parts[0])
        coef[3, l] = scale
        coef[4, l] = scale * parts[1]
        uppers.append(scale * diffusivity[l] if l < layers - 1 else jnp.zeros_like(scale))
        downs.append(scale * diffusivity[l - 1] if l > 0 else jnp.zeros_like(scale))
    pivot = 1.0 + uppers[0]
    coef[0, 0] = jnp.zeros_like(pivot)
    for l in range(layers):
        inverse = 1.0 / pivot
        coef[1, l] = inverse
        coef[2, l] = uppers[l]
        if l + 1 < layers:
            factor = -downs[l + 1] * inverse
            coef[0, l + 1] = factor
            pivot = 1.0 + uppers[l + 1] + downs[l + 1] + factor * uppers[l]


def first_step_kernel(
    place,
    total,
    base_volume,
    diffusivity,
    state,
    div,
    received_a,
    received_b,
    edges_before,
    edges_a,
    edges_b,
    qx,
    rates,
    rates_before,
    inflow,
    new,
    swap_a,
    swap_b,
    edges,
    sent,
    coef,
    fixes,
    star,
):
    layers, rows = base_volume.shape[0], base_volume.shape[1]
    factorize(total, base_volume, diffusivity, coef)
    received = (received_a, received_b)
    edges_swapped = (edges_a, edges_b)
    edge_pass(place, edges_before, edges_swapped, edges_before, edges_swapped, fixes)
    edge = at_edges(state.shape[2:])

    def explicit(l, carry):
        get = x_rows(state, place, received, l, rows)
        flow = x_flows(qx, west_flow(place, received, layers, l), l)
        low = x_faces(get, flow, -1, 1)
        high = x_faces(get, flow, rows - 3, rows - 1)
        fix = [roll(fixes[l], 124 - 8 * i) for i in range(rows)]
        for i in range(rows):
            value = div[l, i] + jnp.where(edge, fix[i], 0.0)
            if i < 2:
                value = value + (low[i + 1] - low[i])
            if i >= rows - 2:
                j = i - rows + 3
                value = value + (high[j] - high[j - 1])
            star[l, i] = explicit_value(
                state[l, i],
                value,
                rates[...],
                rates_before[...],
                inflow[...],
                coef[4, l, i : i + 1, :],
                coef[3, l, i : i + 1, :],
            )
        return carry

    lax.fori_loop(0, layers, explicit, 0)

    def emit(l, i, value):
        new[l, i] = value

    solve(star, coef, emit)
    emit_edges(place, new, swap_a, swap_b, edges, sent)


def state_shapes(shape):
    layers, rows, subs, cols = shape
    return [
        jax.ShapeDtypeStruct(shape, F32),
        jax.ShapeDtypeStruct((layers, 2, subs, cols), F32),
        jax.ShapeDtypeStruct((layers, 2, subs, cols), F32),
        jax.ShapeDtypeStruct((layers, subs, cols), F32),
        jax.ShapeDtypeStruct((layers // 2, subs, cols), F32),
    ]


def first_step(place, total, base_volume, diffusivity, state, *args):
    layers, rows, subs, cols = state.shape
    return pl.pallas_call(
        first_step_kernel,
        in_specs=[SMEM] + [VMEM] * 14,
        out_specs=[VMEM] * 6,
        out_shape=state_shapes(state.shape)
        + [jax.ShapeDtypeStruct((5, layers, rows, cols), F32)],
        scratch_shapes=[
            pltpu.VMEM((layers, subs, cols), F32),
            pltpu.VMEM(state.shape, F32),
        ],
        compiler_params=pltpu.CompilerParams(vmem_limit_bytes=VMEM_BYTES),
        cost_estimate=pl.CostEstimate(flops=2 * 10**7, bytes_accessed=10**7, transcendentals=0),
        name="first_step",
    )(place, total, base_volume, diffusivity, state, *args)


def later_step_kernel(
    final,
    place,
    state,
    received_a,
    received_b,
    edges_before,
    edges_a,
    edges_b,
    flow_a,
    flow_b,
    flow_edges,
    flow_edges_a,
    flow_edges_b,
    qx,
    qy,
    coef,
    rates,
    rates_before,
    inflow,
    *refs,
):
    layers, rows = qx.shape[0], qx.shape[1]
    if final:
        out, fixes, star = refs
        subs = out.shape[0] // (layers * rows)
    else:
        new, swap_a, swap_b, edges, sent, fixes, star = refs
    edge_pass(
        place, edges_before, (edges_a, edges_b), flow_edges, (flow_edges_a, flow_edges_b), fixes
    )
    edge = at_edges(state.shape[2:])

    def layer(l, carry):
        flow = x_flows(qx, west_flow(place, (flow_a, flow_b), layers, l), l)
        get = x_rows(state, place, (received_a, received_b), l, rows)
        rolled = [(roll(state[l, i], 1), roll(state[l, i], -1)) for i in range(rows)]
        faces = x_faces(get, flow, -1, rows - 1)
        x_part = [faces[i + 1] - faces[i] for i in range(rows)]
        shifted = []
        for i in range(rows):
            c, (before, after) = (state[l, i], rolled[i])
            slope = 0.5 * half_minmod(c - before, after - c)
            shifted.append((c + slope, roll(c - slope, -1)))
        base = [
            explicit_value(
                state[l, i],
                x_part[i],
                rates[...],
                rates_before[...],
                inflow[...],
                coef[4, l, i : i + 1, :],
                coef[3, l, i : i + 1, :],
            )
            for i in range(rows)
        ]
        fluxes = []
        for i in range(rows):
            q = qy[l, i : i + 1, :]
            flux = jnp.maximum(q, 0.0) * shifted[i][0] + jnp.minimum(q, 0.0) * shifted[i][1]
            fluxes.append((flux, roll(flux, 1), roll(fixes[l], 124 - 8 * i)))
        for i in range(rows):
            flux, before, fix = fluxes[i]
            y_part = jnp.where(edge, fix, flux - before)
            star[l, i] = base[i] - coef[3, l, i : i + 1, :] * y_part
        return carry

    lax.fori_loop(0, layers, layer, 0, unroll=5)

    def emit(l, i, value):
        if final:
            out[pl.ds(l * rows + i, subs, stride=layers * rows), :] = value
        else:
            new[l, i] = value

    solve(star, coef, emit)
    if not final:
        emit_edges(place, new, swap_a, swap_b, edges, sent)


def later_step(final, place, state, *args):
    layers, rows, subs, cols = state.shape
    if final:
        shapes = jax.ShapeDtypeStruct((subs * layers * rows, cols), F32)
        specs = VMEM
    else:
        shapes = state_shapes(state.shape)
        specs = [VMEM] * 5
    return pl.pallas_call(
        functools.partial(later_step_kernel, final),
        in_specs=[SMEM] + [VMEM] * 17,
        out_specs=specs,
        out_shape=shapes,
        scratch_shapes=[pltpu.VMEM((layers, subs, cols), F32), pltpu.VMEM(state.shape, F32)],
        compiler_params=pltpu.CompilerParams(vmem_limit_bytes=VMEM_BYTES),
        cost_estimate=pl.CostEstimate(flops=3 * 10**7, bytes_accessed=10**7, transcendentals=0),
        name="last_step" if final else "middle_step",
    )(place, state, *args)


def swap(values, axis, first):
    pairs = [(i, i + 1) for i in range(first, lax.axis_size(axis) - 1, 2)]
    return lax.ppermute(values, axis, pairs + [(j, i) for i, j in pairs])


def exchange(swap_a, swap_b, sent):
    rows = (swap(swap_a, "gx", 0), swap(swap_b, "gx", 1))
    columns = (swap(sent, "gy", 0), swap(sent, "gy", 1))
    return (rows, columns)


def local(
    concentration,
    base_volume,
    flow_x,
    flow_y,
    face_wet_x,
    face_wet_y,
    diffusivity,
    decay_rates,
    inflow,
    fine_volume,
    fine_discharge,
    cell_wet,
    seg_local,
):
    subs, layers, rows, cols = concentration.shape
    size_x, size_y = (lax.axis_size("gx"), lax.axis_size("gy"))
    owners = size_x * size_y
    slots = pack_slots(fine_volume, fine_discharge, cell_wet, seg_local)
    arrived = lax.all_to_all(
        slots.reshape(owners, 1, -1), ("gx", "gy"), split_axis=0, concat_axis=0, tiled=True
    ).reshape(slots.shape)

    at_x, at_y = (lax.axis_index("gx"), lax.axis_index("gy"))
    place = jnp.stack(
        [
            (at_x == size_x - 1).astype(jnp.int32),
            (at_y == size_y - 1).astype(jnp.int32),
            at_x.astype(jnp.int32) % 2,
            at_y.astype(jnp.int32) % 2,
        ]
    )
    rates = jnp.concatenate([jnp.zeros((1,), F32), decay_rates]) * STEP
    rates_before = jnp.concatenate([jnp.zeros((1,), F32), rates[:-1]])
    rates, rates_before, inflow = (
        jnp.broadcast_to(v[:, None], (subs, cols)) for v in (rates, rates_before, inflow)
    )
    state, swap_a, swap_b, edges, sent, qx, qy = start(
        place, concentration, flow_x, flow_y, face_wet_x, face_wet_y
    )
    rows_in, columns_in = exchange(swap_a, swap_b, sent)
    flows = (*rows_in, edges, *columns_in, qx, qy)
    div = first_divergence(state, qx, qy)
    constants = (rates, rates_before, inflow)
    state, swap_a, swap_b, edges, sent, coef = first_step(
        place,
        totals(arrived),
        base_volume,
        diffusivity,
        state,
        div,
        *rows_in,
        edges,
        *columns_in,
        qx,
        *constants,
    )
    for step in range(1, SUBSTEPS):
        final = step == SUBSTEPS - 1
        rows_in, columns_in = exchange(swap_a, swap_b, sent)
        result = later_step(
            final, place, state, *rows_in, edges, *columns_in, *flows, coef, *constants
        )
        if not final:
            state, swap_a, swap_b, edges, sent = result
    return result.reshape(concentration.shape)


def solution(mesh):
    fine = P(None, ("gx", "gy"))
    block = P(None, "gx", "gy")
    return jax.shard_map(
        local,
        mesh=mesh,
        in_specs=(
            P(None, None, "gx", "gy"),
            block,
            block,
            block,
            block,
            block,
            block,
            P(),
            P(),
            fine,
            fine,
            P(("gx", "gy")),
            P(("gx", "gy")),
        ),
        out_specs=P(None, None, "gx", "gy"),
        check_vma=False,
    )
```

```python
import functools

import jax
import jax.numpy as jnp
from jax import lax
from jax.experimental import pallas as pl
from jax.experimental.pallas import tpu as pltpu
from jax.sharding import PartitionSpec as P

SUBSTEPS = 3
STEP = 1.0 / SUBSTEPS
VMEM_BYTES = 24 * 1024 * 1024
PACK_VMEM_BYTES = 62 * 1024 * 1024
F32 = jnp.float32
BF16 = jnp.bfloat16

VMEM = pl.BlockSpec(memory_space=pltpu.VMEM)
SMEM = pl.BlockSpec(memory_space=pltpu.SMEM)


def half_minmod(left, right):
    return jnp.minimum(
        jnp.maximum(left, jnp.minimum(right, 0.0)), jnp.maximum(right, 0.0)
    )


def roll(values, shift):
    return pltpu.roll(values, shift % values.shape[-1], values.ndim - 1)


def lanes(shape):
    return lax.broadcasted_iota(jnp.int32, shape, len(shape) - 1)


def pack_kernel(volume, discharge, wet, segment, out):
    layers = volume.shape[0]
    rows = 2 * layers + 1
    groups = wet.shape[0]
    missing = 16 * 128
    label = jnp.where(wet[...] == 1, segment[...], missing).astype(F32)
    for k in range(groups):
        out[k * rows : k * rows + layers, :] = volume[:, k * 128 : (k + 1) * 128]
        out[k * rows + layers : k * rows + 2 * layers, :] = discharge[:, k * 128 : (k + 1) * 128]
        out[k * rows + 2 * layers : (k + 1) * rows, :] = label[k : k + 1, :]


def pack_slots(volume, discharge, wet, segment):
    layers, fine = volume.shape
    groups = fine // 128
    rows = 2 * layers + 1
    step = 128 if groups % 128 == 0 else groups
    return pl.pallas_call(
        pack_kernel,
        grid=(groups // step,),
        in_specs=[
            pl.BlockSpec((layers, step * 128), lambda i: (0, i)),
            pl.BlockSpec((layers, step * 128), lambda i: (0, i)),
            pl.BlockSpec((step, 128), lambda i: (i, 0)),
            pl.BlockSpec((step, 128), lambda i: (i, 0)),
        ],
        out_specs=pl.BlockSpec((step * rows, 128), lambda i: (i, 0)),
        out_shape=jax.ShapeDtypeStruct((groups * rows, 128), F32),
        compiler_params=pltpu.CompilerParams(vmem_limit_bytes=PACK_VMEM_BYTES),
        cost_estimate=pl.CostEstimate(flops=0, bytes_accessed=8 * 10**6, transcendentals=0),
        name="pack_slots",
    )(volume, discharge, wet.reshape(groups, 128), segment.reshape(groups, 128))


def places(shape):
    return lanes(shape) % 8


def pack_layer(rows_of_layer):
    packed = None
    for i, values in enumerate(rows_of_layer):
        moved = roll(values, 8 * i + 4)
        packed = moved if i == 0 else jnp.where(lanes(moved.shape) // 8 == i, moved, packed)
    return packed


def narrow(edges, low, high):
    even, odd = (edges[low], edges[high])
    place = places(even.shape)
    return jnp.where((place >= 2) & (place < 6), even, roll(odd, 4))


def widen(tile, layer):
    return tile if layer % 2 == 0 else roll(tile, -4)


def edge_divergence(own, left, right, flows_own, flows_left):
    place = places(own.shape)

    def divergence(four, flows):
        step = 0.5 * (roll(four, -1) - four)
        slope = half_minmod(roll(step, 1), step)
        flux = jnp.maximum(flows, 0.0) * (four + slope) + jnp.minimum(flows, 0.0) * roll(
            four - slope, -1
        )
        return flux - roll(flux, 1)

    first = divergence(
        jnp.where(place >= 4, own, left),
        jnp.where(places(flows_own.shape) >= 4, flows_own, flows_left),
    )
    last = divergence(jnp.where(place < 4, own, right), flows_own)
    return jnp.where(place < 4, last, first)


def edge_pass(place, edges, edges_swapped, flow_edges, flow_swapped, fixes):
    layers = fixes.shape[0]
    odd = place[3] == 1
    for l in range(layers):
        flow = flow_edges[layers, l : l + 1, :]
        tile = [ref[l // 2] for ref in edges_swapped]
        other = jnp.where(
            odd, *[ref[layers // 2, l // 2 : l // 2 + 1, :] for ref in flow_swapped]
        )
        fixes[l] = edge_divergence(
            edges[l],
            widen(jnp.where(odd, tile[0], tile[1]), l),
            widen(jnp.where(odd, tile[1], tile[0]), l),
            flow,
            widen(other, l),
        )


def at_edges(shape):
    lane = lanes(shape)
    return (lane < 2) | (lane >= 126)


def emit_swaps(place, state, swap_a, swap_b):
    layers, rows = state.shape[0], state.shape[1]
    low = place[2] * (rows - 2)
    swap_b[:layers] = state[:, pl.ds(low, 2)]
    swap_a[:layers] = state[:, pl.ds(rows - 2 - low, 2)]


def emit_sent(edges, sent, with_flows):
    layers = edges.shape[0] - (1 if with_flows else 0)
    for t in range(layers // 2):
        sent[t] = narrow(edges, 2 * t, 2 * t + 1)
        if with_flows:
            even = edges[layers, 2 * t : 2 * t + 1, :]
            odd = edges[layers, 2 * t + 1 : 2 * t + 2, :]
            place = places(even.shape)
            sent[layers // 2, t : t + 1, :] = jnp.where(
                (place >= 2) & (place < 6), even, roll(odd, 4)
            )


def start_kernel(
    place, conc, flow_x, flow_y, wet_x, wet_y, state, swap_a, swap_b, edges, sent, qx, qy
):
    layers, rows = flow_x.shape[0], flow_x.shape[1]
    subs = conc.shape[0] // (layers * rows)
    row = lax.broadcasted_iota(jnp.int32, flow_x.shape, 1)
    col = lax.broadcasted_iota(jnp.int32, flow_x.shape, 2)
    keep_x = jnp.where((row == rows - 1) & (place[0] == 1), 0.0, 1.0)
    keep_y = jnp.where((col == 127) & (place[1] == 1), 0.0, 1.0)
    qx[...] = flow_x[...] * wet_x[...].astype(F32) * keep_x
    qy[...] = flow_y[...] * wet_y[...].astype(F32) * keep_y
    for swap in (swap_a, swap_b):
        swap[layers] = jnp.zeros_like(swap[layers])
    edges[layers] = jnp.zeros_like(edges[layers])
    sent[layers // 2] = jnp.zeros_like(sent[layers // 2])

    def layer(l, carry):
        values = []
        for i in range(rows):
            c = conc[pl.ds(l * rows + i, subs, stride=layers * rows), :]
            values.append(c)
            state[l, i] = c
        edges[l] = pack_layer(values)
        edges[layers, pl.ds(l, 1), :] = pack_layer([qy[l, i : i + 1, :] for i in range(rows)])
        for swap in (swap_a, swap_b):
            swap[layers, 0, pl.ds(l, 1), :] = qx[l, rows - 1 :, :]
        return carry

    lax.fori_loop(0, layers, layer, 0)
    emit_swaps(place, state, swap_a, swap_b)
    emit_sent(edges, sent, True)


def start(place, conc, flow_x, flow_y, wet_x, wet_y):
    subs, layers, rows, cols = conc.shape
    flows = jax.ShapeDtypeStruct(flow_x.shape, F32)
    return pl.pallas_call(
        start_kernel,
        in_specs=[SMEM] + [VMEM] * 5,
        out_specs=[VMEM] * 7,
        out_shape=[
            jax.ShapeDtypeStruct((layers, rows, subs, cols), F32),
            jax.ShapeDtypeStruct((layers + 1, 2, subs, cols), F32),
            jax.ShapeDtypeStruct((layers + 1, 2, subs, cols), F32),
            jax.ShapeDtypeStruct((layers + 1, subs, cols), F32),
            jax.ShapeDtypeStruct((layers // 2 + 1, subs, cols), F32),
            flows,
            flows,
        ],
        compiler_params=pltpu.CompilerParams(vmem_limit_bytes=VMEM_BYTES),
        cost_estimate=pl.CostEstimate(flops=10**6, bytes_accessed=8 * 10**6, transcendentals=0),
        name="start_state",
    )(place, conc.reshape(subs * layers * rows, cols), flow_x, flow_y, wet_x, wet_y)


def y_divergence(c, flows):
    before = [roll(v, 1) for v in c]
    after = [roll(v, -1) for v in c]
    slope = [0.5 * half_minmod(v - b, a - v) for v, b, a in zip(c, before, after)]
    right = [roll(v - s, -1) for v, s in zip(c, slope)]
    flux = [
        jnp.maximum(q, 0.0) * (v + s) + jnp.minimum(q, 0.0) * r
        for q, v, s, r in zip(flows, c, slope, right)
    ]
    return [f - roll(f, 1) for f in flux]


def x_faces(get, flow, first, last):
    here = get(first)
    step = 0.5 * (here - get(first - 1))
    fluxes = []
    left = None
    for i in range(first, last + 2):
        after = get(i + 1)
        step_after = 0.5 * (after - here)
        slope = half_minmod(step, step_after)
        if i > first:
            q = flow(i - 1)
            fluxes.append(
                jnp.maximum(q, 0.0) * left + jnp.minimum(q, 0.0) * (here - slope)
            )
        left = here + slope
        here, step = (after, step_after)
    return fluxes


def x_rows(state, place, swapped, l, rows):
    def get(i):
        if 0 <= i < rows:
            return state[l, i]
        j = i + 2 if i < 0 else i - rows
        pair = [ref[l, j] for ref in (swapped if i < 0 else swapped[::-1])]
        return jnp.where(place[2] == 1, *pair)

    return get


def x_flows(qx, qx_west, l):
    return lambda i: qx_west if i < 0 else qx[l, i : i + 1, :]


def west_flow(place, flow_swapped, layers, l):
    return jnp.where(place[2] == 1, *[ref[layers, 0, pl.ds(l, 1), :] for ref in flow_swapped])


def first_divergence_kernel(state, qx, qy, div):
    layers, rows = qx.shape[0], qx.shape[1]
    edge = at_edges(state.shape[2:])

    def layer(l, carry):
        c = [state[l, i] for i in range(rows)]
        parts = y_divergence(c, [qy[l, i : i + 1, :] for i in range(rows)])
        faces = x_faces(x_rows(state, None, None, l, rows), x_flows(qx, None, l), 1, rows - 3)
        for i in range(rows):
            value = jnp.where(edge, 0.0, parts[i])
            if 2 <= i < rows - 2:
                value = value + (faces[i - 1] - faces[i - 2])
            div[l, i] = value
        return carry

    lax.fori_loop(0, layers, layer, 0)


def first_divergence(state, qx, qy):
    return pl.pallas_call(
        first_divergence_kernel,
        in_specs=[VMEM] * 3,
        out_specs=VMEM,
        out_shape=jax.ShapeDtypeStruct(state.shape, F32),
        compiler_params=pltpu.CompilerParams(vmem_limit_bytes=VMEM_BYTES),
        cost_estimate=pl.CostEstimate(flops=2 * 10**7, bytes_accessed=10**7, transcendentals=0),
        name="first_divergence",
    )(state, qx, qy)


def explicit_value(c, div, rates, rates_before, inflow, renewal, scale):
    carried = pltpu.roll(c, 1, 0)
    return (
        c
        + ((renewal * (inflow - c) - scale * div) + (rates_before * carried - rates * c))
    )


def solve(star, coef, emit):
    layers, rows = star.shape[0], star.shape[1]
    batch = 4

    def some(b, carry):
        ids = [b * batch + j for j in range(batch)]

        def get(which, l, i):
            return coef[which, l, pl.ds(i, 1), :]

        value = [star[0, i] for i in ids]
        for l in range(1, layers):
            value = [star[l, i] - get(0, l, i) * v for i, v in zip(ids, value)]
            for i, v in zip(ids, value):
                star[l, i] = v
        value = [v * get(1, layers - 1, i) for i, v in zip(ids, value)]
        for i, v in zip(ids, value):
            emit(layers - 1, i, v)
        for l in range(layers - 2, -1, -1):
            value = [
                (star[l, i] + get(2, l, i) * v) * get(1, l, i) for i, v in zip(ids, value)
            ]
            for i, v in zip(ids, value):
                emit(l, i, v)
        return carry

    lax.fori_loop(0, rows // batch, some, 0)


def emit_edges(place, state, swap_a, swap_b, edges, sent):
    layers, rows = state.shape[0], state.shape[1]
    emit_swaps(place, state, swap_a, swap_b)

    def some(t, carry):
        for l in range(5):
            l = t * 5 + l
            edges[l] = pack_layer([state[l, i] for i in range(rows)])
        return carry

    lax.fori_loop(0, layers // 5, some, 0)
    emit_sent(edges, sent, False)


ROWS = 21
PIECES = 2


def split_values(slots, chunk, halves, terms):
    base = pl.multiple_of(chunk * (halves * ROWS), 8)
    values = slots[pl.ds(base, halves * ROWS), :]
    high = values.astype(BF16).astype(F32)
    terms[0] = high
    terms[1] = values - high


def spread_slots(terms, spread, hot, halves):
    sub8 = lax.broadcasted_iota(jnp.int32, (8, 128), 0)
    column = lax.broadcasted_iota(jnp.int32, (128, 128), 0).astype(F32).astype(BF16)
    zero = jnp.zeros((16, 128), BF16)
    for j in halves:
        to = slice(j * 128, (j + 1) * 128)

        def term(which, ch):
            at = j * ROWS + ch
            return terms[which, at : at + 1, :]

        label = (term(0, ROWS - 1) + term(1, ROWS - 1)).astype(jnp.int32)
        mask = jnp.where(jnp.broadcast_to((label >> 7) & 7, (8, 128)) == sub8, 1.0, 0.0)
        mask = jnp.concatenate([mask, mask], axis=0).astype(BF16)
        for ch in range(ROWS - 1):
            both = [jnp.broadcast_to(term(which, ch), (8, 128)) for which in range(2)]
            both = jnp.concatenate(both, axis=0).astype(BF16)
            spread[ch * 16 : (ch + 1) * 16, to] = both * mask
        place = jnp.broadcast_to((label & 127).astype(F32), (16, 128)).astype(BF16)
        half = label >> 10
        hits = [
            jnp.broadcast_to(jnp.where(half == h, 1.0, 0.0), (16, 128)).astype(BF16)
            for h in range(2)
        ]
        for g in range(8):
            same = column[g * 16 : (g + 1) * 16] == place
            for h in range(2):
                at = h * 128 + g * 16
                hot[at : at + 16, to] = jnp.where(same, hits[h], zero)


def totals_kernel(slots, total, *scratch):
    sets = (scratch[:3], scratch[3:])
    halves = scratch[1].shape[1] // 128
    chunks = slots.shape[0] // ROWS // halves
    piece = halves // PIECES
    total[...] = jnp.zeros_like(total)
    split_values(slots, 0, halves, sets[0][0])
    spread_slots(*sets[0], range(halves))

    def pair(i, carry):
        added = None
        for now in range(2):
            _, spread, hot = sets[now]
            filled = sets[1 - now]
            later = jnp.minimum(2 * i + 1 + now, chunks - 1)
            split_values(slots, later, halves, filled[0])
            for p in range(PIECES):
                some = slice(p * piece * 128, (p + 1) * piece * 128)
                product = lax.dot_general(
                    spread[:, some],
                    hot[:, some],
                    (((1,), (1,)), ((), ())),
                    preferred_element_type=F32,
                )
                added = product if added is None else added + product
                spread_slots(*filled, range(p * piece, (p + 1) * piece))
        total[...] += added
        return carry

    lax.fori_loop(0, chunks // 2, pair, 0)


def totals(slots):
    depth = min(2048, slots.shape[0] // ROWS * 64)
    return pl.pallas_call(
        totals_kernel,
        in_specs=[VMEM],
        out_specs=VMEM,
        out_shape=jax.ShapeDtypeStruct((320, 256), F32),
        scratch_shapes=[
            pltpu.VMEM((2, depth // 128 * ROWS, 128), F32),
            pltpu.VMEM((320, depth), BF16),
            pltpu.VMEM((256, depth), BF16),
        ]
        * 2,
        compiler_params=pltpu.CompilerParams(vmem_limit_bytes=VMEM_BYTES),
        cost_estimate=pl.CostEstimate(
            flops=12 * 10**9, bytes_accessed=4 * 10**6, transcendentals=0
        ),
        name="aggregate",
    )(slots)


def factorize(total, base_volume, diffusivity, coef):
    layers = base_volume.shape[0]
    uppers, downs = ([], [])
    for l in range(layers):
        parts = []
        for ch in (l, layers + l):
            parts.append(
                jnp.concatenate(
                    [
                        total[ch * 16 : ch * 16 + 8, h * 128 : (h + 1) * 128]
                        + total[ch * 16 + 8 : ch * 16 + 16, h * 128 : (h + 1) * 128]
                        for h in range(2)
                    ],
                    axis=0,
                )
            )
        scale = STEP / (base_volume[l] + parts[0])
        coef[3, l] = scale
        coef[4, l] = scale * parts[1]
        uppers.append(scale * diffusivity[l] if l < layers - 1 else jnp.zeros_like(scale))
        downs.append(scale * diffusivity[l - 1] if l > 0 else jnp.zeros_like(scale))
    pivot = 1.0 + uppers[0]
    coef[0, 0] = jnp.zeros_like(pivot)
    for l in range(layers):
        inverse = 1.0 / pivot
        coef[1, l] = inverse
        coef[2, l] = uppers[l]
        if l + 1 < layers:
            factor = -downs[l + 1] * inverse
            coef[0, l + 1] = factor
            pivot = 1.0 + uppers[l + 1] + downs[l + 1] + factor * uppers[l]


def first_step_kernel(
    place,
    total,
    base_volume,
    diffusivity,
    state,
    div,
    received_a,
    received_b,
    edges_before,
    edges_a,
    edges_b,
    qx,
    rates,
    rates_before,
    inflow,
    new,
    swap_a,
    swap_b,
    edges,
    sent,
    coef,
    fixes,
    star,
):
    layers, rows = base_volume.shape[0], base_volume.shape[1]
    factorize(total, base_volume, diffusivity, coef)
    received = (received_a, received_b)
    edges_swapped = (edges_a, edges_b)
    edge_pass(place, edges_before, edges_swapped, edges_before, edges_swapped, fixes)
    edge = at_edges(state.shape[2:])

    def explicit(l, carry):
        get = x_rows(state, place, received, l, rows)
        flow = x_flows(qx, west_flow(place, received, layers, l), l)
        low = x_faces(get, flow, -1, 1)
        high = x_faces(get, flow, rows - 3, rows - 1)
        fix = [roll(fixes[l], 124 - 8 * i) for i in range(rows)]
        for i in range(rows):
            value = div[l, i] + jnp.where(edge, fix[i], 0.0)
            if i < 2:
                value = value + (low[i + 1] - low[i])
            if i >= rows - 2:
                j = i - rows + 3
                value = value + (high[j] - high[j - 1])
            star[l, i] = explicit_value(
                state[l, i],
                value,
                rates[...],
                rates_before[...],
                inflow[...],
                coef[4, l, i : i + 1, :],
                coef[3, l, i : i + 1, :],
            )
        return carry

    lax.fori_loop(0, layers, explicit, 0)

    def emit(l, i, value):
        new[l, i] = value

    solve(star, coef, emit)
    emit_edges(place, new, swap_a, swap_b, edges, sent)


def state_shapes(shape):
    layers, rows, subs, cols = shape
    return [
        jax.ShapeDtypeStruct(shape, F32),
        jax.ShapeDtypeStruct((layers, 2, subs, cols), F32),
        jax.ShapeDtypeStruct((layers, 2, subs, cols), F32),
        jax.ShapeDtypeStruct((layers, subs, cols), F32),
        jax.ShapeDtypeStruct((layers // 2, subs, cols), F32),
    ]


def first_step(place, total, base_volume, diffusivity, state, *args):
    layers, rows, subs, cols = state.shape
    return pl.pallas_call(
        first_step_kernel,
        in_specs=[SMEM] + [VMEM] * 14,
        out_specs=[VMEM] * 6,
        out_shape=state_shapes(state.shape)
        + [jax.ShapeDtypeStruct((5, layers, rows, cols), F32)],
        scratch_shapes=[
            pltpu.VMEM((layers, subs, cols), F32),
            pltpu.VMEM(state.shape, F32),
        ],
        compiler_params=pltpu.CompilerParams(vmem_limit_bytes=VMEM_BYTES),
        cost_estimate=pl.CostEstimate(flops=2 * 10**7, bytes_accessed=10**7, transcendentals=0),
        name="first_step",
    )(place, total, base_volume, diffusivity, state, *args)


def later_step_kernel(
    final,
    place,
    state,
    received_a,
    received_b,
    edges_before,
    edges_a,
    edges_b,
    flow_a,
    flow_b,
    flow_edges,
    flow_edges_a,
    flow_edges_b,
    qx,
    qy,
    coef,
    rates,
    rates_before,
    inflow,
    *refs,
):
    layers, rows = qx.shape[0], qx.shape[1]
    if final:
        out, fixes, star = refs
        subs = out.shape[0] // (layers * rows)
    else:
        new, swap_a, swap_b, edges, sent, fixes, star = refs
    edge_pass(
        place, edges_before, (edges_a, edges_b), flow_edges, (flow_edges_a, flow_edges_b), fixes
    )
    edge = at_edges(state.shape[2:])

    def layer(l, carry):
        flow = x_flows(qx, west_flow(place, (flow_a, flow_b), layers, l), l)
        get = x_rows(state, place, (received_a, received_b), l, rows)
        rolled = [(roll(state[l, i], 1), roll(state[l, i], -1)) for i in range(rows)]
        faces = x_faces(get, flow, -1, rows - 1)
        x_part = [faces[i + 1] - faces[i] for i in range(rows)]
        shifted = []
        for i in range(rows):
            c, (before, after) = (state[l, i], rolled[i])
            slope = 0.5 * half_minmod(c - before, after - c)
            shifted.append((c + slope, roll(c - slope, -1)))
        base = [
            explicit_value(
                state[l, i],
                x_part[i],
                rates[...],
                rates_before[...],
                inflow[...],
                coef[4, l, i : i + 1, :],
                coef[3, l, i : i + 1, :],
            )
            for i in range(rows)
        ]
        fluxes = []
        for i in range(rows):
            q = qy[l, i : i + 1, :]
            flux = jnp.maximum(q, 0.0) * shifted[i][0] + jnp.minimum(q, 0.0) * shifted[i][1]
            fluxes.append((flux, roll(flux, 1), roll(fixes[l], 124 - 8 * i)))
        for i in range(rows):
            flux, before, fix = fluxes[i]
            y_part = jnp.where(edge, fix, flux - before)
            star[l, i] = base[i] - coef[3, l, i : i + 1, :] * y_part
        return carry

    lax.fori_loop(0, layers, layer, 0, unroll=5)

    def emit(l, i, value):
        if final:
            out[pl.ds(l * rows + i, subs, stride=layers * rows), :] = value
        else:
            new[l, i] = value

    solve(star, coef, emit)
    if not final:
        emit_edges(place, new, swap_a, swap_b, edges, sent)


def later_step(final, place, state, *args):
    layers, rows, subs, cols = state.shape
    if final:
        shapes = jax.ShapeDtypeStruct((subs * layers * rows, cols), F32)
        specs = VMEM
    else:
        shapes = state_shapes(state.shape)
        specs = [VMEM] * 5
    return pl.pallas_call(
        functools.partial(later_step_kernel, final),
        in_specs=[SMEM] + [VMEM] * 17,
        out_specs=specs,
        out_shape=shapes,
        scratch_shapes=[pltpu.VMEM((layers, subs, cols), F32), pltpu.VMEM(state.shape, F32)],
        compiler_params=pltpu.CompilerParams(vmem_limit_bytes=VMEM_BYTES),
        cost_estimate=pl.CostEstimate(flops=3 * 10**7, bytes_accessed=10**7, transcendentals=0),
        name="last_step" if final else "middle_step",
    )(place, state, *args)


def swap(values, axis, first):
    pairs = [(i, i + 1) for i in range(first, lax.axis_size(axis) - 1, 2)]
    return lax.ppermute(values, axis, pairs + [(j, i) for i, j in pairs])


def exchange(swap_a, swap_b, sent):
    rows = (swap(swap_a, "gx", 0), swap(swap_b, "gx", 1))
    columns = (swap(sent, "gy", 0), swap(sent, "gy", 1))
    return (rows, columns)


def local(
    concentration,
    base_volume,
    flow_x,
    flow_y,
    face_wet_x,
    face_wet_y,
    diffusivity,
    decay_rates,
    inflow,
    fine_volume,
    fine_discharge,
    cell_wet,
    seg_local,
):
    subs, layers, rows, cols = concentration.shape
    size_x, size_y = (lax.axis_size("gx"), lax.axis_size("gy"))
    owners = size_x * size_y
    slots = pack_slots(fine_volume, fine_discharge, cell_wet, seg_local)
    arrived = lax.all_to_all(
        slots.reshape(owners, 1, -1), ("gx", "gy"), split_axis=0, concat_axis=0, tiled=True
    ).reshape(slots.shape)

    at_x, at_y = (lax.axis_index("gx"), lax.axis_index("gy"))
    place = jnp.stack(
        [
            (at_x == size_x - 1).astype(jnp.int32),
            (at_y == size_y - 1).astype(jnp.int32),
            at_x.astype(jnp.int32) % 2,
            at_y.astype(jnp.int32) % 2,
        ]
    )
    rates = jnp.concatenate([jnp.zeros((1,), F32), decay_rates]) * STEP
    rates_before = jnp.concatenate([jnp.zeros((1,), F32), rates[:-1]])
    rates, rates_before, inflow = (
        jnp.broadcast_to(v[:, None], (subs, cols)) for v in (rates, rates_before, inflow)
    )
    state, swap_a, swap_b, edges, sent, qx, qy = start(
        place, concentration, flow_x, flow_y, face_wet_x, face_wet_y
    )
    rows_in, columns_in = exchange(swap_a, swap_b, sent)
    flows = (*rows_in, edges, *columns_in, qx, qy)
    div = first_divergence(state, qx, qy)
    constants = (rates, rates_before, inflow)
    state, swap_a, swap_b, edges, sent, coef = first_step(
        place,
        totals(arrived),
        base_volume,
        diffusivity,
        state,
        div,
        *rows_in,
        edges,
        *columns_in,
        qx,
        *constants,
    )
    for step in range(1, SUBSTEPS):
        final = step == SUBSTEPS - 1
        rows_in, columns_in = exchange(swap_a, swap_b, sent)
        result = later_step(
            final, place, state, *rows_in, edges, *columns_in, *flows, coef, *constants
        )
        if not final:
            state, swap_a, swap_b, edges, sent = result
    return result.reshape(concentration.shape)


def solution(mesh):
    fine = P(None, ("gx", "gy"))
    block = P(None, "gx", "gy")
    return jax.shard_map(
        local,
        mesh=mesh,
        in_specs=(
            P(None, None, "gx", "gy"),
            block,
            block,
            block,
            block,
            block,
            block,
            P(),
            P(),
            fine,
            fine,
            P(("gx", "gy")),
            P(("gx", "gy")),
        ),
        out_specs=P(None, None, "gx", "gy"),
        check_vma=False,
    )
```

```python
import functools

import jax
import jax.numpy as jnp
from jax import lax
from jax.experimental import pallas as pl
from jax.experimental.pallas import tpu as pltpu
from jax.sharding import PartitionSpec as P

SUBSTEPS = 3
STEP = 1.0 / SUBSTEPS
VMEM_BYTES = 24 * 1024 * 1024
PACK_VMEM_BYTES = 62 * 1024 * 1024
F32 = jnp.float32
BF16 = jnp.bfloat16

VMEM = pl.BlockSpec(memory_space=pltpu.VMEM)
SMEM = pl.BlockSpec(memory_space=pltpu.SMEM)


def half_minmod(left, right):
    return jnp.minimum(
        jnp.maximum(left, jnp.minimum(right, 0.0)), jnp.maximum(right, 0.0)
    )


def roll(values, shift):
    return pltpu.roll(values, shift % values.shape[-1], values.ndim - 1)


def lanes(shape):
    return lax.broadcasted_iota(jnp.int32, shape, len(shape) - 1)


def pack_kernel(volume, discharge, wet, segment, out):
    layers = volume.shape[0]
    rows = 2 * layers + 1
    groups = wet.shape[0]
    missing = 16 * 128
    label = jnp.where(wet[...] == 1, segment[...], missing).astype(F32)
    for k in range(groups):
        out[k * rows : k * rows + layers, :] = volume[:, k * 128 : (k + 1) * 128]
        out[k * rows + layers : k * rows + 2 * layers, :] = discharge[:, k * 128 : (k + 1) * 128]
        out[k * rows + 2 * layers : (k + 1) * rows, :] = label[k : k + 1, :]


def pack_slots(volume, discharge, wet, segment):
    layers, fine = volume.shape
    groups = fine // 128
    rows = 2 * layers + 1
    step = 128 if groups % 128 == 0 else groups
    return pl.pallas_call(
        pack_kernel,
        grid=(groups // step,),
        in_specs=[
            pl.BlockSpec((layers, step * 128), lambda i: (0, i)),
            pl.BlockSpec((layers, step * 128), lambda i: (0, i)),
            pl.BlockSpec((step, 128), lambda i: (i, 0)),
            pl.BlockSpec((step, 128), lambda i: (i, 0)),
        ],
        out_specs=pl.BlockSpec((step * rows, 128), lambda i: (i, 0)),
        out_shape=jax.ShapeDtypeStruct((groups * rows, 128), F32),
        compiler_params=pltpu.CompilerParams(vmem_limit_bytes=PACK_VMEM_BYTES),
        cost_estimate=pl.CostEstimate(flops=0, bytes_accessed=8 * 10**6, transcendentals=0),
        name="pack_slots",
    )(volume, discharge, wet.reshape(groups, 128), segment.reshape(groups, 128))


def places(shape):
    return lanes(shape) % 8


def pack_layer(rows_of_layer):
    packed = None
    for i, values in enumerate(rows_of_layer):
        moved = roll(values, 8 * i + 4)
        packed = moved if i == 0 else jnp.where(lanes(moved.shape) // 8 == i, moved, packed)
    return packed


def narrow(edges, low, high):
    even, odd = (edges[low], edges[high])
    place = places(even.shape)
    return jnp.where((place >= 2) & (place < 6), even, roll(odd, 4))


def widen(tile, layer):
    return tile if layer % 2 == 0 else roll(tile, -4)


def edge_divergence(own, left, right, flows_own, flows_left):
    place = places(own.shape)

    def divergence(four, flows):
        step = 0.5 * (roll(four, -1) - four)
        slope = half_minmod(roll(step, 1), step)
        flux = jnp.maximum(flows, 0.0) * (four + slope) + jnp.minimum(flows, 0.0) * roll(
            four - slope, -1
        )
        return flux - roll(flux, 1)

    first = divergence(
        jnp.where(place >= 4, own, left),
        jnp.where(places(flows_own.shape) >= 4, flows_own, flows_left),
    )
    last = divergence(jnp.where(place < 4, own, right), flows_own)
    return jnp.where(place < 4, last, first)


def edge_pass(place, edges, edges_swapped, flow_edges, flow_swapped, fixes):
    layers = fixes.shape[0]
    odd = place[3] == 1
    for l in range(layers):
        flow = flow_edges[layers, l : l + 1, :]
        tile = [ref[l // 2] for ref in edges_swapped]
        other = jnp.where(
            odd, *[ref[layers // 2, l // 2 : l // 2 + 1, :] for ref in flow_swapped]
        )
        fixes[l] = edge_divergence(
            edges[l],
            widen(jnp.where(odd, tile[0], tile[1]), l),
            widen(jnp.where(odd, tile[1], tile[0]), l),
            flow,
            widen(other, l),
        )


def at_edges(shape):
    lane = lanes(shape)
    return (lane < 2) | (lane >= 126)


def emit_swaps(place, state, swap_a, swap_b):
    layers, rows = state.shape[0], state.shape[1]
    low = place[2] * (rows - 2)
    swap_b[:layers] = state[:, pl.ds(low, 2)]
    swap_a[:layers] = state[:, pl.ds(rows - 2 - low, 2)]


def emit_sent(edges, sent, with_flows):
    layers = edges.shape[0] - (1 if with_flows else 0)
    for t in range(layers // 2):
        sent[t] = narrow(edges, 2 * t, 2 * t + 1)
        if with_flows:
            even = edges[layers, 2 * t : 2 * t + 1, :]
            odd = edges[layers, 2 * t + 1 : 2 * t + 2, :]
            place = places(even.shape)
            sent[layers // 2, t : t + 1, :] = jnp.where(
                (place >= 2) & (place < 6), even, roll(odd, 4)
            )


def start_kernel(
    place, conc, flow_x, flow_y, wet_x, wet_y, state, swap_a, swap_b, edges, sent, qx, qy
):
    layers, rows = flow_x.shape[0], flow_x.shape[1]
    subs = conc.shape[0] // (layers * rows)
    row = lax.broadcasted_iota(jnp.int32, flow_x.shape, 1)
    col = lax.broadcasted_iota(jnp.int32, flow_x.shape, 2)
    keep_x = jnp.where((row == rows - 1) & (place[0] == 1), 0.0, 1.0)
    keep_y = jnp.where((col == 127) & (place[1] == 1), 0.0, 1.0)
    qx[...] = flow_x[...] * wet_x[...].astype(F32) * keep_x
    qy[...] = flow_y[...] * wet_y[...].astype(F32) * keep_y
    for swap in (swap_a, swap_b):
        swap[layers] = jnp.zeros_like(swap[layers])
    edges[layers] = jnp.zeros_like(edges[layers])
    sent[layers // 2] = jnp.zeros_like(sent[layers // 2])

    def layer(l, carry):
        values = []
        for i in range(rows):
            c = conc[pl.ds(l * rows + i, subs, stride=layers * rows), :]
            values.append(c)
            state[l, i] = c
        edges[l] = pack_layer(values)
        edges[layers, pl.ds(l, 1), :] = pack_layer([qy[l, i : i + 1, :] for i in range(rows)])
        for swap in (swap_a, swap_b):
            swap[layers, 0, pl.ds(l, 1), :] = qx[l, rows - 1 :, :]
        return carry

    lax.fori_loop(0, layers, layer, 0)
    emit_swaps(place, state, swap_a, swap_b)
    emit_sent(edges, sent, True)


def start(place, conc, flow_x, flow_y, wet_x, wet_y):
    subs, layers, rows, cols = conc.shape
    flows = jax.ShapeDtypeStruct(flow_x.shape, F32)
    return pl.pallas_call(
        start_kernel,
        in_specs=[SMEM] + [VMEM] * 5,
        out_specs=[VMEM] * 7,
        out_shape=[
            jax.ShapeDtypeStruct((layers, rows, subs, cols), F32),
            jax.ShapeDtypeStruct((layers + 1, 2, subs, cols), F32),
            jax.ShapeDtypeStruct((layers + 1, 2, subs, cols), F32),
            jax.ShapeDtypeStruct((layers + 1, subs, cols), F32),
            jax.ShapeDtypeStruct((layers // 2 + 1, subs, cols), F32),
            flows,
            flows,
        ],
        compiler_params=pltpu.CompilerParams(vmem_limit_bytes=VMEM_BYTES),
        cost_estimate=pl.CostEstimate(flops=10**6, bytes_accessed=8 * 10**6, transcendentals=0),
        name="start_state",
    )(place, conc.reshape(subs * layers * rows, cols), flow_x, flow_y, wet_x, wet_y)


def y_divergence(c, flows):
    before = [roll(v, 1) for v in c]
    after = [roll(v, -1) for v in c]
    slope = [0.5 * half_minmod(v - b, a - v) for v, b, a in zip(c, before, after)]
    right = [roll(v - s, -1) for v, s in zip(c, slope)]
    flux = [
        jnp.maximum(q, 0.0) * (v + s) + jnp.minimum(q, 0.0) * r
        for q, v, s, r in zip(flows, c, slope, right)
    ]
    return [f - roll(f, 1) for f in flux]


def x_faces(get, flow, first, last):
    here = get(first)
    step = 0.5 * (here - get(first - 1))
    fluxes = []
    left = None
    for i in range(first, last + 2):
        after = get(i + 1)
        step_after = 0.5 * (after - here)
        slope = half_minmod(step, step_after)
        if i > first:
            q = flow(i - 1)
            fluxes.append(
                jnp.maximum(q, 0.0) * left + jnp.minimum(q, 0.0) * (here - slope)
            )
        left = here + slope
        here, step = (after, step_after)
    return fluxes


def x_rows(state, place, swapped, l, rows):
    def get(i):
        if 0 <= i < rows:
            return state[l, i]
        j = i + 2 if i < 0 else i - rows
        pair = [ref[l, j] for ref in (swapped if i < 0 else swapped[::-1])]
        return jnp.where(place[2] == 1, *pair)

    return get


def x_flows(qx, qx_west, l):
    return lambda i: qx_west if i < 0 else qx[l, i : i + 1, :]


def west_flow(place, flow_swapped, layers, l):
    return jnp.where(place[2] == 1, *[ref[layers, 0, pl.ds(l, 1), :] for ref in flow_swapped])


def first_divergence_kernel(state, qx, qy, div):
    layers, rows = qx.shape[0], qx.shape[1]
    edge = at_edges(state.shape[2:])

    def layer(l, carry):
        c = [state[l, i] for i in range(rows)]
        parts = y_divergence(c, [qy[l, i : i + 1, :] for i in range(rows)])
        faces = x_faces(x_rows(state, None, None, l, rows), x_flows(qx, None, l), 1, rows - 3)
        for i in range(rows):
            value = jnp.where(edge, 0.0, parts[i])
            if 2 <= i < rows - 2:
                value = value + (faces[i - 1] - faces[i - 2])
            div[l, i] = value
        return carry

    lax.fori_loop(0, layers, layer, 0)


def first_divergence(state, qx, qy):
    return pl.pallas_call(
        first_divergence_kernel,
        in_specs=[VMEM] * 3,
        out_specs=VMEM,
        out_shape=jax.ShapeDtypeStruct(state.shape, F32),
        compiler_params=pltpu.CompilerParams(vmem_limit_bytes=VMEM_BYTES),
        cost_estimate=pl.CostEstimate(flops=2 * 10**7, bytes_accessed=10**7, transcendentals=0),
        name="first_divergence",
    )(state, qx, qy)


def explicit_value(c, div, rates, rates_before, inflow, renewal, scale):
    carried = pltpu.roll(c, 1, 0)
    return (
        c
        + ((renewal * (inflow - c) - scale * div) + (rates_before * carried - rates * c))
    )


def solve(star, coef, emit):
    layers, rows = star.shape[0], star.shape[1]
    batch = 4

    def some(b, carry):
        ids = [b * batch + j for j in range(batch)]

        def get(which, l, i):
            return coef[which, l, pl.ds(i, 1), :]

        value = [star[0, i] for i in ids]
        for l in range(1, layers):
            value = [star[l, i] - get(0, l, i) * v for i, v in zip(ids, value)]
            for i, v in zip(ids, value):
                star[l, i] = v
        value = [v * get(1, layers - 1, i) for i, v in zip(ids, value)]
        for i, v in zip(ids, value):
            emit(layers - 1, i, v)
        for l in range(layers - 2, -1, -1):
            value = [
                (star[l, i] + get(2, l, i) * v) * get(1, l, i) for i, v in zip(ids, value)
            ]
            for i, v in zip(ids, value):
                emit(l, i, v)
        return carry

    lax.fori_loop(0, rows // batch, some, 0)


def emit_edges(place, state, swap_a, swap_b, edges, sent):
    layers, rows = state.shape[0], state.shape[1]
    emit_swaps(place, state, swap_a, swap_b)

    def some(t, carry):
        for l in range(5):
            l = t * 5 + l
            edges[l] = pack_layer([state[l, i] for i in range(rows)])
        return carry

    lax.fori_loop(0, layers // 5, some, 0)
    emit_sent(edges, sent, False)


ROWS = 21
PITCH_PAD = 8
PIECES = 2


def split_values(slots, chunk, halves, terms):
    base = pl.multiple_of(chunk * (halves * ROWS), 8)
    values = slots[pl.ds(base, halves * ROWS), :]
    high = values.astype(BF16).astype(F32)
    terms[0] = high
    terms[1] = values - high


def spread_slots(terms, spread, hot, halves):
    sub8 = lax.broadcasted_iota(jnp.int32, (8, 128), 0)
    column = lax.broadcasted_iota(jnp.int32, (128, 128), 0).astype(F32).astype(BF16)
    zero = jnp.zeros((16, 128), BF16)
    for j in halves:
        to = slice(j * 128, (j + 1) * 128)

        def term(which, ch):
            at = j * ROWS + ch
            return terms[which, at : at + 1, :]

        label = (term(0, ROWS - 1) + term(1, ROWS - 1)).astype(jnp.int32)
        mask = jnp.where(jnp.broadcast_to((label >> 7) & 7, (8, 128)) == sub8, 1.0, 0.0)
        mask = jnp.concatenate([mask, mask], axis=0).astype(BF16)
        for ch in range(ROWS - 1):
            both = [jnp.broadcast_to(term(which, ch), (8, 128)) for which in range(2)]
            both = jnp.concatenate(both, axis=0).astype(BF16)
            spread[ch * 16 : (ch + 1) * 16, to] = both * mask
        place = jnp.broadcast_to((label & 127).astype(F32), (16, 128)).astype(BF16)
        half = label >> 10
        hits = [
            jnp.broadcast_to(jnp.where(half == h, 1.0, 0.0), (16, 128)).astype(BF16)
            for h in range(2)
        ]
        for g in range(8):
            same = column[g * 16 : (g + 1) * 16] == place
            for h in range(2):
                at = h * 128 + g * 16
                hot[at : at + 16, to] = jnp.where(same, hits[h], zero)


def totals_kernel(slots, total, *scratch):
    sets = (scratch[:3], scratch[3:])
    halves = scratch[1].shape[1] // 128
    chunks = slots.shape[0] // ROWS // halves
    piece = halves // PIECES
    total[...] = jnp.zeros_like(total)
    split_values(slots, 0, halves, sets[0][0])
    spread_slots(*sets[0], range(halves))

    def pair(i, carry):
        added = None
        for now in range(2):
            _, spread, hot = sets[now]
            filled = sets[1 - now]
            later = jnp.minimum(2 * i + 1 + now, chunks - 1)
            split_values(slots, later, halves, filled[0])
            for p in range(PIECES):
                some = slice(p * piece * 128, (p + 1) * piece * 128)
                product = lax.dot_general(
                    spread[:, some],
                    hot[:, some],
                    (((1,), (1,)), ((), ())),
                    preferred_element_type=F32,
                )
                added = product if added is None else added + product
                spread_slots(*filled, range(p * piece, (p + 1) * piece))
        total[...] += added
        return carry

    lax.fori_loop(0, chunks // 2, pair, 0)


def totals(slots):
    depth = min(2048, slots.shape[0] // ROWS * 64)
    return pl.pallas_call(
        totals_kernel,
        in_specs=[VMEM],
        out_specs=VMEM,
        out_shape=jax.ShapeDtypeStruct((320, 256), F32),
        scratch_shapes=[
            pltpu.VMEM((2, depth // 128 * ROWS, 128), F32),
            pltpu.VMEM((320, depth), BF16),
            pltpu.VMEM((256, depth), BF16),
        ]
        * 2,
        compiler_params=pltpu.CompilerParams(vmem_limit_bytes=VMEM_BYTES),
        cost_estimate=pl.CostEstimate(
            flops=12 * 10**9, bytes_accessed=4 * 10**6, transcendentals=0
        ),
        name="aggregate",
    )(slots)


def factorize(total, base_volume, diffusivity, coef):
    layers = base_volume.shape[0]
    uppers, downs = ([], [])
    for l in range(layers):
        parts = []
        for ch in (l, layers + l):
            parts.append(
                jnp.concatenate(
                    [
                        total[ch * 16 : ch * 16 + 8, h * 128 : (h + 1) * 128]
                        + total[ch * 16 + 8 : ch * 16 + 16, h * 128 : (h + 1) * 128]
                        for h in range(2)
                    ],
                    axis=0,
                )
            )
        scale = STEP / (base_volume[l] + parts[0])
        coef[3, l] = scale
        coef[4, l] = scale * parts[1]
        uppers.append(scale * diffusivity[l] if l < layers - 1 else jnp.zeros_like(scale))
        downs.append(scale * diffusivity[l - 1] if l > 0 else jnp.zeros_like(scale))
    pivot = 1.0 + uppers[0]
    coef[0, 0] = jnp.zeros_like(pivot)
    for l in range(layers):
        inverse = 1.0 / pivot
        coef[1, l] = inverse
        coef[2, l] = uppers[l]
        if l + 1 < layers:
            factor = -downs[l + 1] * inverse
            coef[0, l + 1] = factor
            pivot = 1.0 + uppers[l + 1] + downs[l + 1] + factor * uppers[l]


def first_step_kernel(
    place,
    total,
    base_volume,
    diffusivity,
    state,
    div,
    received_a,
    received_b,
    edges_before,
    edges_a,
    edges_b,
    qx,
    rates,
    rates_before,
    inflow,
    new,
    swap_a,
    swap_b,
    edges,
    sent,
    coef,
    fixes,
    star,
):
    layers, rows = base_volume.shape[0], base_volume.shape[1]
    factorize(total, base_volume, diffusivity, coef)
    received = (received_a, received_b)
    edges_swapped = (edges_a, edges_b)
    edge_pass(place, edges_before, edges_swapped, edges_before, edges_swapped, fixes)
    edge = at_edges(state.shape[2:])

    def explicit(l, carry):
        get = x_rows(state, place, received, l, rows)
        flow = x_flows(qx, west_flow(place, received, layers, l), l)
        low = x_faces(get, flow, -1, 1)
        high = x_faces(get, flow, rows - 3, rows - 1)
        fix = [roll(fixes[l], 124 - 8 * i) for i in range(rows)]
        for i in range(rows):
            value = div[l, i] + jnp.where(edge, fix[i], 0.0)
            if i < 2:
                value = value + (low[i + 1] - low[i])
            if i >= rows - 2:
                j = i - rows + 3
                value = value + (high[j] - high[j - 1])
            star[l, i] = explicit_value(
                state[l, i],
                value,
                rates[...],
                rates_before[...],
                inflow[...],
                coef[4, l, i : i + 1, :],
                coef[3, l, i : i + 1, :],
            )
        return carry

    lax.fori_loop(0, layers, explicit, 0)

    def emit(l, i, value):
        new[l, i] = value

    solve(star, coef, emit)
    emit_edges(place, new, swap_a, swap_b, edges, sent)


def state_shapes(shape):
    layers, rows, subs, cols = shape
    return [
        jax.ShapeDtypeStruct(shape, F32),
        jax.ShapeDtypeStruct((layers, 2, subs, cols), F32),
        jax.ShapeDtypeStruct((layers, 2, subs, cols), F32),
        jax.ShapeDtypeStruct((layers, subs, cols), F32),
        jax.ShapeDtypeStruct((layers // 2, subs, cols), F32),
    ]


def first_step(place, total, base_volume, diffusivity, state, *args):
    layers, rows, subs, cols = state.shape
    return pl.pallas_call(
        first_step_kernel,
        in_specs=[SMEM] + [VMEM] * 14,
        out_specs=[VMEM] * 6,
        out_shape=state_shapes(state.shape)
        + [jax.ShapeDtypeStruct((5, layers, rows, cols), F32)],
        scratch_shapes=[
            pltpu.VMEM((layers, subs, cols), F32),
            pltpu.VMEM(state.shape, F32),
        ],
        compiler_params=pltpu.CompilerParams(vmem_limit_bytes=VMEM_BYTES),
        cost_estimate=pl.CostEstimate(flops=2 * 10**7, bytes_accessed=10**7, transcendentals=0),
        name="first_step",
    )(place, total, base_volume, diffusivity, state, *args)


def later_step_kernel(
    final,
    place,
    state,
    received_a,
    received_b,
    edges_before,
    edges_a,
    edges_b,
    flow_a,
    flow_b,
    flow_edges,
    flow_edges_a,
    flow_edges_b,
    qx,
    qy,
    coef,
    rates,
    rates_before,
    inflow,
    *refs,
):
    layers, rows = qx.shape[0], qx.shape[1]
    if final:
        out, fixes, star, staged, sems = refs
        segments = layers * rows
        subs = out.shape[0] // segments
        pitch = staged.shape[0] // subs
    else:
        new, swap_a, swap_b, edges, sent, fixes, star = refs
    edge_pass(
        place, edges_before, (edges_a, edges_b), flow_edges, (flow_edges_a, flow_edges_b), fixes
    )
    edge = at_edges(state.shape[2:])

    def layer(l, carry):
        flow = x_flows(qx, west_flow(place, (flow_a, flow_b), layers, l), l)
        get = x_rows(state, place, (received_a, received_b), l, rows)
        rolled = [(roll(state[l, i], 1), roll(state[l, i], -1)) for i in range(rows)]
        faces = x_faces(get, flow, -1, rows - 1)
        x_part = [faces[i + 1] - faces[i] for i in range(rows)]
        shifted = []
        for i in range(rows):
            c, (before, after) = (state[l, i], rolled[i])
            slope = 0.5 * half_minmod(c - before, after - c)
            shifted.append((c + slope, roll(c - slope, -1)))
        base = [
            explicit_value(
                state[l, i],
                x_part[i],
                rates[...],
                rates_before[...],
                inflow[...],
                coef[4, l, i : i + 1, :],
                coef[3, l, i : i + 1, :],
            )
            for i in range(rows)
        ]
        fluxes = []
        for i in range(rows):
            q = qy[l, i : i + 1, :]
            flux = jnp.maximum(q, 0.0) * shifted[i][0] + jnp.minimum(q, 0.0) * shifted[i][1]
            fluxes.append((flux, roll(flux, 1), roll(fixes[l], 124 - 8 * i)))
        for i in range(rows):
            flux, before, fix = fluxes[i]
            y_part = jnp.where(edge, fix, flux - before)
            star[l, i] = base[i] - coef[3, l, i : i + 1, :] * y_part
        return carry

    lax.fori_loop(0, layers, layer, 0, unroll=5)

    def emit(l, i, value):
        if final:
            staged[pl.ds(l * rows + i, subs, stride=pitch), :] = value
        else:
            new[l, i] = value

    solve(star, coef, emit)
    if final:
        copies = [
            pltpu.make_async_copy(
                staged.at[pl.ds(k * pitch, segments)],
                out.at[pl.ds(k * segments, segments)],
                sems.at[k],
            )
            for k in range(subs)
        ]
        for copy in copies:
            copy.start()
        for copy in copies:
            copy.wait()
    else:
        emit_edges(place, new, swap_a, swap_b, edges, sent)


def later_step(final, place, state, *args):
    layers, rows, subs, cols = state.shape
    scratch = [pltpu.VMEM((layers, subs, cols), F32), pltpu.VMEM(state.shape, F32)]
    if final:
        scratch += [
            pltpu.VMEM((subs * (layers * rows + PITCH_PAD), cols), F32),
            pltpu.SemaphoreType.DMA((subs,)),
        ]
        shapes = jax.ShapeDtypeStruct((subs * layers * rows, cols), F32)
        specs = pl.BlockSpec(memory_space=pl.ANY)
    else:
        shapes = state_shapes(state.shape)
        specs = [VMEM] * 5
    return pl.pallas_call(
        functools.partial(later_step_kernel, final),
        in_specs=[SMEM] + [VMEM] * 17,
        out_specs=specs,
        out_shape=shapes,
        scratch_shapes=scratch,
        compiler_params=pltpu.CompilerParams(vmem_limit_bytes=VMEM_BYTES),
        cost_estimate=pl.CostEstimate(flops=3 * 10**7, bytes_accessed=10**7, transcendentals=0),
        name="last_step" if final else "middle_step",
    )(place, state, *args)


def swap(values, axis, first):
    pairs = [(i, i + 1) for i in range(first, lax.axis_size(axis) - 1, 2)]
    return lax.ppermute(values, axis, pairs + [(j, i) for i, j in pairs])


def exchange(swap_a, swap_b, sent):
    rows = (swap(swap_a, "gx", 0), swap(swap_b, "gx", 1))
    columns = (swap(sent, "gy", 0), swap(sent, "gy", 1))
    return (rows, columns)


def local(
    concentration,
    base_volume,
    flow_x,
    flow_y,
    face_wet_x,
    face_wet_y,
    diffusivity,
    decay_rates,
    inflow,
    fine_volume,
    fine_discharge,
    cell_wet,
    seg_local,
):
    subs, layers, rows, cols = concentration.shape
    size_x, size_y = (lax.axis_size("gx"), lax.axis_size("gy"))
    owners = size_x * size_y
    slots = pack_slots(fine_volume, fine_discharge, cell_wet, seg_local)
    arrived = lax.all_to_all(
        slots.reshape(owners, 1, -1), ("gx", "gy"), split_axis=0, concat_axis=0, tiled=True
    ).reshape(slots.shape)

    at_x, at_y = (lax.axis_index("gx"), lax.axis_index("gy"))
    place = jnp.stack(
        [
            (at_x == size_x - 1).astype(jnp.int32),
            (at_y == size_y - 1).astype(jnp.int32),
            at_x.astype(jnp.int32) % 2,
            at_y.astype(jnp.int32) % 2,
        ]
    )
    rates = jnp.concatenate([jnp.zeros((1,), F32), decay_rates]) * STEP
    rates_before = jnp.concatenate([jnp.zeros((1,), F32), rates[:-1]])
    rates, rates_before, inflow = (
        jnp.broadcast_to(v[:, None], (subs, cols)) for v in (rates, rates_before, inflow)
    )
    state, swap_a, swap_b, edges, sent, qx, qy = start(
        place, concentration, flow_x, flow_y, face_wet_x, face_wet_y
    )
    rows_in, columns_in = exchange(swap_a, swap_b, sent)
    flows = (*rows_in, edges, *columns_in, qx, qy)
    div = first_divergence(state, qx, qy)
    constants = (rates, rates_before, inflow)
    state, swap_a, swap_b, edges, sent, coef = first_step(
        place,
        totals(arrived),
        base_volume,
        diffusivity,
        state,
        div,
        *rows_in,
        edges,
        *columns_in,
        qx,
        *constants,
    )
    for step in range(1, SUBSTEPS):
        final = step == SUBSTEPS - 1
        rows_in, columns_in = exchange(swap_a, swap_b, sent)
        result = later_step(
            final, place, state, *rows_in, edges, *columns_in, *flows, coef, *constants
        )
        if not final:
            state, swap_a, swap_b, edges, sent = result
    return result.reshape(concentration.shape)


def solution(mesh):
    fine = P(None, ("gx", "gy"))
    block = P(None, "gx", "gy")
    return jax.shard_map(
        local,
        mesh=mesh,
        in_specs=(
            P(None, None, "gx", "gy"),
            block,
            block,
            block,
            block,
            block,
            block,
            P(),
            P(),
            fine,
            fine,
            P(("gx", "gy")),
            P(("gx", "gy")),
        ),
        out_specs=P(None, None, "gx", "gy"),
        check_vma=False,
    )
```

```python
import functools

import jax
import jax.numpy as jnp
from jax import lax
from jax.experimental import pallas as pl
from jax.experimental.pallas import tpu as pltpu
from jax.sharding import PartitionSpec as P

SUBSTEPS = 3
STEP = 1.0 / SUBSTEPS
VMEM_BYTES = 24 * 1024 * 1024
PACK_VMEM_BYTES = 62 * 1024 * 1024
F32 = jnp.float32
BF16 = jnp.bfloat16

VMEM = pl.BlockSpec(memory_space=pltpu.VMEM)
SMEM = pl.BlockSpec(memory_space=pltpu.SMEM)


def half_minmod(left, right):
    return jnp.minimum(
        jnp.maximum(left, jnp.minimum(right, 0.0)), jnp.maximum(right, 0.0)
    )


def roll(values, shift):
    return pltpu.roll(values, shift % values.shape[-1], values.ndim - 1)


def lanes(shape):
    return lax.broadcasted_iota(jnp.int32, shape, len(shape) - 1)


def pack_kernel(volume, discharge, wet, segment, out):
    layers = volume.shape[0]
    rows = 2 * layers + 1
    groups = wet.shape[0]
    missing = 16 * 128
    label = jnp.where(wet[...] == 1, segment[...], missing).astype(F32)
    for k in range(groups):
        out[k * rows : k * rows + layers, :] = volume[:, k * 128 : (k + 1) * 128]
        out[k * rows + layers : k * rows + 2 * layers, :] = discharge[:, k * 128 : (k + 1) * 128]
        out[k * rows + 2 * layers : (k + 1) * rows, :] = label[k : k + 1, :]


def pack_slots(volume, discharge, wet, segment):
    layers, fine = volume.shape
    groups = fine // 128
    rows = 2 * layers + 1
    step = 128 if groups % 128 == 0 else groups
    return pl.pallas_call(
        pack_kernel,
        grid=(groups // step,),
        in_specs=[
            pl.BlockSpec((layers, step * 128), lambda i: (0, i)),
            pl.BlockSpec((layers, step * 128), lambda i: (0, i)),
            pl.BlockSpec((step, 128), lambda i: (i, 0)),
            pl.BlockSpec((step, 128), lambda i: (i, 0)),
        ],
        out_specs=pl.BlockSpec((step * rows, 128), lambda i: (i, 0)),
        out_shape=jax.ShapeDtypeStruct((groups * rows, 128), F32),
        compiler_params=pltpu.CompilerParams(vmem_limit_bytes=PACK_VMEM_BYTES),
        cost_estimate=pl.CostEstimate(flops=0, bytes_accessed=8 * 10**6, transcendentals=0),
        name="pack_slots",
    )(volume, discharge, wet.reshape(groups, 128), segment.reshape(groups, 128))


def places(shape):
    return lanes(shape) % 8


def pack_layer(rows_of_layer):
    packed = None
    for i, values in enumerate(rows_of_layer):
        moved = roll(values, 8 * i + 4)
        packed = moved if i == 0 else jnp.where(lanes(moved.shape) // 8 == i, moved, packed)
    return packed


def narrow(edges, low, high):
    even, odd = (edges[low], edges[high])
    place = places(even.shape)
    return jnp.where((place >= 2) & (place < 6), even, roll(odd, 4))


def widen(tile, layer):
    return tile if layer % 2 == 0 else roll(tile, -4)


def edge_divergence(own, left, right, flows_own, flows_left):
    place = places(own.shape)

    def divergence(four, flows):
        step = 0.5 * (roll(four, -1) - four)
        slope = half_minmod(roll(step, 1), step)
        flux = jnp.maximum(flows, 0.0) * (four + slope) + jnp.minimum(flows, 0.0) * roll(
            four - slope, -1
        )
        return flux - roll(flux, 1)

    first = divergence(
        jnp.where(place >= 4, own, left),
        jnp.where(places(flows_own.shape) >= 4, flows_own, flows_left),
    )
    last = divergence(jnp.where(place < 4, own, right), flows_own)
    return jnp.where(place < 4, last, first)


def edge_pass(place, edges, edges_swapped, flow_edges, flow_swapped, fixes):
    layers = fixes.shape[0]
    odd = place[3] == 1
    for l in range(layers):
        flow = flow_edges[layers, l : l + 1, :]
        tile = [ref[l // 2] for ref in edges_swapped]
        other = jnp.where(
            odd, *[ref[layers // 2, l // 2 : l // 2 + 1, :] for ref in flow_swapped]
        )
        fixes[l] = edge_divergence(
            edges[l],
            widen(jnp.where(odd, tile[0], tile[1]), l),
            widen(jnp.where(odd, tile[1], tile[0]), l),
            flow,
            widen(other, l),
        )


def at_edges(shape):
    lane = lanes(shape)
    return (lane < 2) | (lane >= 126)


def emit_swaps(place, state, swap_a, swap_b):
    layers, rows = state.shape[0], state.shape[1]
    low = place[2] * (rows - 2)
    swap_b[:layers] = state[:, pl.ds(low, 2)]
    swap_a[:layers] = state[:, pl.ds(rows - 2 - low, 2)]


def emit_sent(edges, sent, with_flows):
    layers = edges.shape[0] - (1 if with_flows else 0)
    for t in range(layers // 2):
        sent[t] = narrow(edges, 2 * t, 2 * t + 1)
        if with_flows:
            even = edges[layers, 2 * t : 2 * t + 1, :]
            odd = edges[layers, 2 * t + 1 : 2 * t + 2, :]
            place = places(even.shape)
            sent[layers // 2, t : t + 1, :] = jnp.where(
                (place >= 2) & (place < 6), even, roll(odd, 4)
            )


def start_kernel(
    place, conc, flow_x, flow_y, wet_x, wet_y, state, swap_a, swap_b, edges, sent, qx, qy
):
    layers, rows = flow_x.shape[0], flow_x.shape[1]
    subs = conc.shape[0] // (layers * rows)
    row = lax.broadcasted_iota(jnp.int32, flow_x.shape, 1)
    col = lax.broadcasted_iota(jnp.int32, flow_x.shape, 2)
    keep_x = jnp.where((row == rows - 1) & (place[0] == 1), 0.0, 1.0)
    keep_y = jnp.where((col == 127) & (place[1] == 1), 0.0, 1.0)
    qx[...] = flow_x[...] * wet_x[...].astype(F32) * keep_x
    qy[...] = flow_y[...] * wet_y[...].astype(F32) * keep_y
    for swap in (swap_a, swap_b):
        swap[layers] = jnp.zeros_like(swap[layers])
    edges[layers] = jnp.zeros_like(edges[layers])
    sent[layers // 2] = jnp.zeros_like(sent[layers // 2])

    def layer(l, carry):
        values = []
        for i in range(rows):
            c = conc[pl.ds(l * rows + i, subs, stride=layers * rows), :]
            values.append(c)
            state[l, i] = c
        edges[l] = pack_layer(values)
        edges[layers, pl.ds(l, 1), :] = pack_layer([qy[l, i : i + 1, :] for i in range(rows)])
        for swap in (swap_a, swap_b):
            swap[layers, 0, pl.ds(l, 1), :] = qx[l, rows - 1 :, :]
        return carry

    lax.fori_loop(0, layers, layer, 0)
    emit_swaps(place, state, swap_a, swap_b)
    emit_sent(edges, sent, True)


def start(place, conc, flow_x, flow_y, wet_x, wet_y):
    subs, layers, rows, cols = conc.shape
    flows = jax.ShapeDtypeStruct(flow_x.shape, F32)
    return pl.pallas_call(
        start_kernel,
        in_specs=[SMEM] + [VMEM] * 5,
        out_specs=[VMEM] * 7,
        out_shape=[
            jax.ShapeDtypeStruct((layers, rows, subs, cols), F32),
            jax.ShapeDtypeStruct((layers + 1, 2, subs, cols), F32),
            jax.ShapeDtypeStruct((layers + 1, 2, subs, cols), F32),
            jax.ShapeDtypeStruct((layers + 1, subs, cols), F32),
            jax.ShapeDtypeStruct((layers // 2 + 1, subs, cols), F32),
            flows,
            flows,
        ],
        compiler_params=pltpu.CompilerParams(vmem_limit_bytes=VMEM_BYTES),
        cost_estimate=pl.CostEstimate(flops=10**6, bytes_accessed=8 * 10**6, transcendentals=0),
        name="start_state",
    )(place, conc.reshape(subs * layers * rows, cols), flow_x, flow_y, wet_x, wet_y)


def y_divergence(c, flows):
    before = [roll(v, 1) for v in c]
    after = [roll(v, -1) for v in c]
    slope = [0.5 * half_minmod(v - b, a - v) for v, b, a in zip(c, before, after)]
    right = [roll(v - s, -1) for v, s in zip(c, slope)]
    flux = [
        jnp.maximum(q, 0.0) * (v + s) + jnp.minimum(q, 0.0) * r
        for q, v, s, r in zip(flows, c, slope, right)
    ]
    return [f - roll(f, 1) for f in flux]


def x_faces(get, flow, first, last):
    here = get(first)
    step = 0.5 * (here - get(first - 1))
    fluxes = []
    left = None
    for i in range(first, last + 2):
        after = get(i + 1)
        step_after = 0.5 * (after - here)
        slope = half_minmod(step, step_after)
        if i > first:
            q = flow(i - 1)
            fluxes.append(
                jnp.maximum(q, 0.0) * left + jnp.minimum(q, 0.0) * (here - slope)
            )
        left = here + slope
        here, step = (after, step_after)
    return fluxes


def x_rows(state, place, swapped, l, rows):
    def get(i):
        if 0 <= i < rows:
            return state[l, i]
        j = i + 2 if i < 0 else i - rows
        pair = [ref[l, j] for ref in (swapped if i < 0 else swapped[::-1])]
        return jnp.where(place[2] == 1, *pair)

    return get


def x_flows(qx, qx_west, l):
    return lambda i: qx_west if i < 0 else qx[l, i : i + 1, :]


def west_flow(place, flow_swapped, layers, l):
    return jnp.where(place[2] == 1, *[ref[layers, 0, pl.ds(l, 1), :] for ref in flow_swapped])


def first_divergence_kernel(state, qx, qy, div):
    layers, rows = qx.shape[0], qx.shape[1]
    edge = at_edges(state.shape[2:])

    def layer(l, carry):
        c = [state[l, i] for i in range(rows)]
        parts = y_divergence(c, [qy[l, i : i + 1, :] for i in range(rows)])
        faces = x_faces(x_rows(state, None, None, l, rows), x_flows(qx, None, l), 1, rows - 3)
        for i in range(rows):
            value = jnp.where(edge, 0.0, parts[i])
            if 2 <= i < rows - 2:
                value = value + (faces[i - 1] - faces[i - 2])
            div[l, i] = value
        return carry

    lax.fori_loop(0, layers, layer, 0)


def first_divergence(state, qx, qy):
    return pl.pallas_call(
        first_divergence_kernel,
        in_specs=[VMEM] * 3,
        out_specs=VMEM,
        out_shape=jax.ShapeDtypeStruct(state.shape, F32),
        compiler_params=pltpu.CompilerParams(vmem_limit_bytes=VMEM_BYTES),
        cost_estimate=pl.CostEstimate(flops=2 * 10**7, bytes_accessed=10**7, transcendentals=0),
        name="first_divergence",
    )(state, qx, qy)


def explicit_value(c, div, rates, rates_before, inflow, renewal, scale):
    carried = pltpu.roll(c, 1, 0)
    return (
        c
        + ((renewal * (inflow - c) - scale * div) + (rates_before * carried - rates * c))
    )


def solve(star, coef, emit):
    layers, rows = star.shape[0], star.shape[1]
    batch = 4

    def some(b, carry):
        ids = [b * batch + j for j in range(batch)]

        def get(which, l, i):
            return coef[which, l, pl.ds(i, 1), :]

        value = [star[0, i] for i in ids]
        for l in range(1, layers):
            value = [star[l, i] - get(0, l, i) * v for i, v in zip(ids, value)]
            for i, v in zip(ids, value):
                star[l, i] = v
        value = [v * get(1, layers - 1, i) for i, v in zip(ids, value)]
        for i, v in zip(ids, value):
            emit(layers - 1, i, v)
        for l in range(layers - 2, -1, -1):
            value = [
                (star[l, i] + get(2, l, i) * v) * get(1, l, i) for i, v in zip(ids, value)
            ]
            for i, v in zip(ids, value):
                emit(l, i, v)
        return carry

    lax.fori_loop(0, rows // batch, some, 0)


def emit_edges(place, state, swap_a, swap_b, edges, sent):
    layers, rows = state.shape[0], state.shape[1]
    emit_swaps(place, state, swap_a, swap_b)

    def some(t, carry):
        for l in range(5):
            l = t * 5 + l
            edges[l] = pack_layer([state[l, i] for i in range(rows)])
        return carry

    lax.fori_loop(0, layers // 5, some, 0)
    emit_sent(edges, sent, False)


ROWS = 21
PITCH_PAD = 8
PIECES = 2


def split_values(slots, chunk, halves, terms):
    base = pl.multiple_of(chunk * (halves * ROWS), 8)
    values = slots[pl.ds(base, halves * ROWS), :]
    high = values.astype(BF16).astype(F32)
    terms[0] = high
    terms[1] = values - high


def spread_slots(terms, spread, hot, halves):
    sub8 = lax.broadcasted_iota(jnp.int32, (8, 128), 0)
    column = lax.broadcasted_iota(jnp.int32, (128, 128), 0).astype(F32).astype(BF16)
    zero = jnp.zeros((16, 128), BF16)
    for j in halves:
        to = slice(j * 128, (j + 1) * 128)

        def term(which, ch):
            at = j * ROWS + ch
            return terms[which, at : at + 1, :]

        label = (term(0, ROWS - 1) + term(1, ROWS - 1)).astype(jnp.int32)
        mask = jnp.where(jnp.broadcast_to((label >> 7) & 7, (8, 128)) == sub8, 1.0, 0.0)
        mask = jnp.concatenate([mask, mask], axis=0).astype(BF16)
        for ch in range(ROWS - 1):
            both = [jnp.broadcast_to(term(which, ch), (8, 128)) for which in range(2)]
            both = jnp.concatenate(both, axis=0).astype(BF16)
            spread[ch * 16 : (ch + 1) * 16, to] = both * mask
        place = jnp.broadcast_to((label & 127).astype(F32), (16, 128)).astype(BF16)
        half = label >> 10
        hits = [
            jnp.broadcast_to(jnp.where(half == h, 1.0, 0.0), (16, 128)).astype(BF16)
            for h in range(2)
        ]
        for g in range(8):
            same = column[g * 16 : (g + 1) * 16] == place
            for h in range(2):
                at = h * 128 + g * 16
                hot[at : at + 16, to] = jnp.where(same, hits[h], zero)


def totals_kernel(slots, total, *scratch):
    sets = (scratch[:3], scratch[3:])
    halves = scratch[1].shape[1] // 128
    chunks = slots.shape[0] // ROWS // halves
    piece = halves // PIECES
    total[...] = jnp.zeros_like(total)
    split_values(slots, 0, halves, sets[0][0])
    spread_slots(*sets[0], range(halves))

    def pair(i, carry):
        added = None
        for now in range(2):
            _, spread, hot = sets[now]
            filled = sets[1 - now]
            later = jnp.minimum(2 * i + 1 + now, chunks - 1)
            split_values(slots, later, halves, filled[0])
            for p in range(PIECES):
                some = slice(p * piece * 128, (p + 1) * piece * 128)
                product = lax.dot_general(
                    spread[:, some],
                    hot[:, some],
                    (((1,), (1,)), ((), ())),
                    preferred_element_type=F32,
                )
                added = product if added is None else added + product
                spread_slots(*filled, range(p * piece, (p + 1) * piece))
        total[...] += added
        return carry

    lax.fori_loop(0, chunks // 2, pair, 0)


def totals(slots):
    depth = min(4096, slots.shape[0] // ROWS * 64)
    return pl.pallas_call(
        totals_kernel,
        in_specs=[VMEM],
        out_specs=VMEM,
        out_shape=jax.ShapeDtypeStruct((320, 256), F32),
        scratch_shapes=[
            pltpu.VMEM((2, depth // 128 * ROWS, 128), F32),
            pltpu.VMEM((320, depth), BF16),
            pltpu.VMEM((256, depth), BF16),
        ]
        * 2,
        compiler_params=pltpu.CompilerParams(vmem_limit_bytes=VMEM_BYTES),
        cost_estimate=pl.CostEstimate(
            flops=12 * 10**9, bytes_accessed=4 * 10**6, transcendentals=0
        ),
        name="aggregate",
    )(slots)


def factorize(total, base_volume, diffusivity, coef):
    layers = base_volume.shape[0]
    uppers, downs = ([], [])
    for l in range(layers):
        parts = []
        for ch in (l, layers + l):
            parts.append(
                jnp.concatenate(
                    [
                        total[ch * 16 : ch * 16 + 8, h * 128 : (h + 1) * 128]
                        + total[ch * 16 + 8 : ch * 16 + 16, h * 128 : (h + 1) * 128]
                        for h in range(2)
                    ],
                    axis=0,
                )
            )
        scale = STEP / (base_volume[l] + parts[0])
        coef[3, l] = scale
        coef[4, l] = scale * parts[1]
        uppers.append(scale * diffusivity[l] if l < layers - 1 else jnp.zeros_like(scale))
        downs.append(scale * diffusivity[l - 1] if l > 0 else jnp.zeros_like(scale))
    pivot = 1.0 + uppers[0]
    coef[0, 0] = jnp.zeros_like(pivot)
    for l in range(layers):
        inverse = 1.0 / pivot
        coef[1, l] = inverse
        coef[2, l] = uppers[l]
        if l + 1 < layers:
            factor = -downs[l + 1] * inverse
            coef[0, l + 1] = factor
            pivot = 1.0 + uppers[l + 1] + downs[l + 1] + factor * uppers[l]


def first_step_kernel(
    place,
    total,
    base_volume,
    diffusivity,
    state,
    div,
    received_a,
    received_b,
    edges_before,
    edges_a,
    edges_b,
    qx,
    rates,
    rates_before,
    inflow,
    new,
    swap_a,
    swap_b,
    edges,
    sent,
    coef,
    fixes,
    star,
):
    layers, rows = base_volume.shape[0], base_volume.shape[1]
    factorize(total, base_volume, diffusivity, coef)
    received = (received_a, received_b)
    edges_swapped = (edges_a, edges_b)
    edge_pass(place, edges_before, edges_swapped, edges_before, edges_swapped, fixes)
    edge = at_edges(state.shape[2:])

    def explicit(l, carry):
        get = x_rows(state, place, received, l, rows)
        flow = x_flows(qx, west_flow(place, received, layers, l), l)
        low = x_faces(get, flow, -1, 1)
        high = x_faces(get, flow, rows - 3, rows - 1)
        fix = [roll(fixes[l], 124 - 8 * i) for i in range(rows)]
        for i in range(rows):
            value = div[l, i] + jnp.where(edge, fix[i], 0.0)
            if i < 2:
                value = value + (low[i + 1] - low[i])
            if i >= rows - 2:
                j = i - rows + 3
                value = value + (high[j] - high[j - 1])
            star[l, i] = explicit_value(
                state[l, i],
                value,
                rates[...],
                rates_before[...],
                inflow[...],
                coef[4, l, i : i + 1, :],
                coef[3, l, i : i + 1, :],
            )
        return carry

    lax.fori_loop(0, layers, explicit, 0)

    def emit(l, i, value):
        new[l, i] = value

    solve(star, coef, emit)
    emit_edges(place, new, swap_a, swap_b, edges, sent)


def state_shapes(shape):
    layers, rows, subs, cols = shape
    return [
        jax.ShapeDtypeStruct(shape, F32),
        jax.ShapeDtypeStruct((layers, 2, subs, cols), F32),
        jax.ShapeDtypeStruct((layers, 2, subs, cols), F32),
        jax.ShapeDtypeStruct((layers, subs, cols), F32),
        jax.ShapeDtypeStruct((layers // 2, subs, cols), F32),
    ]


def first_step(place, total, base_volume, diffusivity, state, *args):
    layers, rows, subs, cols = state.shape
    return pl.pallas_call(
        first_step_kernel,
        in_specs=[SMEM] + [VMEM] * 14,
        out_specs=[VMEM] * 6,
        out_shape=state_shapes(state.shape)
        + [jax.ShapeDtypeStruct((5, layers, rows, cols), F32)],
        scratch_shapes=[
            pltpu.VMEM((layers, subs, cols), F32),
            pltpu.VMEM(state.shape, F32),
        ],
        compiler_params=pltpu.CompilerParams(vmem_limit_bytes=VMEM_BYTES),
        cost_estimate=pl.CostEstimate(flops=2 * 10**7, bytes_accessed=10**7, transcendentals=0),
        name="first_step",
    )(place, total, base_volume, diffusivity, state, *args)


def later_step_kernel(
    final,
    place,
    state,
    received_a,
    received_b,
    edges_before,
    edges_a,
    edges_b,
    flow_a,
    flow_b,
    flow_edges,
    flow_edges_a,
    flow_edges_b,
    qx,
    qy,
    coef,
    rates,
    rates_before,
    inflow,
    *refs,
):
    layers, rows = qx.shape[0], qx.shape[1]
    if final:
        out, fixes, star, staged, sems = refs
        segments = layers * rows
        subs = out.shape[0] // segments
        pitch = staged.shape[0] // subs
    else:
        new, swap_a, swap_b, edges, sent, fixes, star = refs
    edge_pass(
        place, edges_before, (edges_a, edges_b), flow_edges, (flow_edges_a, flow_edges_b), fixes
    )
    edge = at_edges(state.shape[2:])

    def layer(l, carry):
        flow = x_flows(qx, west_flow(place, (flow_a, flow_b), layers, l), l)
        get = x_rows(state, place, (received_a, received_b), l, rows)
        rolled = [(roll(state[l, i], 1), roll(state[l, i], -1)) for i in range(rows)]
        faces = x_faces(get, flow, -1, rows - 1)
        x_part = [faces[i + 1] - faces[i] for i in range(rows)]
        shifted = []
        for i in range(rows):
            c, (before, after) = (state[l, i], rolled[i])
            slope = 0.5 * half_minmod(c - before, after - c)
            shifted.append((c + slope, roll(c - slope, -1)))
        base = [
            explicit_value(
                state[l, i],
                x_part[i],
                rates[...],
                rates_before[...],
                inflow[...],
                coef[4, l, i : i + 1, :],
                coef[3, l, i : i + 1, :],
            )
            for i in range(rows)
        ]
        fluxes = []
        for i in range(rows):
            q = qy[l, i : i + 1, :]
            flux = jnp.maximum(q, 0.0) * shifted[i][0] + jnp.minimum(q, 0.0) * shifted[i][1]
            fluxes.append((flux, roll(flux, 1), roll(fixes[l], 124 - 8 * i)))
        for i in range(rows):
            flux, before, fix = fluxes[i]
            y_part = jnp.where(edge, fix, flux - before)
            star[l, i] = base[i] - coef[3, l, i : i + 1, :] * y_part
        return carry

    lax.fori_loop(0, layers, layer, 0, unroll=5)

    def emit(l, i, value):
        if final:
            staged[pl.ds(l * rows + i, subs, stride=pitch), :] = value
        else:
            new[l, i] = value

    solve(star, coef, emit)
    if final:
        copies = [
            pltpu.make_async_copy(
                staged.at[pl.ds(k * pitch, segments)],
                out.at[pl.ds(k * segments, segments)],
                sems.at[k],
            )
            for k in range(subs)
        ]
        for copy in copies:
            copy.start()
        for copy in copies:
            copy.wait()
    else:
        emit_edges(place, new, swap_a, swap_b, edges, sent)


def later_step(final, place, state, *args):
    layers, rows, subs, cols = state.shape
    scratch = [pltpu.VMEM((layers, subs, cols), F32), pltpu.VMEM(state.shape, F32)]
    if final:
        scratch += [
            pltpu.VMEM((subs * (layers * rows + PITCH_PAD), cols), F32),
            pltpu.SemaphoreType.DMA((subs,)),
        ]
        shapes = jax.ShapeDtypeStruct((subs * layers * rows, cols), F32)
        specs = pl.BlockSpec(memory_space=pl.ANY)
    else:
        shapes = state_shapes(state.shape)
        specs = [VMEM] * 5
    return pl.pallas_call(
        functools.partial(later_step_kernel, final),
        in_specs=[SMEM] + [VMEM] * 17,
        out_specs=specs,
        out_shape=shapes,
        scratch_shapes=scratch,
        compiler_params=pltpu.CompilerParams(vmem_limit_bytes=VMEM_BYTES),
        cost_estimate=pl.CostEstimate(flops=3 * 10**7, bytes_accessed=10**7, transcendentals=0),
        name="last_step" if final else "middle_step",
    )(place, state, *args)


def swap(values, axis, first):
    pairs = [(i, i + 1) for i in range(first, lax.axis_size(axis) - 1, 2)]
    return lax.ppermute(values, axis, pairs + [(j, i) for i, j in pairs])


def exchange(swap_a, swap_b, sent):
    rows = (swap(swap_a, "gx", 0), swap(swap_b, "gx", 1))
    columns = (swap(sent, "gy", 0), swap(sent, "gy", 1))
    return (rows, columns)


def local(
    concentration,
    base_volume,
    flow_x,
    flow_y,
    face_wet_x,
    face_wet_y,
    diffusivity,
    decay_rates,
    inflow,
    fine_volume,
    fine_discharge,
    cell_wet,
    seg_local,
):
    subs, layers, rows, cols = concentration.shape
    size_x, size_y = (lax.axis_size("gx"), lax.axis_size("gy"))
    owners = size_x * size_y
    slots = pack_slots(fine_volume, fine_discharge, cell_wet, seg_local)
    arrived = lax.all_to_all(
        slots.reshape(owners, 1, -1), ("gx", "gy"), split_axis=0, concat_axis=0, tiled=True
    ).reshape(slots.shape)

    at_x, at_y = (lax.axis_index("gx"), lax.axis_index("gy"))
    place = jnp.stack(
        [
            (at_x == size_x - 1).astype(jnp.int32),
            (at_y == size_y - 1).astype(jnp.int32),
            at_x.astype(jnp.int32) % 2,
            at_y.astype(jnp.int32) % 2,
        ]
    )
    rates = jnp.concatenate([jnp.zeros((1,), F32), decay_rates]) * STEP
    rates_before = jnp.concatenate([jnp.zeros((1,), F32), rates[:-1]])
    rates, rates_before, inflow = (
        jnp.broadcast_to(v[:, None], (subs, cols)) for v in (rates, rates_before, inflow)
    )
    state, swap_a, swap_b, edges, sent, qx, qy = start(
        place, concentration, flow_x, flow_y, face_wet_x, face_wet_y
    )
    rows_in, columns_in = exchange(swap_a, swap_b, sent)
    flows = (*rows_in, edges, *columns_in, qx, qy)
    div = first_divergence(state, qx, qy)
    constants = (rates, rates_before, inflow)
    state, swap_a, swap_b, edges, sent, coef = first_step(
        place,
        totals(arrived),
        base_volume,
        diffusivity,
        state,
        div,
        *rows_in,
        edges,
        *columns_in,
        qx,
        *constants,
    )
    for step in range(1, SUBSTEPS):
        final = step == SUBSTEPS - 1
        rows_in, columns_in = exchange(swap_a, swap_b, sent)
        result = later_step(
            final, place, state, *rows_in, edges, *columns_in, *flows, coef, *constants
        )
        if not final:
            state, swap_a, swap_b, edges, sent = result
    return result.reshape(concentration.shape)


def solution(mesh):
    fine = P(None, ("gx", "gy"))
    block = P(None, "gx", "gy")
    return jax.shard_map(
        local,
        mesh=mesh,
        in_specs=(
            P(None, None, "gx", "gy"),
            block,
            block,
            block,
            block,
            block,
            block,
            P(),
            P(),
            fine,
            fine,
            P(("gx", "gy")),
            P(("gx", "gy")),
        ),
        out_specs=P(None, None, "gx", "gy"),
        check_vma=False,
    )
```
